32 devices in a mesh: dp: 16 (over z, y, core), tensor: 2 (over x).
Axes of the slice: x: 2, y: 2, z: 4, core: 2. Of those that a mesh axis runs over, the one named last changes fastest.
Arguments:
- tokens: bfloat16 [16, 1024, 768], P('dp'), may hold values from -6 to 6
- lengths: int32 [16, 4], P('dp'), may hold values from 1 to 512, 1024 in all within a row
- cotangent: bfloat16 [16, 1024, 768], P('dp'), may hold values from -6 to 6
- norm_gain_one: float32 [768], replicated, may hold values from 0.5 to 1.5
- norm_shift_one: float32 [768], replicated, may hold values from -2 to 2
- w_qkv: bfloat16 [768, 3, 768], P(None, None, 'tensor'), may hold values from -0.21875 to 0.21875
- w_out: bfloat16 [768, 768], P('tensor'), may hold values from -2.5 to 2.5
- b_out: float32 [768], replicated, may hold values from -2 to 2
- norm_gain_two: float32 [768], replicated, may hold values from 0.5 to 1.5
- norm_shift_two: float32 [768], replicated, may hold values from -2 to 2
- w_up: bfloat16 [768, 3072], P(None, 'tensor'), may hold values from -0.21875 to 0.21875
- b_up: float32 [3072], P('tensor'), may hold values from -2 to 2
- w_down: bfloat16 [3072, 768], P('tensor'), may hold values from -0.109375 to 0.109375
- b_down: float32 [768], replicated, may hold values from -2 to 2
Outputs:
- output: bfloat16 [16, 1024, 768], P('dp')
- grad_tokens: float32 [16, 1024, 768], P('dp')
- grad_norm_gain_one: float32 [768], replicated
- grad_norm_shift_one: float32 [768], replicated
- grad_w_qkv: float32 [768, 3, 768], P('dp', None, 'tensor')
- grad_w_out: float32 [768, 768], P('tensor', 'dp')
- grad_b_out: float32 [768], replicated
- grad_norm_gain_two: float32 [768], replicated
- grad_norm_shift_two: float32 [768], replicated
- grad_w_up: float32 [768, 3072], P('dp', 'tensor')
- grad_b_up: float32 [3072], P('tensor')
- grad_w_down: float32 [3072, 768], P('tensor', 'dp')
- grad_b_down: float32 [768], replicated
The draws below stay inside these ranges and needn't reach their ends.
Inputs may be any that keep to these rules, and one draw needn't show every extreme that they name: Each row's 4 lengths sum to 1024, and the longest document of every row has exactly 512 tokens.
All inputs are finite; a program needn't handle non-finite values.
Results may differ from the reference program's by a relative error of at most 0.012.
Values may be sent and summed in bfloat16 or wider, within the bound.
No kernel may reach another device: no remote copies, remote signals or barrier semaphores. Data moves between devices by JAX's collectives and lax.ppermute only.
A program may use at most 192 MiB of HBM per device.

```python
import math
import jax
import jax.numpy as jnp
import numpy as np
from jax import lax

D = 768
HEADS = 12
HEAD_DIM = 64
FF = 3072
LEN = 1024
DOCS = 4
ROWS = 16


def level_of(stream_key, dims, cuts, smallest, largest):
    loudness, own = 1.0, jax.random.fold_in(stream_key, 6)
    for dim, shards_of in cuts:
        steps = jnp.exp(jax.random.uniform(jax.random.fold_in(own, dim), (shards_of,), jnp.float32, smallest / len(cuts), largest / len(cuts)))
        loudness = loudness * jnp.repeat(steps, dims[dim] // shards_of).reshape([-1 if axis == dim else 1 for axis in range(len(dims))])
    return loudness


def profile(number_of, total, most, skew):
    loads = [(1 << 20) // math.isqrt(rank ** skew) + 1 for rank in range(2, number_of + 1)]
    surplus, counts = total - most - (number_of - 1), [1] * (number_of - 1)
    while surplus > 0:
        free = [i for i in range(number_of - 1) if counts[i] < most]
        pool, remaining = sum([loads[i] for i in free]), surplus
        for i in free:
            more = min(most - counts[i], max(1, remaining * loads[i] // pool), surplus)
            counts[i] = counts[i] + more
            surplus = surplus - more
    return np.array([most] + counts)


def ragged(own_key, number_of, total, reach, lean):
    if number_of == 2:
        one = jax.random.randint(own_key, (), max(1, total - reach), min(reach, total - 1) + 1)
        return jnp.stack([one, total - one])
    tallies = jnp.asarray(profile(number_of, total, reach, lean), jnp.int32)
    couples = (number_of - 1) // 2
    source_of, sink = tallies[1:1 + 2 * couples:2], tallies[2:2 + 2 * couples:2]
    room = jnp.minimum(source_of - 1, reach - sink)
    shifted = jax.random.randint(jax.random.fold_in(own_key, 1), (couples,), 0, 1 << 20) % (room + 1)
    tallies = tallies.at[1:1 + 2 * couples:2].set(source_of - shifted).at[2:2 + 2 * couples:2].set(sink + shifted)
    return tallies[jax.random.permutation(jax.random.fold_in(own_key, 2), number_of)]


def noise(rng, shape, width, reach, shards=(), kind=jnp.bfloat16):
    loudness = level_of(rng, shape, shards, -0.22, 0.18) if shards else 1.0
    result = jax.random.normal(rng, shape, jnp.float32) * width * loudness
    return jnp.minimum(jnp.maximum(result, -reach), reach).astype(kind)


def setup_inputs(seed: int = 0) -> dict:
    key_of = jax.random.split(jax.random.key(seed), 15)
    tokens = noise(key_of[0], (ROWS, LEN, D), 1.0, 6.0, ((0, 16),))
    lengths = jax.vmap(lambda own: ragged(own, DOCS, LEN, LEN // 2, 2))(jax.random.split(key_of[1], ROWS)).reshape((ROWS, DOCS)).astype(jnp.int32)
    cotangent = noise(key_of[2], (ROWS, LEN, D), 1.0, 6.0, ((0, 16),))
    norm_gain_one = jnp.clip(1.0 + 0.1 * jax.random.normal(key_of[3], (D,), jnp.float32), 0.5, 1.5)
    norm_shift_one = noise(key_of[4], (D,), 0.3, 2.0, (), jnp.float32)
    w_qkv = noise(key_of[5], (D, 3, D), D ** -0.5, 0.21875, ((2, 2),))
    w_out = noise(key_of[6], (D, D), (D * 8 // LEN) ** -0.5, 2.5, ((0, 2),))
    b_out = noise(key_of[7], (D,), 0.3, 2.0, (), jnp.float32)
    norm_gain_two = jnp.clip(1.0 + 0.1 * jax.random.normal(key_of[8], (D,), jnp.float32), 0.5, 1.5)
    norm_shift_two = noise(key_of[9], (D,), 0.3, 2.0, (), jnp.float32)
    w_up = noise(key_of[10], (D, FF), D ** -0.5, 0.21875, ((1, 2),))
    b_up = noise(key_of[11], (FF,), 0.3, 2.0, ((0, 2),), jnp.float32)
    w_down = noise(key_of[12], (FF, D), FF ** -0.5, 0.109375, ((0, 2),))
    b_down = noise(key_of[13], (D,), 0.3, 2.0, (), jnp.float32)
    return {"tokens": tokens, "lengths": lengths, "cotangent": cotangent, "norm_gain_one": norm_gain_one, "norm_shift_one": norm_shift_one, "w_qkv": w_qkv, "w_out": w_out, "b_out": b_out, "norm_gain_two": norm_gain_two, "norm_shift_two": norm_shift_two, "w_up": w_up, "b_up": b_up, "w_down": w_down, "b_down": b_down}


@jax.custom_vjp
def low(v):
    return lax.optimization_barrier(v.astype(jnp.bfloat16)).astype(jnp.float32)

@jax.custom_vjp
def low_back(v):
    return v

def low_keep(v):
    return (low(v), None)

def low_pass(kept, grad):
    return (grad,)

def back_keep(v):
    return (v, None)

def back_low(kept, grad):
    return (low(grad),)
low.defvjp(low_keep, low_pass)
low_back.defvjp(back_keep, back_low)
norm_eps = 1e-05
masked_value = -1e+30
highest = lax.Precision.HIGHEST

def layer_norm(values, norm_gain, norm_shift):
    average = lax.optimization_barrier(jnp.mean(values, axis=-1, keepdims=True))
    centred = values - average
    variance = lax.optimization_barrier(jnp.mean(centred * centred, axis=-1, keepdims=True))
    return centred * lax.rsqrt(variance + norm_eps) * norm_gain + norm_shift

def doc_layout(lengths_row):
    doc_ends = jnp.cumsum(lengths_row).astype(jnp.int32)
    doc_starts = (doc_ends - lengths_row).astype(jnp.int32)
    position = jnp.arange(LEN, dtype=jnp.int32)
    doc_index = lax.optimization_barrier(jnp.sum((position[:, None] >= doc_ends[None, :]).astype(jnp.int32), axis=1, dtype=jnp.int32))
    is_first = jnp.any(position[:, None] == doc_starts[None, :], axis=1)
    return (position, doc_index, is_first)

def row_forward(tokens_row, lengths_row, params):
    gain_one, shift_one, w_qkv, w_out, b_out, gain_two, shift_two, w_up, b_up, w_down, b_down = params
    position, doc_index, is_first = doc_layout(lengths_row)
    same_doc = doc_index[:, None] == doc_index[None, :]
    allowed = same_doc & (position[None, :] <= position[:, None])
    selectable = same_doc & (position[None, :] < position[:, None]) & jnp.logical_not(is_first)[None, :]
    normed = low(layer_norm(tokens_row, gain_one, shift_one))
    project = low(low_back(jnp.einsum('ld,dce->cle', normed, w_qkv, precision=highest)))
    heads_view = project.reshape(3, LEN, HEADS, HEAD_DIM)
    score_scale = HEAD_DIM ** (-0.5)
    scores = jnp.einsum('qhe,khe->hqk', heads_view[0], heads_view[1], precision=highest) * score_scale
    chosen = jnp.where(selectable, jnp.square(jnp.maximum(scores[0], 0.0)), 0.0)
    penalty = 2.0 / LEN * (jnp.cumsum(chosen, axis=0) - chosen)
    logits = jnp.where(allowed[None], low_back(scores) - penalty[None], masked_value)
    row_top = lax.optimization_barrier(jnp.max(logits, axis=-1, keepdims=True))
    exponent = jnp.exp(logits - row_top)
    probability = low(exponent / lax.optimization_barrier(jnp.sum(exponent, axis=-1, keepdims=True)))
    context = jnp.einsum('hqk,khe->qhe', probability, heads_view[2], precision=highest).reshape(LEN, D)
    context = low(low_back(context))
    middle = tokens_row + (low_back(jnp.dot(context, w_out, precision=highest)) + b_out)
    normed_two = low(layer_norm(middle, gain_two, shift_two))
    upward = low_back(jnp.dot(normed_two, w_up, precision=highest) + b_up)
    active = low(jax.nn.gelu(upward, approximate=True))
    return middle + jnp.dot(active, w_down, precision=highest) + b_down

def reference(tokens, lengths, cotangent, norm_gain_one, norm_shift_one, w_qkv, w_out, b_out, norm_gain_two, norm_shift_two, w_up, b_up, w_down, b_down):
    params = tuple((array.astype(jnp.float32) for array in (norm_gain_one, norm_shift_one, w_qkv, w_out, b_out, norm_gain_two, norm_shift_two, w_up, b_up, w_down, b_down)))
    inputs = tokens.astype(jnp.float32)

    def forward(token_values, *weights):

        def one_row(row_pair):
            return row_forward(row_pair[0], row_pair[1], weights)
        return lax.map(jax.checkpoint(one_row), (token_values, lengths))
    outputs, pullback = jax.vjp(forward, inputs, *params)
    gradients = pullback(cotangent.astype(jnp.float32))
    return (outputs.astype(jnp.bfloat16), gradients[0], gradients[1], gradients[2], gradients[3], gradients[4], gradients[5], gradients[6], gradients[7], gradients[8], gradients[9], gradients[10], gradients[11])
```

```python
import functools

import jax
import jax.numpy as jnp
from jax import lax
from jax.experimental import pallas as pl
from jax.experimental.pallas import tpu as pltpu
from jax.sharding import PartitionSpec as P

HEAD_DIM = 64
LONGEST = 512
BLK = 256
EPS = 1e-05
FAR = 1e30
AXES = ("dp", "tensor")
f32 = jnp.float32
bf16 = jnp.bfloat16


def dot(a, b, ca=1, cb=0, precision=None):
    return lax.dot_general(
        a, b, (((ca,), (cb,)), ((), ())), preferred_element_type=f32, precision=precision
    )


def spec(shape, index=None):
    if index is None:
        zeros = (0,) * len(shape)
        return pl.BlockSpec(shape, lambda *_: zeros)
    return pl.BlockSpec(shape, index)


def params(mib=48):
    return pltpu.CompilerParams(vmem_limit_bytes=mib * 1024 * 1024)


def cost(flops, nbytes, trans=0):
    return pl.CostEstimate(flops=int(flops), bytes_accessed=int(nbytes), transcendentals=int(trans))


def starts_at(pos, lengths_ref, docs):
    start = jnp.zeros_like(pos)
    end = lengths_ref[0, 0]
    for d in range(1, docs):
        start = jnp.where(pos >= end, end, start)
        end = end + lengths_ref[0, d]
    return start


def standard(x):
    mean = jnp.mean(x, axis=-1, keepdims=True)
    c = x - mean
    var = jnp.mean(c * c, axis=-1, keepdims=True)
    rstd = lax.rsqrt(var + EPS)
    return c * rstd, rstd


def norm_back(xhat, rstd, gain, grad):
    gg = grad * gain
    m1 = jnp.mean(gg, axis=-1, keepdims=True)
    m2 = jnp.mean(gg * xhat, axis=-1, keepdims=True)
    return rstd * (gg - m1 - xhat * m2)


def qkv_kernel(scale, x_ref, g_ref, b_ref, w_ref, q_ref, k_ref, v_ref, n_ref, nt_ref):
    xhat, _ = standard(x_ref[...].astype(f32))
    n = (xhat * g_ref[...] + b_ref[...]).astype(bf16)
    n_ref[...] = n
    nt_ref[...] = n.T
    q_ref[...] = (dot(n, w_ref[0]).astype(bf16).astype(f32) * scale).astype(bf16)
    k_ref[...] = dot(n, w_ref[1]).astype(bf16)
    v_ref[...] = dot(n, w_ref[2]).astype(bf16)


def qkv_call(x, gain, shift, w3):
    L, D = x.shape
    HL = w3.shape[2]
    row = lambda w: spec((BLK, w), lambda i: (i, 0))
    return pl.pallas_call(
        functools.partial(qkv_kernel, HEAD_DIM**-0.5),
        grid=(L // BLK,),
        in_specs=[row(D), spec((1, D)), spec((1, D)), spec((3, D, HL))],
        out_specs=[row(HL)] * 3 + [row(D), spec((D, BLK), lambda i: (0, i))],
        out_shape=[jax.ShapeDtypeStruct((L, HL), bf16)] * 3
        + [jax.ShapeDtypeStruct((L, D), bf16), jax.ShapeDtypeStruct((D, L), bf16)],
        compiler_params=params(24),
        cost_estimate=cost(2 * L * D * 3 * HL, 10e6),
        name="norm_qkv",
    )(x, gain, shift, w3)


def cot_kernel(c_ref, w_ref, ga_ref, ct_ref, cs_ref):
    @pl.when(pl.program_id(0) == 0)
    def _():
        cs_ref[...] = jnp.zeros_like(cs_ref)

    c = c_ref[...]
    ct_ref[...] = c.T
    cs_ref[...] += jnp.sum(c.astype(f32), axis=0, keepdims=True)
    ga_ref[...] = dot(c, w_ref[...], 1, 1).astype(bf16)


def cot_call(c, w_down):
    L, D = c.shape
    F = w_down.shape[0]
    row = lambda w: spec((BLK, w), lambda i: (i, 0))
    return pl.pallas_call(
        cot_kernel,
        grid=(L // BLK,),
        in_specs=[row(D), spec((F, D))],
        out_specs=[row(F), spec((D, BLK), lambda i: (0, i)), spec((1, D))],
        out_shape=[
            jax.ShapeDtypeStruct((L, F), bf16),
            jax.ShapeDtypeStruct((D, L), bf16),
            jax.ShapeDtypeStruct((1, D), f32),
        ],
        compiler_params=params(24),
        cost_estimate=cost(2 * L * D * F, 10e6),
        name="cot_down",
    )(c, w_down)


def windows(L):
    reach = LONGEST // BLK
    return [(max(0, (i - reach)) * BLK, (i + 1) * BLK) for i in range(L // BLK)]


def attend_kernel(
    docs, strength, len_ref, n_ref, wp_ref, q_ref, k_ref, v_ref, ctx_ref, lse_ref, pq_ref, pk_ref, bias_ref
):
    L = q_ref.shape[0]
    pair = pl.program_id(0)
    wins = windows(L)
    lane = lax.broadcasted_iota(jnp.int32, (1, 128), 1)

    @pl.when(pair == 0)
    def _():
        n = n_ref[...]
        w = wp_ref[...]
        pq = (dot(n, w[:, :128]).astype(bf16).astype(f32) * HEAD_DIM**-0.5).astype(bf16)
        pk = dot(n, w[:, 128:]).astype(bf16)
        pq_ref[...] = pq
        pk_ref[...] = pk
        rows = lax.broadcasted_iota(jnp.int32, (BLK, BLK), 0)
        cols = lax.broadcasted_iota(jnp.int32, (BLK, BLK), 1)
        below = jnp.where(cols < rows, 1.0, 0.0).astype(bf16)
        carry = jnp.zeros((1, L), f32)
        for i, (lo, hi) in enumerate(wins):
            W = hi - lo
            s = dot(pq[i * BLK : (i + 1) * BLK], pk[lo:hi], 1, 1)
            ipos = i * BLK + lax.broadcasted_iota(jnp.int32, (BLK, 1), 0)
            jpos = lo + lax.broadcasted_iota(jnp.int32, (1, W), 1)
            istart = starts_at(ipos, len_ref, docs)
            jstart = starts_at(jpos, len_ref, docs)
            inside = jpos >= istart
            allowed = inside & (jpos <= ipos)
            selectable = inside & (jpos < ipos) & (jpos != jstart)
            r = jnp.maximum(s, 0.0)
            chosen = jnp.where(selectable, r * r, 0.0)
            pen = strength * (carry[:, lo:hi] + dot(below, chosen.astype(bf16)))
            bias_ref[i, :, :W] = jnp.where(allowed, pen, FAR)
            add = jnp.sum(chosen, axis=0, keepdims=True)
            parts = [carry[:, lo:hi] + add]
            if lo > 0:
                parts.insert(0, carry[:, :lo])
            if hi < L:
                parts.append(carry[:, hi:])
            carry = jnp.concatenate(parts, axis=1) if len(parts) > 1 else parts[0]

    for i, (lo, hi) in enumerate(wins):
        W = hi - lo
        q = q_ref[i * BLK : (i + 1) * BLK, :]
        k = k_ref[lo:hi, :]
        v = v_ref[lo:hi, :]
        bias = bias_ref[i, :, :W]
        outs, tops = [], []
        for h in range(2):
            mine = (lane // HEAD_DIM) == h
            s = dot(jnp.where(mine, q, jnp.zeros_like(q)), k, 1, 1) - bias
            top = jnp.max(s, axis=-1, keepdims=True)
            p = jnp.exp(s - top)
            total = jnp.sum(p, axis=-1, keepdims=True)
            o = dot(p.astype(bf16), v) / total
            outs.append(o)
            tops.append(top + jnp.log(total))
        first = (lane // HEAD_DIM) == 0
        ctx_ref[i * BLK : (i + 1) * BLK, :] = jnp.where(first, outs[0], outs[1]).astype(bf16)
        both = jnp.where(lane == 0, tops[0], tops[1])
        lse_ref[0, :, i * BLK : (i + 1) * BLK] = both.T[:8, :]


def attend_call(lengths, n, wp, q, k, v):
    L, HL = q.shape
    D = n.shape[1]
    pairs = HL // 128
    col = spec((L, 128), lambda p: (0, p))
    wide = LONGEST + BLK
    area = sum((hi - lo) * BLK for lo, hi in windows(L))
    return pl.pallas_call(
        functools.partial(attend_kernel, lengths.shape[1], 2.0 / L),
        grid=(pairs,),
        in_specs=[
            pl.BlockSpec(memory_space=pltpu.SMEM),
            spec((L, D)),
            spec((D, 256)),
            col,
            col,
            col,
        ],
        out_specs=[
            col,
            spec((1, 8, L), lambda p: (p, 0, 0)),
            spec((L, 128)),
            spec((L, 128)),
        ],
        out_shape=[
            jax.ShapeDtypeStruct((L, HL), bf16),
            jax.ShapeDtypeStruct((pairs, 8, L), f32),
            jax.ShapeDtypeStruct((L, 128), bf16),
            jax.ShapeDtypeStruct((L, 128), bf16),
        ],
        scratch_shapes=[pltpu.VMEM((L // BLK, BLK, wide), f32)],
        compiler_params=params(40),
        cost_estimate=cost(area * 128 * 2 * 2 * 2 * pairs, 8e6, area * pairs * 2),
        name="attend",
    )(lengths, n, wp, q, k, v)


def middle_kernel(x_ref, ca_ref, cb_ref, wa_ref, wb_ref, bo_ref, g_ref, b_ref, mid_ref, n_ref, nt_ref):
    att = dot(ca_ref[...], wa_ref[...]) + dot(cb_ref[...], wb_ref[...])
    mid = x_ref[...].astype(f32) + (att + bo_ref[...])
    mid_ref[...] = mid
    xhat, _ = standard(mid)
    n = (xhat * g_ref[...] + b_ref[...]).astype(bf16)
    n_ref[...] = n
    nt_ref[...] = n.T


def middle_call(x, ca, cb, wa, wb, b_out, gain, shift):
    L, D = x.shape
    HL = ca.shape[1]
    row = lambda w: spec((BLK, w), lambda i: (i, 0))
    return pl.pallas_call(
        middle_kernel,
        grid=(L // BLK,),
        in_specs=[row(D), row(HL), row(HL), spec((HL, D)), spec((HL, D))] + [spec((1, D))] * 3,
        out_specs=[row(D), row(D), spec((D, BLK), lambda i: (0, i))],
        out_shape=[
            jax.ShapeDtypeStruct((L, D), f32),
            jax.ShapeDtypeStruct((L, D), bf16),
            jax.ShapeDtypeStruct((D, L), bf16),
        ],
        compiler_params=params(24),
        cost_estimate=cost(2 * L * D * 2 * HL, 12e6),
        name="middle",
    )(x, ca, cb, wa, wb, b_out, gain, shift)


C0 = 0.7978845608028654
C1 = 0.044715


def gelu_pair(u):
    u2 = u * u
    t = jnp.tanh(u * (C0 + (C0 * C1) * u2))
    h = 0.5 + 0.5 * t
    a = u * h
    d = h + a * (1.0 - h) * (2.0 * C0 + (6.0 * C0 * C1) * u2)
    return a, d


def mlp_own_kernel(
    n_ref, nt_ref, ct_ref, ga_ref, wu_ref, wd_ref, bu_ref, out_ref, gn_ref, dwu_ref, dwd_ref, dbu_ref, a_ref, gu_ref
):
    first = pl.program_id(0) == 0

    @pl.when(first)
    def _():
        out_ref[...] = jnp.zeros_like(out_ref)
        gn_ref[...] = jnp.zeros_like(gn_ref)

    wu = wu_ref[...]
    wd = wd_ref[...]
    db = jnp.zeros((1, wu.shape[1]), f32)
    for m in range(n_ref.shape[0] // BLK):
        r = slice(m * BLK, (m + 1) * BLK)
        u = dot(n_ref[r, :], wu) + bu_ref[...]
        a, d = gelu_pair(u)
        a = a.astype(bf16)
        gu = (d * ga_ref[r, :].astype(f32)).astype(bf16)
        db = db + jnp.sum(gu.astype(f32), axis=0, keepdims=True)
        a_ref[r, :] = a
        gu_ref[r, :] = gu
        out_ref[r, :] += dot(a, wd)
        gn_ref[r, :] += dot(gu, wu, 1, 1)
    dbu_ref[...] = db
    dwu_ref[...] = dot(nt_ref[...], gu_ref[...]).astype(bf16)
    dwd_ref[...] = dot(ct_ref[...], a_ref[...]).astype(bf16)


def mlp_own_call(n, nt, ct, ga, w_up, w_down, b_up):
    L, D = n.shape
    F = w_up.shape[1]
    CH = 512
    colf = lambda r: spec((r, CH), lambda j: (0, j))
    return pl.pallas_call(
        mlp_own_kernel,
        grid=(F // CH,),
        in_specs=[
            spec((L, D)),
            spec((D, L)),
            spec((D, L)),
            colf(L),
            colf(D),
            spec((CH, D), lambda j: (j, 0)),
            colf(1),
        ],
        out_specs=[spec((L, D)), spec((L, D)), colf(D), colf(D), colf(1)],
        out_shape=[
            jax.ShapeDtypeStruct((L, D), f32),
            jax.ShapeDtypeStruct((L, D), f32),
            jax.ShapeDtypeStruct((D, F), bf16),
            jax.ShapeDtypeStruct((D, F), bf16),
            jax.ShapeDtypeStruct((1, F), f32),
        ],
        scratch_shapes=[pltpu.VMEM((L, CH), bf16), pltpu.VMEM((L, CH), bf16)],
        compiler_params=params(48),
        cost_estimate=cost(2 * L * D * F * 5, 24e6, L * F),
        name="mlp_own",
    )(n, nt, ct, ga, w_up, w_down, b_up)


def mlp_other_kernel(n_ref, c_ref, wu_ref, wd_ref, bu_ref, oin_ref, gin_ref, out_ref, gn_ref):
    @pl.when(pl.program_id(0) == 0)
    def _():
        out_ref[...] = oin_ref[...]
        gn_ref[...] = gin_ref[...]

    wu = wu_ref[...]
    wd = wd_ref[...]
    for m in range(n_ref.shape[0] // BLK):
        r = slice(m * BLK, (m + 1) * BLK)
        u = dot(n_ref[r, :], wu) + bu_ref[...]
        a, d = gelu_pair(u)
        gu = (d * dot(c_ref[r, :], wd, 1, 1)).astype(bf16)
        out_ref[r, :] += dot(a.astype(bf16), wd)
        gn_ref[r, :] += dot(gu, wu, 1, 1)


def mlp_other_call(n, c, w_up, w_down, b_up, out, gn):
    L, D = n.shape
    F = w_up.shape[1]
    CH = 512
    return pl.pallas_call(
        mlp_other_kernel,
        grid=(F // CH,),
        in_specs=[
            spec((L, D)),
            spec((L, D)),
            spec((D, CH), lambda j: (0, j)),
            spec((CH, D), lambda j: (j, 0)),
            spec((1, CH), lambda j: (0, j)),
            spec((L, D)),
            spec((L, D)),
        ],
        out_specs=[spec((L, D)), spec((L, D))],
        out_shape=[jax.ShapeDtypeStruct((L, D), f32)] * 2,
        compiler_params=params(48),
        cost_estimate=cost(2 * L * D * F * 4, 24e6, L * F),
        name="mlp_other",
    )(n, c, w_up, w_down, b_up, out, gn)


def mid_back_kernel(
    mid_ref, mo_ref, gn_ref, c_ref, bd_ref, g_ref, wo_ref, ctx_ref, out_ref, gm_ref, gc_ref, dd_ref, dwo_ref, sums_ref, acc_ref
):
    i = pl.program_id(0)

    @pl.when(i == 0)
    def _():
        sums_ref[...] = jnp.zeros_like(sums_ref)
        acc_ref[...] = jnp.zeros_like(acc_ref)

    mid = mid_ref[...]
    out_ref[...] = (mid + mo_ref[...] + bd_ref[...]).astype(bf16)
    gn = gn_ref[...]
    xhat, rstd = standard(mid)
    gm = c_ref[...].astype(f32) + norm_back(xhat, rstd, g_ref[...], gn)
    sums_ref[0:1, :] += jnp.sum(gn * xhat, axis=0, keepdims=True)
    sums_ref[1:2, :] += jnp.sum(gn, axis=0, keepdims=True)
    sums_ref[2:3, :] += jnp.sum(gm, axis=0, keepdims=True)
    gb = gm.astype(bf16)
    gm_ref[...] = gb
    gc = dot(gb, wo_ref[...], 1, 1).astype(bf16)
    gc_ref[...] = gc
    ctx = ctx_ref[...]
    prod = gc.astype(f32) * ctx.astype(f32)
    heads = lax.broadcasted_iota(jnp.int32, (8, 128), 0)
    lane = lax.broadcasted_iota(jnp.int32, (8, 128), 1)
    pick = jnp.where(lane // HEAD_DIM == heads, 1.0, 0.0)
    for p in range(ctx.shape[1] // 128):
        dd_ref[p] = dot(pick, prod[:, p * 128 : (p + 1) * 128], 1, 1, lax.Precision.HIGHEST)
    acc_ref[...] += dot(gb, ctx, 0, 0)

    @pl.when(i == pl.num_programs(0) - 1)
    def _():
        dwo_ref[...] = acc_ref[...].astype(bf16)


def mid_back_call(mid, mo, gn, c, b_down, gain, w_out, ctx):
    L, D = mid.shape
    HL = ctx.shape[1]
    row = lambda w: spec((BLK, w), lambda i: (i, 0))
    return pl.pallas_call(
        mid_back_kernel,
        grid=(L // BLK,),
        in_specs=[row(D), row(D), row(D), row(D), spec((1, D)), spec((1, D)), spec((HL, D)), row(HL)],
        out_specs=[
            row(D),
            row(D),
            row(HL),
            spec((HL // 128, 8, BLK), lambda i: (0, 0, i)),
            spec((D, HL)),
            spec((8, D)),
        ],
        out_shape=[
            jax.ShapeDtypeStruct((L, D), bf16),
            jax.ShapeDtypeStruct((L, D), bf16),
            jax.ShapeDtypeStruct((L, HL), bf16),
            jax.ShapeDtypeStruct((HL // 128, 8, L), f32),
            jax.ShapeDtypeStruct((D, HL), bf16),
            jax.ShapeDtypeStruct((8, D), f32),
        ],
        scratch_shapes=[pltpu.VMEM((D, HL), f32)],
        compiler_params=params(40),
        cost_estimate=cost(2 * L * D * 2 * HL, 20e6),
        name="mid_back",
    )(mid, mo, gn, c, b_down, gain, w_out, ctx)


def back_windows(L):
    reach = LONGEST // BLK
    return [(j * BLK, min(L, (j + reach + 1) * BLK)) for j in range(L // BLK)]


def back_kernel(
    docs,
    strength,
    len_ref,
    pq_ref,
    pk_ref,
    q_ref,
    k_ref,
    v_ref,
    g_ref,
    lse_ref,
    dd_ref,
    dq_ref,
    dk_ref,
    dv_ref,
    pick_ref,
    bias_ref,
    gp_ref,
    dqa_ref,
):
    L = q_ref.shape[0]
    pair = pl.program_id(0)
    wins = back_windows(L)
    scale = HEAD_DIM**-0.5
    lane = lax.broadcasted_iota(jnp.int32, (1, 128), 1)
    first = (lane // HEAD_DIM) == 0

    def layout(j, lo, hi):
        W = hi - lo
        jpos = j * BLK + lax.broadcasted_iota(jnp.int32, (BLK, 1), 0)
        ipos = lo + lax.broadcasted_iota(jnp.int32, (1, W), 1)
        istart = starts_at(ipos, len_ref, docs)
        jstart = starts_at(jpos, len_ref, docs)
        inside = jpos >= istart
        return inside & (jpos <= ipos), inside & (jpos < ipos) & (jpos != jstart)

    @pl.when(pair == 0)
    def _():
        gp_ref[...] = jnp.zeros_like(gp_ref)
        rows = lax.broadcasted_iota(jnp.int32, (BLK, BLK), 0)
        cols = lax.broadcasted_iota(jnp.int32, (BLK, BLK), 1)
        above = jnp.where(rows < cols, 1.0, 0.0).astype(bf16)
        for j, (lo, hi) in enumerate(wins):
            s = dot(pk_ref[j * BLK : (j + 1) * BLK, :], pq_ref[lo:hi, :], 1, 1)
            allowed, selectable = layout(j, lo, hi)
            r = jnp.maximum(s, 0.0)
            chosen = jnp.where(selectable, r * r, 0.0)
            carry = jnp.zeros((BLK, 1), f32)
            for t in range((hi - lo) // BLK):
                c = chosen[:, t * BLK : (t + 1) * BLK]
                pen = strength * (carry + dot(c.astype(bf16), above))
                bias_ref[j, :, t * BLK : (t + 1) * BLK] = jnp.where(
                    allowed[:, t * BLK : (t + 1) * BLK], pen, FAR
                )
                carry = carry + jnp.sum(c, axis=1, keepdims=True)

    dqa_ref[...] = jnp.zeros_like(dqa_ref)
    for j, (lo, hi) in enumerate(wins):
        W = hi - lo
        kb = k_ref[j * BLK : (j + 1) * BLK, :]
        vb = v_ref[j * BLK : (j + 1) * BLK, :]
        qw = q_ref[lo:hi, :]
        gw = g_ref[lo:hi, :]
        bias = bias_ref[j, :, :W]
        zero = jnp.zeros_like(kb)
        dvs, dks, dqs = [], [], []
        gp = gp_ref[j, :, :W]
        for h in range(2):
            mine = (lane // HEAD_DIM) == h
            s = dot(jnp.where(mine, kb, zero), qw, 1, 1)
            p = jnp.exp(s - bias - lse_ref[0, h : h + 1, lo:hi])
            dp = dot(jnp.where(mine, vb, zero), gw, 1, 1)
            ds = p * (dp - dd_ref[0, h : h + 1, lo:hi])
            gp = gp - ds
            pb = p.astype(bf16)
            sb = ds.astype(bf16)
            dvs.append(dot(pb, gw))
            dks.append(dot(sb, qw))
            dqs.append(dot(sb, kb, 0, 0))
        gp_ref[j, :, :W] = gp
        dv_ref[j * BLK : (j + 1) * BLK, :] = jnp.where(first, dvs[0], dvs[1]).astype(bf16)
        dk_ref[j * BLK : (j + 1) * BLK, :] = jnp.where(first, dks[0], dks[1]).astype(bf16)
        dqa_ref[lo:hi, :] += jnp.where(first, dqs[0], dqs[1])
    dq_ref[...] = (dqa_ref[...] * scale).astype(bf16)

    @pl.when(pair == pl.num_programs(0) - 1)
    def _():
        rows = lax.broadcasted_iota(jnp.int32, (BLK, BLK), 0)
        cols = lax.broadcasted_iota(jnp.int32, (BLK, BLK), 1)
        later = jnp.where(rows > cols, 1.0, 0.0).astype(bf16)
        dqa_ref[...] = jnp.zeros_like(dqa_ref)
        pick_ref[...] = jnp.zeros_like(pick_ref)
        for j, (lo, hi) in enumerate(wins):
            kb = pk_ref[j * BLK : (j + 1) * BLK, :]
            s = dot(kb, pq_ref[lo:hi, :], 1, 1)
            _, selectable = layout(j, lo, hi)
            r2 = jnp.where(selectable, 2.0 * strength * jnp.maximum(s, 0.0), 0.0)
            carry = jnp.zeros((BLK, 1), f32)
            dk0 = jnp.zeros((BLK, 128), f32)
            for t in reversed(range((hi - lo) // BLK)):
                b = slice(t * BLK, (t + 1) * BLK)
                gp = gp_ref[j, :, b]
                gs = ((carry + dot(gp.astype(bf16), later)) * r2[:, b]).astype(bf16)
                carry = carry + jnp.sum(gp, axis=1, keepdims=True)
                at = slice(lo + t * BLK, lo + (t + 1) * BLK)
                dk0 = dk0 + dot(gs, pq_ref[at, :])
                dqa_ref[at, :] += dot(gs, kb, 0, 0)
            pick_ref[j * BLK : (j + 1) * BLK, :] = pltpu.roll(dk0, HEAD_DIM, 1).astype(bf16)
        pick_ref[...] = (pick_ref[...].astype(f32) + dqa_ref[...] * scale).astype(bf16)


def back_call(lengths, pq, pk, q, k, v, g, lse, dd):
    L, HL = q.shape
    pairs = HL // 128
    col = spec((L, 128), lambda p: (0, p))
    stat = spec((1, 8, L), lambda p: (p, 0, 0))
    wide = LONGEST + BLK
    area = sum((hi - lo) * BLK for lo, hi in back_windows(L))
    return pl.pallas_call(
        functools.partial(back_kernel, lengths.shape[1], 2.0 / L),
        grid=(pairs,),
        in_specs=[pl.BlockSpec(memory_space=pltpu.SMEM), spec((L, 128)), spec((L, 128)), col, col, col, col, stat, stat],
        out_specs=[col, col, col, spec((L, 128))],
        out_shape=[jax.ShapeDtypeStruct((L, HL), bf16)] * 3 + [jax.ShapeDtypeStruct((L, 128), bf16)],
        scratch_shapes=[
            pltpu.VMEM((L // BLK, BLK, wide), f32),
            pltpu.VMEM((L // BLK, BLK, wide), f32),
            pltpu.VMEM((L, 128), f32),
        ],
        compiler_params=params(40),
        cost_estimate=cost(area * 128 * 2 * 5 * 2 * pairs, 8e6, area * pairs * 2),
        name="attend_back",
    )(lengths, pq, pk, q, k, v, g, lse, dd)


def proj_back_kernel(
    dq_ref, dk_ref, dv_ref, pick_ref, nt_ref, w_ref, wp_ref, x_ref, gn_ref, dw_ref, sums_ref, acc_ref
):
    i = pl.program_id(0)

    @pl.when(i == 0)
    def _():
        sums_ref[...] = jnp.zeros_like(sums_ref)
        acc_ref[...] = jnp.zeros_like(acc_ref)

    dq, dk, dv, pick = dq_ref[...], dk_ref[...], dv_ref[...], pick_ref[...]
    gn = dot(dq, w_ref[0], 1, 1) + dot(dk, w_ref[1], 1, 1) + dot(dv, w_ref[2], 1, 1) + dot(pick, wp_ref[...], 1, 1)
    gn_ref[...] = gn.astype(bf16)
    xhat, _ = standard(x_ref[...].astype(f32))
    sums_ref[0:1, :] += jnp.sum(gn * xhat, axis=0, keepdims=True)
    sums_ref[1:2, :] += jnp.sum(gn, axis=0, keepdims=True)
    acc_ref[...] += dot(nt_ref[...], jnp.concatenate([dq, dk, dv, pick], axis=1))

    @pl.when(i == pl.num_programs(0) - 1)
    def _():
        dw_ref[...] = acc_ref[...].astype(bf16)


def proj_back_call(dq, dk, dv, pick, nt, w3, wp, x):
    L, HL = dq.shape
    D = x.shape[1]
    N = 3 * HL + 128
    row = lambda w: spec((BLK, w), lambda i: (i, 0))
    return pl.pallas_call(
        proj_back_kernel,
        grid=(L // BLK,),
        in_specs=[
            row(HL),
            row(HL),
            row(HL),
            row(128),
            spec((D, BLK), lambda i: (0, i)),
            spec((3, D, HL)),
            spec((D, 128)),
            row(D),
        ],
        out_specs=[row(D), spec((D, N)), spec((8, D))],
        out_shape=[
            jax.ShapeDtypeStruct((L, D), bf16),
            jax.ShapeDtypeStruct((D, N), bf16),
            jax.ShapeDtypeStruct((8, D), f32),
        ],
        scratch_shapes=[pltpu.VMEM((D, N), f32)],
        compiler_params=params(40),
        cost_estimate=cost(2 * L * D * N * 2, 16e6),
        name="proj_back",
    )(dq, dk, dv, pick, nt, w3, wp, x)


def last_kernel(x_ref, ga_ref, gb_ref, gm_ref, g_ref, o_ref):
    xhat, rstd = standard(x_ref[...].astype(f32))
    gn = ga_ref[...].astype(f32) + gb_ref[...].astype(f32)
    o_ref[...] = gm_ref[...].astype(f32) + norm_back(xhat, rstd, g_ref[...], gn)


def last_call(x, ga, gb, gm, gain):
    L, D = x.shape
    row = spec((BLK, D), lambda i: (i, 0))
    return pl.pallas_call(
        last_kernel,
        grid=(L // BLK,),
        in_specs=[row] * 4 + [spec((1, D))],
        out_specs=row,
        out_shape=jax.ShapeDtypeStruct((L, D), f32),
        compiler_params=params(24),
        cost_estimate=cost(L * D * 20, 10e6),
        name="norm_back",
    )(x, ga, gb, gm, gain)


def links(dp, tensor):
    def swap(bit):
        return [(p * tensor + t, (p ^ bit) * tensor + t) for p in range(dp) for t in range(tensor)]

    across = [(p * tensor + t, p * tensor + (1 - t)) for p in range(dp) for t in range(tensor)]
    head_zero = [(p * tensor, p * tensor + 1) for p in range(dp)]
    return swap, across, head_zero


def shards(
    dp,
    tensor,
    tokens,
    lengths,
    cotangent,
    norm_gain_one,
    norm_shift_one,
    w_qkv,
    w_out,
    b_out,
    norm_gain_two,
    norm_shift_two,
    w_up,
    b_up,
    w_down,
    b_down,
):
    _, L, D = tokens.shape
    HL = w_out.shape[0]
    F = w_up.shape[1]
    swap, across, head_zero = links(dp, tensor)
    t = lax.axis_index("tensor")
    d = lax.axis_index("dp")
    send = lambda a, perm: lax.ppermute(a, AXES, perm)

    def other_half(w):
        rows = w.shape[0] // 4
        core, y = d % 2, (d // 2) % 2
        mine = send(lax.dynamic_slice_in_dim(w, (2 * y + core) * rows, rows, 0), across)
        theirs = send(mine, swap(2))
        mine_c, theirs_c = send(mine, swap(1)), send(theirs, swap(1))
        whole = jnp.zeros_like(w)
        for part, slot in (
            (mine, 2 * y + core),
            (theirs, 2 * (1 - y) + core),
            (mine_c, 2 * y + 1 - core),
            (theirs_c, 2 * (1 - y) + 1 - core),
        ):
            whole = lax.dynamic_update_slice_in_dim(whole, part, slot * rows, 0)
        return whole

    def reduce_rows(g):
        rows = g.shape[0] // dp
        q = d // 2
        groups = dp // 2
        parts = g.reshape(groups, 2, rows, g.shape[1])
        keep = lax.dynamic_index_in_dim(parts, d % 2, 1, False)
        gone = lax.dynamic_index_in_dim(parts, 1 - d % 2, 1, False)
        parts = (keep.astype(f32) + send(gone, swap(1)).astype(f32)).astype(bf16)
        bit = 1
        while bit < groups:
            parts = parts.reshape(groups // (2 * bit), 2, rows, g.shape[1])
            mine = (q // bit) % 2
            keep = lax.dynamic_index_in_dim(parts, mine, 1, False)
            gone = lax.dynamic_index_in_dim(parts, 1 - mine, 1, False)
            total = keep.astype(f32) + send(gone, swap(2 * bit)).astype(f32)
            bit *= 2
            parts = total.astype(bf16) if bit < groups else total
        return parts.reshape(rows, g.shape[1])

    def sum_dp(v):
        bit = 1
        while bit < dp:
            v = v + send(v, swap(bit))
            bit *= 2
        return v

    x = tokens.reshape(L, D)
    cot = cotangent.reshape(L, D)
    line = lambda v: v.reshape(1, -1)
    w3 = jnp.transpose(w_qkv, (1, 0, 2))

    wp_own = jnp.concatenate([w3[0, :, :HEAD_DIM], w3[1, :, :HEAD_DIM]], axis=1)
    wp = jnp.where(t == 0, wp_own, send(wp_own, head_zero))
    blank = jnp.zeros((D, HEAD_DIM), bf16)
    wp_wide = jnp.concatenate([wp[:, :HEAD_DIM], blank, wp[:, HEAD_DIM:], blank], axis=1)

    w_out_b = other_half(w_out)
    w_up_b = other_half(w_up)
    w_down_b = other_half(w_down)
    b_up_b = send(b_up, across)

    q, k, v, n1, n1t = qkv_call(x, line(norm_gain_one), line(norm_shift_one), w3)
    ga, cot_t, cot_sum = cot_call(cot, w_down)
    ctx, lse, pq, pk = attend_call(lengths, n1, wp_wide, q, k, v)
    ctx_b = send(ctx, across)
    mid, n2, n2t = middle_call(
        x, ctx, ctx_b, w_out, w_out_b, line(b_out), line(norm_gain_two), line(norm_shift_two)
    )
    mo, gn2, dwu, dwd, dbu = mlp_own_call(n2, n2t, cot_t, ga, w_up, w_down, line(b_up))
    up_share = reduce_rows(dwu)
    down_share = reduce_rows(dwd)
    mo, gn2 = mlp_other_call(n2, cot, w_up_b, w_down_b, line(b_up_b), mo, gn2)
    out, gm, gc, dd, dwo, sums2 = mid_back_call(mid, mo, gn2, cot, line(b_down), line(norm_gain_two), w_out, ctx)
    out_share = reduce_rows(dwo)
    dq, dk, dv, pick = back_call(lengths, pq, pk, q, k, v, gc, lse, dd)
    gn1, dwq, sums1 = proj_back_call(dq, dk, dv, pick, n1t, w3, wp, x)
    gn1_b = send(gn1, across)
    grad_tokens = last_call(x, gn1, gn1_b, gm, line(norm_gain_one))

    qkv_share = reduce_rows(dwq)
    extra = qkv_share[:, 3 * HL :]
    extra = extra + send(extra, across)
    extra = jnp.where(t == 0, extra, jnp.zeros_like(extra))
    wide = ((0, 0), (0, HL - HEAD_DIM))
    qkv_share = qkv_share[:, : 3 * HL] + jnp.concatenate(
        [jnp.pad(extra[:, :HEAD_DIM], wide), jnp.pad(extra[:, HEAD_DIM:], wide), jnp.zeros((extra.shape[0], HL), f32)],
        axis=1,
    )

    early = sum_dp(jnp.concatenate([sums2[:3].reshape(-1), cot_sum.reshape(-1), dbu.reshape(-1)]).reshape(-1, 128))
    early = early.reshape(-1)
    late = sum_dp(sums1[:2].reshape(-1, 128))
    late = (late + send(late, across)).reshape(2, D)
    return (
        out.reshape(1, L, D),
        grad_tokens.reshape(1, L, D),
        late[0],
        late[1],
        qkv_share.reshape(-1, 3, HL),
        out_share.T,
        early[2 * D : 3 * D],
        early[:D],
        early[D : 2 * D],
        up_share,
        early[4 * D :],
        down_share.T,
        early[3 * D : 4 * D],
    )


def solution(mesh):
    in_specs = (
        P("dp", None, None),
        P("dp", None),
        P("dp", None, None),
        P(),
        P(),
        P(None, None, "tensor"),
        P("tensor", None),
        P(),
        P(),
        P(),
        P(None, "tensor"),
        P("tensor"),
        P("tensor", None),
        P(),
    )
    out_specs = (
        P("dp", None, None),
        P("dp", None, None),
        P(),
        P(),
        P("dp", None, "tensor"),
        P("tensor", "dp"),
        P(),
        P(),
        P(),
        P("dp", "tensor"),
        P("tensor"),
        P("tensor", "dp"),
        P(),
    )
    body = functools.partial(shards, mesh.shape["dp"], mesh.shape["tensor"])
    return jax.shard_map(body, mesh=mesh, in_specs=in_specs, out_specs=out_specs, check_vma=False)
```

```python
import functools

import jax
import jax.numpy as jnp
from jax import lax
from jax.experimental import pallas as pl
from jax.experimental.pallas import tpu as pltpu
from jax.sharding import PartitionSpec as P

HEAD_DIM = 64
LONGEST = 512
BLK = 256
EPS = 1e-05
FAR = 1e30
AXES = ("dp", "tensor")
f32 = jnp.float32
bf16 = jnp.bfloat16


def dot(a, b, ca=1, cb=0, precision=None):
    return lax.dot_general(
        a, b, (((ca,), (cb,)), ((), ())), preferred_element_type=f32, precision=precision
    )


def spec(shape, index=None):
    if index is None:
        zeros = (0,) * len(shape)
        return pl.BlockSpec(shape, lambda *_: zeros)
    return pl.BlockSpec(shape, index)


def params(mib=60):
    return pltpu.CompilerParams(vmem_limit_bytes=60 * 1024 * 1024)


ANY = pl.BlockSpec(memory_space=pl.ANY)
SMEM = pl.BlockSpec(memory_space=pltpu.SMEM)


def sds(shape, dtype):
    return jax.ShapeDtypeStruct(shape, dtype)


def cost(flops, nbytes, trans=0):
    return pl.CostEstimate(flops=int(flops), bytes_accessed=int(nbytes), transcendentals=int(trans))


def starts_at(pos, lengths_ref, docs):
    start = jnp.zeros_like(pos)
    end = lengths_ref[0, 0]
    for d in range(1, docs):
        start = jnp.where(pos >= end, end, start)
        end = end + lengths_ref[0, d]
    return start


def standard(x):
    mean = jnp.mean(x, axis=-1, keepdims=True)
    c = x - mean
    var = jnp.mean(c * c, axis=-1, keepdims=True)
    rstd = lax.rsqrt(var + EPS)
    return c * rstd, rstd


def norm_back(xhat, rstd, gain, grad):
    gg = grad * gain
    m1 = jnp.mean(gg, axis=-1, keepdims=True)
    m2 = jnp.mean(gg * xhat, axis=-1, keepdims=True)
    return rstd * (gg - m1 - xhat * m2)


def ids():
    d = lax.axis_index("dp")
    return lax.axis_index("tensor"), lax.rem(d, 2), lax.rem(d // 2, 2)


def quarters():
    _, core, y = ids()
    return [2 * y + core, 2 * (1 - y) + core, 2 * y + 1 - core, 2 * (1 - y) + 1 - core]


def pick_weights(own, got):
    t, _, _ = ids()
    return jnp.where(t == 0, own.astype(f32), got.astype(f32)).astype(bf16)


class Mover:
    def __init__(self, sems):
        self.sems, self.count, self.open = sems, 0, []

    def start(self, src, dst):
        op = pltpu.make_async_copy(src, dst, self.sems.at[self.count])
        self.count += 1
        op.start()
        return op

    def put(self, src, dst):
        self.open.append(self.start(src, dst))

    def finish(self):
        for op in self.open:
            op.wait()


def row_of(ref):
    return ref[...].reshape(1, -1)


LIGHT = ("mlp_own", "dw_last", "norm_qkv", "cot_down")


def call(kernel, name, ins, outs, scratch, sems, flops, nbytes, *args):
    full = lambda a: pl.BlockSpec(memory_space=pltpu.VMEM)
    return pl.pallas_call(
        kernel,
        in_specs=[full(a) if s is None else s for s, a in zip(ins, args, strict=True)],
        out_specs=[full(o) if inside else ANY for o, inside in outs],
        out_shape=[o for o, _ in outs],
        scratch_shapes=[pltpu.VMEM(s, t) for s, t in scratch] + [pltpu.SemaphoreType.DMA((sems,))],
        compiler_params=params(),
        cost_estimate=cost(1e3, 1e3) if name in LIGHT else cost(flops, nbytes),
        name=name,
    )(*args)


def pick_kernel(w_ref, wp_ref, qv, kv, sems):
    mv = Mover(sems)
    a = mv.start(w_ref.at[0, :, 0:128], qv)
    b = mv.start(w_ref.at[1, :, 0:128], kv)
    a.wait()
    b.wait()
    lane = lax.broadcasted_iota(jnp.int32, (1, 128), 1)
    k = pltpu.roll(kv[...].astype(f32), HEAD_DIM, 1)
    wp_ref[...] = jnp.where(lane < HEAD_DIM, qv[...].astype(f32), k).astype(bf16)


def pick_call(w3):
    D = w3.shape[1]
    return call(
        pick_kernel, "pick", [ANY], [(sds((D, 128), bf16), True)], [((D, 128), bf16)] * 2, 2, 1e3, 4e5, w3
    )[0]


def pack_kernel(wd_ref, wu_ref, wo_ref, bu_ref, one_ref, two_ref, onev, twov, sems):
    mv = Mover(sems)
    _, core, y = ids()
    s = 2 * y + core
    D = wo_ref.shape[1]
    ro, ru, rd = wo_ref.shape[0] // 4, wu_ref.shape[0] // 4, wd_ref.shape[0] // 4
    halves = wu_ref.shape[1] // D
    from_row = lambda n: pl.ds(pl.multiple_of(s * n, 16), n)
    get_one = mv.start(wo_ref.at[from_row(ro)], onev.at[0:ro])
    packs = []
    for h in range(halves):
        packs.append(mv.start(wu_ref.at[from_row(ru), h * D : (h + 1) * D], twov.at[h * ru : (h + 1) * ru]))
    packs.append(mv.start(wd_ref.at[from_row(rd)], twov.at[halves * ru : halves * ru + rd]))
    rest = row_of(bu_ref)
    pieces = []
    for _ in range(3):
        piece = rest.astype(bf16)
        rest = rest - piece.astype(f32)
        pieces.append(piece.astype(f32))
    flat = [p[:, h * D : (h + 1) * D] for p in pieces for h in range(halves)]
    onev[ro : ro + 16, :] = jnp.concatenate(flat + [jnp.zeros((16 - len(flat), D), f32)], axis=0).astype(bf16)
    get_one.wait()
    mv.put(onev, one_ref)
    for op in packs:
        op.wait()
    mv.put(twov, two_ref)
    mv.finish()


def pack_call(w_down, w_up, w_out, b_up):
    F, D = w_down.shape
    one = w_out.shape[0] // 4 + 16
    two = (w_up.shape[0] * (F // D) + F) // 4
    return call(
        pack_kernel,
        "pack",
        [ANY] * 3 + [None],
        [(sds((one, D), bf16), False), (sds((two, D), bf16), False)],
        [((one, D), bf16), ((two, D), bf16)],
        8,
        1e3,
        3e6,
        w_down, w_up, w_out, b_up,
    )


def start_kernel(x_ref, w_ref, g_ref, b_ref, q_ref, k_ref, v_ref, n_ref, xv, wv, nv, qv, kv, vv, sems):
    mv = Mover(sems)
    L, D = x_ref.shape
    half = L // 2
    gets = [mv.start(x_ref.at[0:half], xv.at[0:half]), mv.start(w_ref, wv), mv.start(x_ref.at[half:L], xv.at[half:L])]
    gain, shift = row_of(g_ref), row_of(b_ref)
    gets[0].wait()
    for m in range(L // BLK):
        r = slice(m * BLK, (m + 1) * BLK)
        if m * BLK == half:
            gets[2].wait()
        xhat, _ = standard(xv[r, :].astype(f32))
        n = (xhat * gain + shift).astype(bf16)
        nv[r, :] = n
        if m == 0:
            gets[1].wait()
        qv[r, :] = (dot(n, wv[0]).astype(bf16).astype(f32) * HEAD_DIM**-0.5).astype(bf16)
        kv[r, :] = dot(n, wv[1]).astype(bf16)
        vv[r, :] = dot(n, wv[2]).astype(bf16)
        if (m + 1) * BLK % half == 0:
            done = slice((m + 1) * BLK - half, (m + 1) * BLK)
            for src, dst in ((nv, n_ref), (qv, q_ref), (kv, k_ref), (vv, v_ref)):
                mv.put(src.at[done, :], dst.at[done, :])
    mv.finish()


def start_call(x, w3, gain, shift):
    L, D = x.shape
    HL = w3.shape[2]
    half = (L, HL)
    return call(
        start_kernel,
        "norm_qkv",
        [ANY] * 2 + [None] * 2,
        [(sds(half, bf16), False)] * 3 + [(sds((L, D), bf16), False)],
        [((L, D), bf16), ((3, D, HL), bf16), ((L, D), bf16)] + [(half, bf16)] * 3,
        11,
        2 * L * D * 3 * HL,
        9e6,
        x, w3, gain, shift,
    )


def cot_kernel(c_ref, wd_ref, ga_ref, cs_ref, cv, wdv, gav, sems):
    mv = Mover(sems)
    L, D = c_ref.shape
    gets = [mv.start(c_ref, cv), mv.start(wd_ref, wdv)]
    for op in gets:
        op.wait()
    cs = jnp.zeros((1, D), f32)
    for m in range(L // BLK):
        r = slice(m * BLK, (m + 1) * BLK)
        c = cv[r, :]
        cs = cs + jnp.sum(c.astype(f32), axis=0, keepdims=True)
        gav[r, :] = dot(c, wdv[...], 1, 1).astype(bf16)
        mv.put(gav.at[r, :], ga_ref.at[r, :])
    cs_ref[...] = cs
    mv.finish()


def cot_call(c, w_down):
    L, D = c.shape
    F = w_down.shape[0]
    return call(
        cot_kernel,
        "cot_down",
        [ANY] * 2,
        [(sds((L, F), bf16), False), (sds((1, D), f32), True)],
        [((L, D), bf16), ((F, D), bf16), ((L, F), bf16)],
        2 + L // BLK,
        2 * L * D * F,
        7e6,
        c, w_down,
    )


def windows(L):
    reach = LONGEST // BLK
    return [range(max(0, i - reach), i + 1) for i in range(L // BLK)]


def back_windows(L):
    reach = LONGEST // BLK
    found, at = [], 0
    for j in range(L // BLK):
        lo, hi = j * BLK, min(L, (j + reach + 1) * BLK)
        found.append((lo, hi, at))
        at += hi - lo
    return found, at


def attend_kernel(
    docs, strength, len_ref, n_ref, wpa_ref, wpb_ref, q_ref, k_ref, v_ref,
    ctx_ref, inv_ref, pq_ref, pk_ref, p_ref, r_ref,
    nv, qv, kv, vv, vt, cv, pv, rv, bias_ref, sems,
):
    mv = Mover(sems)
    get_n = mv.start(n_ref, nv)
    get_v = mv.start(v_ref, vv)
    get_q = mv.start(q_ref, qv)
    get_k = mv.start(k_ref, kv)
    L, HL = q_ref.shape
    wins, _ = back_windows(L)
    lane = lax.broadcasted_iota(jnp.int32, (1, 128), 1)
    left = lane < HEAD_DIM
    w = pick_weights(wpa_ref[...], wpb_ref[...])
    get_n.wait()
    both = dot(nv[...], w)
    pq_ref[...] = jnp.where(left, both.astype(bf16).astype(f32) * HEAD_DIM**-0.5, 0.0).astype(bf16)
    pk_ref[...] = jnp.where(left, pltpu.roll(both, HEAD_DIM, 1), 0.0).astype(bf16)
    get_v.wait()
    for m in range(L // BLK):
        vt[:, m * BLK : (m + 1) * BLK] = vv[m * BLK : (m + 1) * BLK, :].T
    rows = lax.broadcasted_iota(jnp.int32, (BLK, BLK), 0)
    cols = lax.broadcasted_iota(jnp.int32, (BLK, BLK), 1)
    above = jnp.where(rows < cols, 1.0, 0.0).astype(bf16)
    carry = [jnp.zeros((BLK, 1), f32)] * (L // BLK)
    get_q.wait()
    get_k.wait()
    for i, blocks in enumerate(windows(L)):
        mine = slice(i * BLK, (i + 1) * BLK)
        ipos = i * BLK + lax.broadcasted_iota(jnp.int32, (1, BLK), 1)
        istart = starts_at(ipos, len_ref, docs)
        places = {}
        for j in blocks:
            here = slice(j * BLK, (j + 1) * BLK)
            at = wins[j][2] + (i - j) * BLK
            places[j] = slice(at, at + BLK)
            s = dot(pk_ref[here, :], pq_ref[mine, :], 1, 1)
            jpos = j * BLK + lax.broadcasted_iota(jnp.int32, (BLK, 1), 0)
            inside = jpos >= istart
            fresh = jpos != starts_at(jpos, len_ref, docs)
            if j == i:
                allowed = inside & (jpos <= ipos)
                selectable = inside & (jpos < ipos) & fresh
            else:
                allowed, selectable = inside, inside & fresh
            r = jnp.where(selectable, jnp.maximum(s, 0.0), 0.0)
            rv[:, places[j]] = (r * (2.0 * strength)).astype(bf16)
            c = r * r
            pen = strength * (carry[j] + dot(c.astype(bf16), above))
            bias_ref[j - blocks[0]] = jnp.where(allowed, pen, FAR)
            if i + 1 < L // BLK and j in windows(L)[i + 1]:
                carry[j] = carry[j] + jnp.sum(c, axis=1, keepdims=True)
        invs, outs = [], []
        for h in range(HL // HEAD_DIM):
            cs = slice(h // 2 * 128, (h // 2 + 1) * 128)
            q = jnp.where((lane // HEAD_DIM) == h % 2, qv[mine, cs], jnp.zeros((BLK, 128), bf16))
            ss = [dot(kv[j * BLK : (j + 1) * BLK, cs], q, 1, 1) - bias_ref[j - blocks[0]] for j in blocks]
            top = functools.reduce(jnp.maximum, [jnp.max(s, axis=0, keepdims=True) for s in ss])
            total = jnp.zeros((1, BLK), f32)
            out = jnp.zeros((HEAD_DIM, BLK), f32)
            for j, s in zip(blocks, ss, strict=True):
                e = jnp.exp(s - top)
                total = total + jnp.sum(e, axis=0, keepdims=True)
                e = e.astype(bf16)
                pv[h, :, places[j]] = e
                out = out + dot(vt[h * HEAD_DIM : (h + 1) * HEAD_DIM, j * BLK : (j + 1) * BLK], e)
            inv = 1.0 / total
            invs.append(inv)
            outs.append(out * inv)
        inv_ref[:, mine] = jnp.concatenate(invs + [jnp.zeros((8 - len(invs), BLK), f32)], axis=0)
        for p in range(HL // 128):
            pair = jnp.concatenate(outs[2 * p : 2 * p + 2], axis=0)
            cv[mine, p * 128 : (p + 1) * 128] = pair.T.astype(bf16)
        mv.put(cv.at[mine, :], ctx_ref.at[mine, :])
        for j in blocks:
            mv.put(pv.at[:, :, places[j]], p_ref.at[:, :, places[j]])
    mv.put(rv, r_ref)
    mv.finish()


def attend_call(lengths, n, wpa, wpb, q, k, v):
    L, HL = q.shape
    D = n.shape[1]
    heads = HL // HEAD_DIM
    _, wide = back_windows(L)
    half = (L, HL)
    return call(
        functools.partial(attend_kernel, lengths.shape[1], 2.0 / L),
        "attend",
        [SMEM, ANY, None, None, ANY, ANY, ANY],
        [
            (sds(half, bf16), False),
            (sds((8, L), f32), True),
            (sds((L, 128), bf16), True),
            (sds((L, 128), bf16), True),
            (sds((heads, BLK, wide), bf16), False),
            (sds((BLK, wide), bf16), False),
        ],
        [((L, D), bf16)]
        + [(half, bf16)] * 3
        + [
            ((HL, L), bf16),
            (half, bf16),
            ((heads, BLK, wide), bf16),
            ((BLK, wide), bf16),
            ((LONGEST // BLK + 1, BLK, BLK), f32),
        ],
        5 + L // BLK + wide // BLK,
        1e12,
        14e6,
        lengths, n, wpa, wpb, q, k, v,
    )


C0 = 0.7978845608028654
C1 = 0.044715
CHUNK = 512


def gelu_pair(u):
    u2 = u * u
    t = jnp.tanh(u * (C0 + (C0 * C1) * u2))
    h = 0.5 + 0.5 * t
    a = u * h
    d = h + a * (1.0 - h) * (2.0 * C0 + (6.0 * C0 * C1) * u2)
    return a, d


def own_kernel(
    x_ref, ca_ref, cb_ref, wo_ref, p0_ref, p1_ref, p2_ref, p3_ref, wu_ref, wd_ref, ga_ref, c_ref,
    bo_ref, g_ref, b_ref, bu_ref,
    mid_ref, n_ref, gn_ref, mo_ref, keep_ref, send_ref, dbu_ref,
    xv, cav, cbv, wov, wbv, wuv, wdv, gav, cv, mv_, nv, gnv, mov, av, guv, keepv, sendv, sems,
):
    mv = Mover(sems)
    L, D = x_ref.shape
    F = wu_ref.shape[1]
    HL = ca_ref.shape[1]
    _, core, _ = ids()
    gets = [mv.start(ca_ref, cav), mv.start(wo_ref, wov), mv.start(cb_ref, cbv), mv.start(x_ref, xv)]
    ro, at = HL // 4, 0
    for part, slot in zip((p0_ref, p1_ref, p2_ref, p3_ref), quarters()):
        gets.append(mv.start(part.at[at : at + ro], wbv.at[pl.ds(pl.multiple_of(slot * ro, 16), ro)]))
    later = [mv.start(wu_ref, wuv), mv.start(ga_ref, gav), mv.start(wd_ref, wdv), mv.start(c_ref, cv)]
    bo, gain, shift, bu = row_of(bo_ref), row_of(g_ref), row_of(b_ref), row_of(bu_ref)
    for op in gets:
        op.wait()
    for m in range(L // BLK):
        r = slice(m * BLK, (m + 1) * BLK)
        att = dot(cav[r, :], wov[...]) + dot(cbv[r, :], wbv[...])
        mid = xv[r, :].astype(f32) + (att + bo)
        mv_[r, :] = mid
        xhat, _ = standard(mid)
        nv[r, :] = (xhat * gain + shift).astype(bf16)
    mv.put(mv_, mid_ref)
    mv.put(nv, n_ref)
    for op in later:
        op.wait()
    for j in range(F // CHUNK):
        at = slice(j * CHUNK, (j + 1) * CHUNK)
        db = jnp.zeros((1, CHUNK), f32)
        for m in range(L // BLK):
            r = slice(m * BLK, (m + 1) * BLK)
            a, d = gelu_pair(dot(nv[r, :], wuv[:, at]) + bu[:, at])
            a = a.astype(bf16)
            gu = d * gav[r, at].astype(f32)
            db = db + jnp.sum(gu, axis=0, keepdims=True)
            gu = gu.astype(bf16)
            av[r, :] = a
            guv[r, :] = gu
            mo = dot(a, wdv[at, :])
            gn = dot(gu, wuv[:, at], 1, 1)
            if j == 0:
                mov[r, :] = mo
                gnv[r, :] = gn
            else:
                mov[r, :] += mo
                gnv[r, :] += gn
        dbu_ref[:, at] = db
        dwu = dot(nv[...], guv[...], 0, 0)
        dwd = dot(cv[...], av[...], 0, 0)
        keepv[:, at] = jnp.where(core == 0, dwu, dwd).astype(bf16)
        sendv[:, at] = jnp.where(core == 0, dwd, dwu).astype(bf16)
        mv.put(sendv.at[:, at], send_ref.at[:, at])
        mv.put(keepv.at[:, at], keep_ref.at[:, at])
        if j == F // CHUNK - 1:
            mv.put(gnv, gn_ref)
            mv.put(mov, mo_ref)
    mv.finish()


def own_call(x, ca, cb, w_out, parts, w_up, w_down, ga, c, b_out, gain, shift, b_up):
    L, D = x.shape
    HL = ca.shape[1]
    F = w_up.shape[1]
    return call(
        own_kernel,
        "mlp_own",
        [ANY] * 12 + [None] * 4,
        [
            (sds((L, D), f32), False),
            (sds((L, D), bf16), False),
            (sds((L, D), f32), False),
            (sds((L, D), f32), False),
            (sds((D, F), bf16), False),
            (sds((D, F), bf16), False),
            (sds((1, F), f32), True),
        ],
        [
            ((L, D), bf16),
            ((L, HL), bf16),
            ((L, HL), bf16),
            ((HL, D), bf16),
            ((HL, D), bf16),
            ((D, F), bf16),
            ((F, D), bf16),
            ((L, F), bf16),
            ((L, D), bf16),
            ((L, D), f32),
            ((L, D), bf16),
            ((L, D), f32),
            ((L, D), f32),
            ((L, CHUNK), bf16),
            ((L, CHUNK), bf16),
            ((D, F), bf16),
            ((D, F), bf16),
        ],
        16 + 2 * (F // CHUNK),
        2 * L * D * F * 5 + 4 * L * D * HL,
        36e6,
        x, ca, cb, w_out, *parts, w_up, w_down, ga, c, b_out, gain, shift, b_up,
    )


def other_kernel(
    n_ref, c_ref, a0_ref, d0_ref, d1_ref, d2_ref, d3_ref, gn_ref, mo_ref, mid_ref, wo_ref, ctx_ref,
    g_ref, bd_ref, inv_ref,
    out_ref, gm_ref, gc_ref, dd_ref, sums_ref, keep_ref, send_ref,
    nv, cv, wuv, wdv, bv, gnv, mov, midv, wov, ctxv, gna, moa, outv, gmv, gcv, sems,
):
    mv = Mover(sems)
    L, D = n_ref.shape
    F = wdv.shape[0]
    HL = ctx_ref.shape[1]
    halves = F // D
    gets = [mv.start(n_ref, nv)]
    parts = list(zip((d0_ref, d1_ref, d2_ref, d3_ref), quarters()))
    ru, rd = D // 4, F // 4
    for part, slot in parts:
        for h in range(halves):
            dst = wuv.at[pl.ds(pl.multiple_of(slot * ru, 16), ru), h * D : (h + 1) * D]
            gets.append(mv.start(part.at[h * ru : (h + 1) * ru], dst))
    n = a0_ref.shape[0]
    gets.append(mv.start(a0_ref.at[n - 16 : n], bv))
    downs = [mv.start(c_ref, cv)]
    for part, slot in parts:
        dst = wdv.at[pl.ds(pl.multiple_of(slot * rd, 16), rd)]
        downs.append(mv.start(part.at[halves * ru : halves * ru + rd], dst))
    _, core, _ = ids()
    later = [
        mv.start(src, dst)
        for src, dst in ((gn_ref, gnv), (mo_ref, mov), (mid_ref, midv), (wo_ref, wov), (ctx_ref, ctxv))
    ]
    gain, bd = row_of(g_ref), row_of(bd_ref)
    for op in gets:
        op.wait()
    b = bv[...].astype(f32)
    bu = [b[h : h + 1] + b[halves + h : halves + h + 1] + b[2 * halves + h : 2 * halves + h + 1] for h in range(halves)]
    bu = jnp.concatenate(bu, axis=1)
    for j in range(F // CHUNK):
        at = slice(j * CHUNK, (j + 1) * CHUNK)
        for m in range(L // BLK):
            r = slice(m * BLK, (m + 1) * BLK)
            a, d = gelu_pair(dot(nv[r, :], wuv[:, at]) + bu[:, at])
            if j == 0 and m == 0:
                for op in downs:
                    op.wait()
            gu = (d * dot(cv[r, :], wdv[at, :], 1, 1)).astype(bf16)
            mo = dot(a.astype(bf16), wdv[at, :])
            gn = dot(gu, wuv[:, at], 1, 1)
            if j == 0:
                moa[r, :] = mo
                gna[r, :] = gn
            else:
                moa[r, :] += mo
                gna[r, :] += gn
    for op in later:
        op.wait()
    heads = lax.broadcasted_iota(jnp.int32, (8, HL), 0)
    lane = lax.broadcasted_iota(jnp.int32, (8, HL), 1)
    pick = jnp.where(lane // HEAD_DIM == heads, 1.0, 0.0).astype(bf16)
    s0 = s1 = s2 = jnp.zeros((1, D), f32)
    for m in range(L // BLK):
        r = slice(m * BLK, (m + 1) * BLK)
        mid = midv[r, :]
        outv[r, :] = (mid + (mov[r, :] + moa[r, :]) + bd).astype(bf16)
        gn = gnv[r, :] + gna[r, :]
        xhat, rstd = standard(mid)
        gm = cv[r, :].astype(f32) + norm_back(xhat, rstd, gain, gn)
        s0 = s0 + jnp.sum(gn * xhat, axis=0, keepdims=True)
        s1 = s1 + jnp.sum(gn, axis=0, keepdims=True)
        s2 = s2 + jnp.sum(gm, axis=0, keepdims=True)
        gb = gm.astype(bf16)
        gmv[r, :] = gb
        inv = inv_ref[:, r]
        high = inv.astype(bf16)
        low = (inv - high.astype(f32)).astype(bf16)
        gc = (dot(gb, wov[...], 1, 1) * (dot(high, pick, 0, 0) + dot(low, pick, 0, 0))).astype(bf16)
        gcv[r, :] = gc
        prod = gc.astype(f32) * ctxv[r, :].astype(f32)
        high = prod.astype(bf16)
        low = (prod - high.astype(f32)).astype(bf16)
        dd_ref[:, r] = dot(pick, high, 1, 1) + dot(pick, low, 1, 1)
        if m == L // BLK // 2 - 1 or m == L // BLK - 1:
            half = slice((m + 1) * BLK - L // 2, (m + 1) * BLK)
            for src, dst in ((gcv, gc_ref), (gmv, gm_ref), (outv, out_ref)):
                mv.put(src.at[half, :], dst.at[half, :])
    sums_ref[...] = jnp.concatenate([s0, s1, s2, jnp.zeros((5, D), f32)], axis=0)
    dwo = dot(gmv[...], ctxv[...], 0, 0)
    left, right = dwo[:, : HL // 2], dwo[:, HL // 2 :]
    keep_ref[...] = jnp.where(core == 0, left, right).astype(bf16)
    send_ref[...] = jnp.where(core == 0, right, left).astype(bf16)
    mv.finish()


def other_call(n, c, one, twos, gn, mo, mid, w_out, ctx, gain, b_down, inv):
    L, D = n.shape
    HL = ctx.shape[1]
    F = twos[0].shape[0] * 2
    return call(
        other_kernel,
        "mlp_other",
        [ANY] * 12 + [None] * 3,
        [
            (sds((L, D), bf16), False),
            (sds((L, D), bf16), False),
            (sds((L, HL), bf16), False),
            (sds((8, L), f32), True),
            (sds((8, D), f32), True),
            (sds((D, HL // 2), bf16), True),
            (sds((D, HL // 2), bf16), True),
        ],
        [
            ((L, D), bf16),
            ((L, D), bf16),
            ((D, F), bf16),
            ((F, D), bf16),
            ((16, D), bf16),
            ((L, D), f32),
            ((L, D), f32),
            ((L, D), f32),
            ((HL, D), bf16),
            ((L, HL), bf16),
            ((L, D), f32),
            ((L, D), f32),
            ((L, D), bf16),
            ((L, D), bf16),
            ((L, HL), bf16),
        ],
        4 * (F // D) + 4 + 8 + 6,
        2 * L * D * F * 4 + 2 * L * D * HL,
        30e6,
        n, c, one, *twos, gn, mo, mid, w_out, ctx, gain, b_down, inv,
    )


def head_grads(pairs, offset, wins, blocks, dd_ref, qv, kv, vv, gv, pv, dqa, dpv, gp_of, done):
    width = len(pairs) * 128
    scale = HEAD_DIM**-0.5
    lane = lax.broadcasted_iota(jnp.int32, (1, 128), 1)
    seen = set()
    for j, (lo, hi, at) in enumerate(wins):
        here = slice(j * BLK, (j + 1) * BLK)
        n = (hi - lo) // BLK
        blocks[j].wait()
        gps = [gp_of(j, t) for t in range(n)]
        for o, p in enumerate(pairs):
            cs = slice((p - offset) * 128, (p - offset + 1) * 128)
            kb, vb = kv[here, cs], vv[here, cs]
            dk = dv = jnp.zeros((BLK, 128), f32)
            for t in range(n):
                i = slice(lo + t * BLK, lo + (t + 1) * BLK)
                b = slice(at + t * BLK, at + (t + 1) * BLK)
                q, g = qv[i, cs], gv[i, cs]
                dq = jnp.zeros((BLK, 128), f32)
                for h in range(2):
                    mine = (lane // HEAD_DIM) == h
                    only = lambda a: jnp.where(mine, a, jnp.zeros_like(a))
                    gh = only(g)
                    pb = pv[2 * (p - offset) + h, :, b]
                    dp = dot(vb, gh, 1, 1)
                    ds = pb.astype(f32) * (dp - dd_ref[2 * p + h : 2 * p + h + 1, i])
                    gps[t] = gps[t] - ds
                    sb = ds.astype(bf16)
                    dv = dv + dot(pb, gh)
                    dk = dk + dot(sb, only(q))
                    dq = dq + dot(sb, only(kb), 0, 0)
                if (p, i.start) in seen:
                    dqa[i, cs] += dq
                else:
                    seen.add((p, i.start))
                    dqa[i, cs] = dq
            os = slice(o * 128, (o + 1) * 128)
            dpv[here, width + o * 128 : width + (o + 1) * 128] = dk.astype(bf16)
            dpv[here, 2 * width + o * 128 : 2 * width + (o + 1) * 128] = dv.astype(bf16)
            dpv[here, os] = (dqa[here, cs] * scale).astype(bf16)
        done(j, gps)


def halves_out(acc, keep, gone):
    _, core, _ = ids()
    half = acc.shape[1] // 2
    left, right = acc[:, :half], acc[:, half:]
    keep[...] = jnp.where(core == 0, left, right).astype(bf16)
    gone[...] = jnp.where(core == 0, right, left).astype(bf16)


def back_a_kernel(
    q_ref, k_ref, v_ref, g_ref, p_ref, n_ref, dd_ref,
    dp_ref, gp_ref, keep_ref, send_ref,
    qv, kv, vv, gv, pv, nv, dqa, dpv, gpv, sems,
):
    mv = Mover(sems)
    L, HL = q_ref.shape
    wins, _ = back_windows(L)
    pairs = range(HL // 128 - 1)
    heads = 2 * len(pairs)
    part = slice(0, len(pairs) * 128)
    gets = [mv.start(v_ref.at[:, part], vv), mv.start(g_ref.at[:, part], gv)]
    blocks = []
    for j, (lo, hi, at) in enumerate(wins):
        w = slice(at, at + hi - lo)
        blocks.append(mv.start(p_ref.at[0:heads, :, w], pv.at[:, :, w]))
        if j == 0:
            gets += [mv.start(q_ref.at[:, part], qv), mv.start(k_ref.at[:, part], kv)]
    later = mv.start(n_ref, nv)
    for op in gets:
        op.wait()

    def done(j, gps):
        lo, hi, at = wins[j]
        for t, gp in enumerate(gps):
            gpv[:, at + t * BLK : at + (t + 1) * BLK] = gp
        mv.put(gpv.at[:, at : at + hi - lo], gp_ref.at[:, at : at + hi - lo])

    zero = jnp.zeros((BLK, BLK), f32)
    head_grads(pairs, 0, wins, blocks, dd_ref, qv, kv, vv, gv, pv, dqa, dpv, lambda j, t: zero, done)
    mv.put(dpv, dp_ref)
    later.wait()
    halves_out(dot(nv[...], dpv[...], 0, 0), keep_ref, send_ref)
    mv.finish()


def back_a_call(q, k, v, g, p, n, dd):
    L, HL = q.shape
    D = n.shape[1]
    heads = HL // HEAD_DIM - 2
    _, wide = back_windows(L)
    width = heads * HEAD_DIM
    part = (L, width)
    return call(
        back_a_kernel,
        "attend_back_a",
        [ANY] * 6 + [None],
        [
            (sds((L, 3 * width), bf16), False),
            (sds((BLK, wide), f32), False),
            (sds((D, 3 * width // 2), bf16), True),
            (sds((D, 3 * width // 2), bf16), True),
        ],
        [(part, bf16)] * 4
        + [((heads, BLK, wide), bf16), ((L, D), bf16), (part, f32), ((L, 3 * width), bf16), ((BLK, wide), f32)],
        8 + 2 * (L // BLK),
        BLK * wide * 128 * 2 * 4 * heads + 2 * L * D * 3 * width,
        18e6,
        q, k, v, g, p, n, dd,
    )


def back_b_kernel(
    q_ref, k_ref, v_ref, g_ref, p_ref, gp_ref, r_ref, dpa_ref, x_ref, w_ref, pq_ref, pk_ref, dd_ref, wpa_ref, wpb_ref,
    gna_ref, gnb_ref, dp_ref, sums_ref,
    qv, kv, vv, gv, pv, gpv, rv, dpav, xv, wv, dqa, pqa, dpv, gnv, sems,
):
    mv = Mover(sems)
    L, HL = q_ref.shape
    D = x_ref.shape[1]
    wins, _ = back_windows(L)
    pair = HL // 128 - 1
    part = slice(pair * 128, HL)
    gets = [mv.start(v_ref.at[:, part], vv), mv.start(g_ref.at[:, part], gv)]
    blocks = []
    for j, (lo, hi, at) in enumerate(wins):
        w = slice(at, at + hi - lo)
        blocks.append(mv.start(p_ref.at[2 * pair : 2 * pair + 2, :, w], pv.at[:, :, w]))
        if j == 0:
            gets += [mv.start(q_ref.at[:, part], qv), mv.start(k_ref.at[:, part], kv), mv.start(gp_ref, gpv)]
    later = [mv.start(r_ref, rv), mv.start(dpa_ref, dpav), mv.start(w_ref, wv), mv.start(x_ref, xv)]
    rr = lax.broadcasted_iota(jnp.int32, (BLK, BLK), 0)
    cc = lax.broadcasted_iota(jnp.int32, (BLK, BLK), 1)
    later_of = jnp.where(rr > cc, 1.0, 0.0).astype(bf16)
    wp = pick_weights(wpa_ref[...], wpb_ref[...])
    scale = HEAD_DIM**-0.5
    sums = [jnp.zeros((1, D), f32)] * 2
    seen = set()
    for op in gets:
        op.wait()

    def done(j, gps):
        lo, hi, at = wins[j]
        here = slice(j * BLK, (j + 1) * BLK)
        if j == 0:
            for op in later:
                op.wait()
        kb = pk_ref[here, :]
        carry = jnp.zeros((BLK, 1), f32)
        dk0 = jnp.zeros((BLK, 128), f32)
        for t in reversed(range((hi - lo) // BLK)):
            i = slice(lo + t * BLK, lo + (t + 1) * BLK)
            b = slice(at + t * BLK, at + (t + 1) * BLK)
            gs = ((carry + dot(gps[t].astype(bf16), later_of)) * rv[:, b].astype(f32)).astype(bf16)
            carry = carry + jnp.sum(gps[t], axis=1, keepdims=True)
            dk0 = dk0 + dot(gs, pq_ref[i, :])
            dq = dot(gs, kb, 0, 0)
            if i.start in seen:
                pqa[i, :] += dq
            else:
                seen.add(i.start)
                pqa[i, :] = dq
        dpv[here, 384:512] = (pltpu.roll(dk0, HEAD_DIM, 1) + pqa[here, :] * scale).astype(bf16)
        gn = dot(dpv[here, 384:], wp, 1, 1)
        n = pair * 128
        for c in range(3):
            gn = gn + dot(dpav[here, c * n : (c + 1) * n], wv[c, :, 0:n], 1, 1)
            gn = gn + dot(dpv[here, c * 128 : (c + 1) * 128], wv[c, :, n:], 1, 1)
        gnv[here, :] = gn.astype(bf16)
        low = (j + 1) * BLK <= L // 2
        to = here if low else slice(here.start - L // 2, here.stop - L // 2)
        mv.put(gnv.at[here, :], (gna_ref if low else gnb_ref).at[to, :])
        mv.put(dpv.at[here, :], dp_ref.at[here, :])
        xhat, _ = standard(xv[here, :].astype(f32))
        sums[0] = sums[0] + jnp.sum(gn * xhat, axis=0, keepdims=True)
        sums[1] = sums[1] + jnp.sum(gn, axis=0, keepdims=True)

    gp_of = lambda j, t: gpv[:, wins[j][2] + t * BLK : wins[j][2] + (t + 1) * BLK]
    head_grads([pair], pair, wins, blocks, dd_ref, qv, kv, vv, gv, pv, dqa, dpv, gp_of, done)
    sums_ref[...] = jnp.concatenate(sums + [jnp.zeros((6, D), f32)], axis=0)
    mv.finish()


def back_b_call(q, k, v, g, p, gp, r, dpa, x, w3, pq, pk, dd, wpa, wpb):
    L, HL = q.shape
    D = x.shape[1]
    _, wide = back_windows(L)
    one = (L, 128)
    return call(
        back_b_kernel,
        "attend_back_b",
        [ANY] * 10 + [None] * 5,
        [(sds((L // 2, D), bf16), False)] * 2 + [(sds((L, 512), bf16), False), (sds((8, D), f32), True)],
        [(one, bf16)] * 4
        + [
            ((2, BLK, wide), bf16),
            ((BLK, wide), f32),
            ((BLK, wide), bf16),
            (dpa.shape, bf16),
            ((L, D), bf16),
            ((3, D, HL), bf16),
            (one, f32),
            (one, f32),
            ((L, 512), bf16),
            ((L, D), bf16),
        ],
        9 + 3 * (L // BLK),
        BLK * wide * 128 * 2 * 4 * 3 + 2 * L * D * (3 * HL + 128),
        20e6,
        q, k, v, g, p, gp, r, dpa, x, w3, pq, pk, dd, wpa, wpb,
    )


def dw_kernel(n_ref, dp_ref, keep_ref, send_ref, sems):
    halves_out(dot(n_ref[...], dp_ref[...], 0, 0), keep_ref, send_ref)


def dw_call(n, dp):
    L, D = n.shape
    N = dp.shape[1]
    half = sds((D, N // 2), bf16)
    return call(
        dw_kernel, "dw_last", [None] * 2, [(half, True), (half, True)], [], 1, 2 * L * D * N, 4e6, n, dp
    )


def last_kernel(x_ref, ga_ref, gb_ref, gm_ref, g_ref, *rest):
    o_ref = rest[-1]
    xhat, rstd = standard(x_ref[...].astype(f32))
    gn = ga_ref[...].astype(f32) + gb_ref[...].astype(f32)
    o_ref[...] = gm_ref[...].astype(f32) + norm_back(xhat, rstd, row_of(g_ref), gn)


def last_call(half, whole, x, ga, gb, gm, gain):
    L, D = x.shape
    steps = 2
    mine = spec((L // 2 // steps, D), lambda i: (i, 0))
    far = spec((L // 2 // steps, D), lambda i: (i + steps * half, 0))
    more = [] if whole is None else [whole]
    return pl.pallas_call(
        last_kernel,
        grid=(steps,),
        in_specs=[far, mine, mine, far, spec((D,))] + [ANY] * len(more),
        out_specs=far,
        out_shape=sds((L, D), f32),
        input_output_aliases={5: 0} if more else {},
        compiler_params=params(),
        cost_estimate=cost(1e3, 1e3),
        name="norm_back",
    )(x, ga, gb, gm, gain, *more)


def links(dp, tensor):
    def swap(bit):
        return [(p * tensor + t, (p ^ bit) * tensor + t) for p in range(dp) for t in range(tensor)]

    across = [(p * tensor + t, p * tensor + (1 - t)) for p in range(dp) for t in range(tensor)]
    head_zero = [(p * tensor, p * tensor + 1) for p in range(dp)]
    return swap, across, head_zero


def after(value, *others):
    return lax.optimization_barrier((value, *others))[0]


def after3(a, b, c, *others):
    return lax.optimization_barrier((a, b, c, *others))[:3]


def shards(
    dp,
    tensor,
    tokens,
    lengths,
    cotangent,
    norm_gain_one,
    norm_shift_one,
    w_qkv,
    w_out,
    b_out,
    norm_gain_two,
    norm_shift_two,
    w_up,
    b_up,
    w_down,
    b_down,
):
    _, L, D = tokens.shape
    HL = w_out.shape[0]
    F = w_up.shape[1]
    swap, across, head_zero = links(dp, tensor)
    t = lax.axis_index("tensor")
    d = lax.axis_index("dp")
    core = d % 2
    groups = dp // 2
    rows = D // groups
    send = lambda a, perm: lax.ppermute(a, AXES, perm)

    def sum_dp(v):
        bit = 1
        while bit < dp:
            v = v + send(v, swap(bit))
            bit *= 2
        return v

    def fold(pieces, bit):
        totals = [(keep.astype(f32) + got.astype(f32)).astype(bf16) for keep, got in pieces]
        totals = [a.reshape(groups // (2 * bit), 2, rows, a.shape[-1]) for a in totals]
        mine = (d // (2 * bit)) % 2
        pick = lambda which: jnp.concatenate([lax.dynamic_index_in_dim(a, which, 1, False) for a in totals], axis=-1)
        return pick(mine), pick(1 - mine)

    def finish(keep, got):
        total = (keep.astype(f32) + got.astype(f32)).reshape(2, rows // 2, keep.shape[-1])
        mine = lax.dynamic_index_in_dim(total, core, 0, False)
        got = send(after(lax.dynamic_index_in_dim(total, 1 - core, 0, False), gn_b_got), swap(1))
        return jnp.where(core == 0, mine, got), jnp.where(core == 0, got, mine)

    x = tokens.reshape(L, D)
    cot = cotangent.reshape(L, D)
    w3 = jnp.transpose(w_qkv, (1, 0, 2))

    wp_own = pick_call(w3)
    one, two = pack_call(w_down, w_up, w_out, after(b_up, wp_own))
    wp_got = send(wp_own, head_zero)
    q, k, v, n1 = start_call(after(x, one), w3, norm_gain_one, norm_shift_one)
    one_x, two_x = send(one, across), send(two, across)
    ctx, inv, pq, pk, prob, reach = attend_call(lengths, n1, wp_own, wp_got, q, k, v)
    ctx_b = send(ctx, across)
    one_y = send(after(one_x, ctx), swap(2))
    ga, cot_sum = cot_call(after(cot, ctx), w_down)
    two_y = send(after(two_x, ga, one_y), swap(2))
    one_x, one_y = lax.optimization_barrier((one_x, one_y, ga))[:2]
    ones = [one_x, one_y, send(one_x, swap(1)), send(one_y, swap(1))]
    mid, n2, gn2, mo, keep_a, gone_a, dbu = own_call(
        x, ctx, after(ctx_b, ga), w_out, ones, w_up, w_down, ga, cot, b_out, norm_gain_two, norm_shift_two, b_up
    )
    got_a = send(after(gone_a, two_y), swap(1))
    two_x, two_y = lax.optimization_barrier((two_x, two_y, mid))[:2]
    twos = [two_x, two_y, send(two_x, swap(1)), send(two_y, swap(1))]
    keep_a, gone_a = fold([(keep_a, got_a)], 1)
    got_a = send(gone_a, swap(2))
    out, gm, gc, dd, sums2, keep_o, gone_o = other_call(
        n2, after(cot, gone_a), one_x, twos, gn2, mo, mid, w_out, ctx, norm_gain_two, b_down, inv
    )
    got_o = send(gone_o, swap(1))
    dp_a, gp, keep_c, gone_c = back_a_call(q, k, v, gc, prob, n1, dd)
    got_c = send(gone_c, swap(1))
    keep_a, gone_a = fold([(keep_a, after(got_a, dp_a))], 2)
    got_a = send(gone_a, swap(4))
    gn_a, gn_b, dp_b, sums1 = back_b_call(
        q, k, v, gc, prob, after(gp, gone_a), reach, dp_a, x, w3, pq, pk, dd, wp_own, wp_got
    )
    gn_a_got = send(gn_a, across)
    gn_b_got = send(gn_b, across)
    keep_d, gone_d = dw_call(n1, dp_b)
    got_d = send(gone_d, swap(1))
    got_c = after(got_c, dp_b)
    keep_c, gone_c = fold([(keep_c, got_c), (keep_o, got_o), (keep_d, got_d)], 1)
    got_c = send(gone_c, swap(2))
    keep_c, gone_c = fold([(keep_c, got_c)], 2)
    got_c = send(gone_c, swap(4))

    small = jnp.concatenate(
        [sums1[:2].reshape(-1), sums2[:3].reshape(-1), cot_sum.reshape(-1), dbu.reshape(-1)]
    ).reshape(-1, 128)
    small = sum_dp(after(small, gone_c))
    late = small[: 2 * D // 128]
    late = (late + send(after(late, gn_b_got), across)).reshape(2, D)
    early = small[2 * D // 128 :].reshape(-1)

    def rest(keep, got, bit):
        while 2 * bit < dp:
            keep, gone = fold([(keep, got)], bit)
            bit *= 2
            got = send(after(gone, gn_a_got), swap(bit))
        return finish(keep, got)

    keep_a, gone_a = fold([(keep_a, got_a)], 4)
    left_a, right_a = rest(keep_a, send(gone_a, swap(8)), 8)
    left_c, right_c = rest(keep_c, got_c, 4)
    up_share, down_share = left_a, right_a
    n = 3 * (HL - 128) // 2
    m = n + HL // 2
    out_share = jnp.concatenate([left_c[:, n:m], right_c[:, n:m]], axis=1)
    c = jnp.concatenate([left_c[:, :n], right_c[:, :n]], axis=1).reshape(-1, 3, HL - 128)
    e = jnp.concatenate([left_c[:, m:], right_c[:, m:]], axis=1)
    extra = e[:, 384:]
    extra = extra + send(after(extra, gn_b_got), across)
    extra = jnp.where(t == 0, extra, jnp.zeros_like(extra))
    zeros = jnp.zeros((extra.shape[0], HL - HEAD_DIM), f32)
    extra = jnp.concatenate(
        [extra[:, :HEAD_DIM], zeros, extra[:, HEAD_DIM:], zeros, jnp.zeros((extra.shape[0], HL), f32)], axis=1
    )
    qkv_share = jnp.concatenate([c, e[:, :384].reshape(-1, 3, 128)], axis=2) + extra.reshape(-1, 3, HL)
    grad_tokens = last_call(0, None, x, gn_a, gn_a_got, gm, norm_gain_one)
    grad_tokens = last_call(1, grad_tokens, x, gn_b, gn_b_got, gm, norm_gain_one)
    return (
        out.reshape(1, L, D),
        grad_tokens.reshape(1, L, D),
        late[0],
        late[1],
        qkv_share,
        out_share.T,
        early[2 * D : 3 * D],
        early[:D],
        early[D : 2 * D],
        up_share,
        early[4 * D :],
        down_share.T,
        early[3 * D : 4 * D],
    )


def solution(mesh):
    in_specs = (
        P("dp", None, None),
        P("dp", None),
        P("dp", None, None),
        P(),
        P(),
        P(None, None, "tensor"),
        P("tensor", None),
        P(),
        P(),
        P(),
        P(None, "tensor"),
        P("tensor"),
        P("tensor", None),
        P(),
    )
    out_specs = (
        P("dp", None, None),
        P("dp", None, None),
        P(),
        P(),
        P("dp", None, "tensor"),
        P("tensor", "dp"),
        P(),
        P(),
        P(),
        P("dp", "tensor"),
        P("tensor"),
        P("tensor", "dp"),
        P(),
    )
    body = functools.partial(shards, mesh.shape["dp"], mesh.shape["tensor"])
    return jax.shard_map(body, mesh=mesh, in_specs=in_specs, out_specs=out_specs, check_vma=False)
```

```python
import functools

import jax
import jax.numpy as jnp
from jax import lax
from jax.experimental import pallas as pl
from jax.experimental.pallas import tpu as pltpu
from jax.sharding import PartitionSpec as P

HEAD_DIM = 64
LONGEST = 512
BLK = 256
EPS = 1e-05
FAR = 1e30
AXES = ("dp", "tensor")
f32 = jnp.float32
bf16 = jnp.bfloat16


def dot(a, b, ca=1, cb=0, precision=None):
    return lax.dot_general(
        a, b, (((ca,), (cb,)), ((), ())), preferred_element_type=f32, precision=precision
    )


def spec(shape, index=None):
    if index is None:
        zeros = (0,) * len(shape)
        return pl.BlockSpec(shape, lambda *_: zeros)
    return pl.BlockSpec(shape, index)


def params(mib=60):
    return pltpu.CompilerParams(vmem_limit_bytes=60 * 1024 * 1024)


ANY = pl.BlockSpec(memory_space=pl.ANY)
SMEM = pl.BlockSpec(memory_space=pltpu.SMEM)


def sds(shape, dtype):
    return jax.ShapeDtypeStruct(shape, dtype)


def cost(flops, nbytes, trans=0):
    return pl.CostEstimate(flops=int(flops), bytes_accessed=int(nbytes), transcendentals=int(trans))


def starts_at(pos, lengths_ref, docs):
    start = jnp.zeros_like(pos)
    end = lengths_ref[0, 0]
    for d in range(1, docs):
        start = jnp.where(pos >= end, end, start)
        end = end + lengths_ref[0, d]
    return start


def standard(x):
    mean = jnp.mean(x, axis=-1, keepdims=True)
    c = x - mean
    var = jnp.mean(c * c, axis=-1, keepdims=True)
    rstd = lax.rsqrt(var + EPS)
    return c * rstd, rstd


def norm_back(xhat, rstd, gain, grad):
    gg = grad * gain
    m1 = jnp.mean(gg, axis=-1, keepdims=True)
    m2 = jnp.mean(gg * xhat, axis=-1, keepdims=True)
    return rstd * (gg - m1 - xhat * m2)


def ids():
    d = lax.axis_index("dp")
    return lax.axis_index("tensor"), lax.rem(d, 2), lax.rem(d // 2, 2)


def quarters():
    _, core, y = ids()
    return [2 * y + core, 2 * (1 - y) + core, 2 * y + 1 - core, 2 * (1 - y) + 1 - core]


def pick_weights(own, got):
    t, _, _ = ids()
    return jnp.where(t == 0, own.astype(f32), got.astype(f32)).astype(bf16)


class Mover:
    def __init__(self, sems):
        self.sems, self.count, self.open = sems, 0, []

    def start(self, src, dst):
        op = pltpu.make_async_copy(src, dst, self.sems.at[self.count])
        self.count += 1
        op.start()
        return op

    def put(self, src, dst):
        self.open.append(self.start(src, dst))

    def finish(self):
        for op in self.open:
            op.wait()


def row_of(ref):
    return ref[...].reshape(1, -1)


LIGHT = ("mlp_own", "dw_last", "norm_qkv", "cot_down")


def call(kernel, name, ins, outs, scratch, sems, flops, nbytes, *args):
    full = lambda a: pl.BlockSpec(memory_space=pltpu.VMEM)
    return pl.pallas_call(
        kernel,
        in_specs=[full(a) if s is None else s for s, a in zip(ins, args, strict=True)],
        out_specs=[full(o) if inside else ANY for o, inside in outs],
        out_shape=[o for o, _ in outs],
        scratch_shapes=[pltpu.VMEM(s, t) for s, t in scratch] + [pltpu.SemaphoreType.DMA((sems,))],
        compiler_params=params(),
        cost_estimate=cost(1e3, 1e3) if name in LIGHT else cost(flops, nbytes),
        name=name,
    )(*args)


def pick_kernel(w_ref, wp_ref, qv, kv, sems):
    mv = Mover(sems)
    a = mv.start(w_ref.at[0, :, 0:128], qv)
    b = mv.start(w_ref.at[1, :, 0:128], kv)
    a.wait()
    b.wait()
    lane = lax.broadcasted_iota(jnp.int32, (1, 128), 1)
    k = pltpu.roll(kv[...].astype(f32), HEAD_DIM, 1)
    wp_ref[...] = jnp.where(lane < HEAD_DIM, qv[...].astype(f32), k).astype(bf16)


def pick_call(w3):
    D = w3.shape[1]
    return call(
        pick_kernel, "pick", [ANY], [(sds((D, 128), bf16), True)], [((D, 128), bf16)] * 2, 2, 1e3, 4e5, w3
    )[0]


def pack_kernel(wd_ref, wu_ref, wo_ref, bu_ref, one_ref, two_ref, onev, twov, sems):
    mv = Mover(sems)
    _, core, y = ids()
    s = 2 * y + core
    D = wo_ref.shape[1]
    ro, ru, rd = wo_ref.shape[0] // 4, wu_ref.shape[0] // 4, wd_ref.shape[0] // 4
    halves = wu_ref.shape[1] // D
    from_row = lambda n: pl.ds(pl.multiple_of(s * n, 16), n)
    get_one = mv.start(wo_ref.at[from_row(ro)], onev.at[0:ro])
    packs = []
    for h in range(halves):
        packs.append(mv.start(wu_ref.at[from_row(ru), h * D : (h + 1) * D], twov.at[h * ru : (h + 1) * ru]))
    packs.append(mv.start(wd_ref.at[from_row(rd)], twov.at[halves * ru : halves * ru + rd]))
    rest = row_of(bu_ref)
    pieces = []
    for _ in range(3):
        piece = rest.astype(bf16)
        rest = rest - piece.astype(f32)
        pieces.append(piece.astype(f32))
    flat = [p[:, h * D : (h + 1) * D] for p in pieces for h in range(halves)]
    onev[ro : ro + 16, :] = jnp.concatenate(flat + [jnp.zeros((16 - len(flat), D), f32)], axis=0).astype(bf16)
    get_one.wait()
    mv.put(onev, one_ref)
    for op in packs:
        op.wait()
    mv.put(twov, two_ref)
    mv.finish()


def pack_call(w_down, w_up, w_out, b_up):
    F, D = w_down.shape
    one = w_out.shape[0] // 4 + 16
    two = (w_up.shape[0] * (F // D) + F) // 4
    return call(
        pack_kernel,
        "pack",
        [ANY] * 3 + [None],
        [(sds((one, D), bf16), False), (sds((two, D), bf16), False)],
        [((one, D), bf16), ((two, D), bf16)],
        8,
        1e3,
        3e6,
        w_down, w_up, w_out, b_up,
    )


def start_kernel(x_ref, w_ref, g_ref, b_ref, q_ref, k_ref, v_ref, n_ref, xv, wv, nv, qv, kv, vv, sems):
    mv = Mover(sems)
    L, D = x_ref.shape
    half = L // 2
    gets = [mv.start(x_ref.at[0:half], xv.at[0:half]), mv.start(w_ref, wv), mv.start(x_ref.at[half:L], xv.at[half:L])]
    gain, shift = row_of(g_ref), row_of(b_ref)
    gets[0].wait()
    for m in range(L // BLK):
        r = slice(m * BLK, (m + 1) * BLK)
        if m * BLK == half:
            gets[2].wait()
        xhat, _ = standard(xv[r, :].astype(f32))
        n = (xhat * gain + shift).astype(bf16)
        nv[r, :] = n
        if m == 0:
            gets[1].wait()
        qv[r, :] = (dot(n, wv[0]).astype(bf16).astype(f32) * HEAD_DIM**-0.5).astype(bf16)
        kv[r, :] = dot(n, wv[1]).astype(bf16)
        vv[r, :] = dot(n, wv[2]).astype(bf16)
        if (m + 1) * BLK % half == 0:
            done = slice((m + 1) * BLK - half, (m + 1) * BLK)
            for src, dst in ((nv, n_ref), (qv, q_ref), (kv, k_ref), (vv, v_ref)):
                mv.put(src.at[done, :], dst.at[done, :])
    mv.finish()


def start_call(x, w3, gain, shift):
    L, D = x.shape
    HL = w3.shape[2]
    half = (L, HL)
    return call(
        start_kernel,
        "norm_qkv",
        [ANY] * 2 + [None] * 2,
        [(sds(half, bf16), False)] * 3 + [(sds((L, D), bf16), False)],
        [((L, D), bf16), ((3, D, HL), bf16), ((L, D), bf16)] + [(half, bf16)] * 3,
        11,
        2 * L * D * 3 * HL,
        9e6,
        x, w3, gain, shift,
    )


def cot_kernel(c_ref, wd_ref, ga_ref, cs_ref, cv, wdv, gav, sems):
    mv = Mover(sems)
    L, D = c_ref.shape
    gets = [mv.start(c_ref, cv), mv.start(wd_ref, wdv)]
    for op in gets:
        op.wait()
    cs = jnp.zeros((1, D), f32)
    for m in range(L // BLK):
        r = slice(m * BLK, (m + 1) * BLK)
        c = cv[r, :]
        cs = cs + jnp.sum(c.astype(f32), axis=0, keepdims=True)
        gav[r, :] = dot(c, wdv[...], 1, 1).astype(bf16)
        mv.put(gav.at[r, :], ga_ref.at[r, :])
    cs_ref[...] = cs
    mv.finish()


def cot_call(c, w_down):
    L, D = c.shape
    F = w_down.shape[0]
    return call(
        cot_kernel,
        "cot_down",
        [ANY] * 2,
        [(sds((L, F), bf16), False), (sds((1, D), f32), True)],
        [((L, D), bf16), ((F, D), bf16), ((L, F), bf16)],
        2 + L // BLK,
        2 * L * D * F,
        7e6,
        c, w_down,
    )


def windows(L):
    reach = LONGEST // BLK
    return [range(max(0, i - reach), i + 1) for i in range(L // BLK)]


def back_windows(L):
    reach = LONGEST // BLK
    found, at = [], 0
    for j in range(L // BLK):
        lo, hi = j * BLK, min(L, (j + reach + 1) * BLK)
        found.append((lo, hi, at))
        at += hi - lo
    return found, at


def attend_kernel(
    docs, strength, len_ref, n_ref, wpa_ref, wpb_ref, q_ref, k_ref, v_ref,
    ctx_ref, inv_ref, pq_ref, pk_ref, p_ref, r_ref,
    nv, qv, kv, vv, vt, cv, pv, rv, bias_ref, sems,
):
    mv = Mover(sems)
    get_n = mv.start(n_ref, nv)
    get_v = mv.start(v_ref, vv)
    get_q = mv.start(q_ref, qv)
    get_k = mv.start(k_ref, kv)
    L, HL = q_ref.shape
    wins, _ = back_windows(L)
    lane = lax.broadcasted_iota(jnp.int32, (1, 128), 1)
    left = lane < HEAD_DIM
    w = pick_weights(wpa_ref[...], wpb_ref[...])
    get_n.wait()
    both = dot(nv[...], w)
    pq_ref[...] = jnp.where(left, both.astype(bf16).astype(f32) * HEAD_DIM**-0.5, 0.0).astype(bf16)
    pk_ref[...] = jnp.where(left, pltpu.roll(both, HEAD_DIM, 1), 0.0).astype(bf16)
    get_v.wait()
    for m in range(L // BLK):
        vt[:, m * BLK : (m + 1) * BLK] = vv[m * BLK : (m + 1) * BLK, :].T
    rows = lax.broadcasted_iota(jnp.int32, (BLK, BLK), 0)
    cols = lax.broadcasted_iota(jnp.int32, (BLK, BLK), 1)
    above = jnp.where(rows < cols, 1.0, 0.0).astype(bf16)
    carry = [jnp.zeros((BLK, 1), f32)] * (L // BLK)
    get_q.wait()
    get_k.wait()
    for i, blocks in enumerate(windows(L)):
        mine = slice(i * BLK, (i + 1) * BLK)
        ipos = i * BLK + lax.broadcasted_iota(jnp.int32, (1, BLK), 1)
        istart = starts_at(ipos, len_ref, docs)
        places = {}
        for j in blocks:
            here = slice(j * BLK, (j + 1) * BLK)
            at = wins[j][2] + (i - j) * BLK
            places[j] = slice(at, at + BLK)
            s = dot(pk_ref[here, :], pq_ref[mine, :], 1, 1)
            jpos = j * BLK + lax.broadcasted_iota(jnp.int32, (BLK, 1), 0)
            inside = jpos >= istart
            fresh = jpos != starts_at(jpos, len_ref, docs)
            if j == i:
                allowed = inside & (jpos <= ipos)
                selectable = inside & (jpos < ipos) & fresh
            else:
                allowed, selectable = inside, inside & fresh
            r = jnp.where(selectable, jnp.maximum(s, 0.0), 0.0)
            rv[:, places[j]] = (r * (2.0 * strength)).astype(bf16)
            c = r * r
            pen = strength * (carry[j] + dot(c.astype(bf16), above))
            bias_ref[j - blocks[0]] = jnp.where(allowed, pen, FAR)
            if i + 1 < L // BLK and j in windows(L)[i + 1]:
                carry[j] = carry[j] + jnp.sum(c, axis=1, keepdims=True)
        invs, outs = [], []
        for h in range(HL // HEAD_DIM):
            cs = slice(h // 2 * 128, (h // 2 + 1) * 128)
            q = jnp.where((lane // HEAD_DIM) == h % 2, qv[mine, cs], jnp.zeros((BLK, 128), bf16))
            ss = [dot(kv[j * BLK : (j + 1) * BLK, cs], q, 1, 1) - bias_ref[j - blocks[0]] for j in blocks]
            top = functools.reduce(jnp.maximum, [jnp.max(s, axis=0, keepdims=True) for s in ss])
            total = jnp.zeros((1, BLK), f32)
            out = jnp.zeros((HEAD_DIM, BLK), f32)
            for j, s in zip(blocks, ss, strict=True):
                e = jnp.exp(s - top)
                total = total + jnp.sum(e, axis=0, keepdims=True)
                e = e.astype(bf16)
                pv[h, :, places[j]] = e
                out = out + dot(vt[h * HEAD_DIM : (h + 1) * HEAD_DIM, j * BLK : (j + 1) * BLK], e)
            inv = 1.0 / total
            invs.append(inv)
            outs.append(out * inv)
        inv_ref[:, mine] = jnp.concatenate(invs + [jnp.zeros((8 - len(invs), BLK), f32)], axis=0)
        for p in range(HL // 128):
            pair = jnp.concatenate(outs[2 * p : 2 * p + 2], axis=0)
            cv[mine, p * 128 : (p + 1) * 128] = pair.T.astype(bf16)
        mv.put(cv.at[mine, :], ctx_ref.at[mine, :])
        for j in blocks:
            mv.put(pv.at[:, :, places[j]], p_ref.at[:, :, places[j]])
    mv.put(rv, r_ref)
    mv.finish()


def attend_call(lengths, n, wpa, wpb, q, k, v):
    L, HL = q.shape
    D = n.shape[1]
    heads = HL // HEAD_DIM
    _, wide = back_windows(L)
    half = (L, HL)
    return call(
        functools.partial(attend_kernel, lengths.shape[1], 2.0 / L),
        "attend",
        [SMEM, ANY, None, None, ANY, ANY, ANY],
        [
            (sds(half, bf16), False),
            (sds((8, L), f32), True),
            (sds((L, 128), bf16), True),
            (sds((L, 128), bf16), True),
            (sds((heads, BLK, wide), bf16), False),
            (sds((BLK, wide), bf16), False),
        ],
        [((L, D), bf16)]
        + [(half, bf16)] * 3
        + [
            ((HL, L), bf16),
            (half, bf16),
            ((heads, BLK, wide), bf16),
            ((BLK, wide), bf16),
            ((LONGEST // BLK + 1, BLK, BLK), f32),
        ],
        5 + L // BLK + wide // BLK,
        1e12,
        14e6,
        lengths, n, wpa, wpb, q, k, v,
    )


C0 = 0.7978845608028654
C1 = 0.044715
CHUNK = 512


def gelu_pair(u):
    u2 = u * u
    t = jnp.tanh(u * (C0 + (C0 * C1) * u2))
    h = 0.5 + 0.5 * t
    a = u * h
    d = h + a * (1.0 - h) * (2.0 * C0 + (6.0 * C0 * C1) * u2)
    return a, d


def own_kernel(
    x_ref, ca_ref, cb_ref, wo_ref, p0_ref, p1_ref, p2_ref, p3_ref, wu_ref, wd_ref, ga_ref, c_ref,
    bo_ref, g_ref, b_ref, bu_ref,
    mid_ref, n_ref, gn_ref, mo_ref, keep_ref, send_ref, dbu_ref,
    xv, cav, cbv, wov, wbv, wuv, wdv, gav, cv, mv_, nv, gnv, mov, av, guv, keepv, sendv, sems,
):
    mv = Mover(sems)
    L, D = x_ref.shape
    F = wu_ref.shape[1]
    HL = ca_ref.shape[1]
    _, core, _ = ids()
    gets = [mv.start(ca_ref, cav), mv.start(wo_ref, wov), mv.start(cb_ref, cbv), mv.start(x_ref, xv)]
    ro, at = HL // 4, 0
    for part, slot in zip((p0_ref, p1_ref, p2_ref, p3_ref), quarters()):
        gets.append(mv.start(part.at[at : at + ro], wbv.at[pl.ds(pl.multiple_of(slot * ro, 16), ro)]))
    later = [mv.start(wu_ref, wuv), mv.start(ga_ref, gav), mv.start(wd_ref, wdv), mv.start(c_ref, cv)]
    bo, gain, shift, bu = row_of(bo_ref), row_of(g_ref), row_of(b_ref), row_of(bu_ref)
    for op in gets:
        op.wait()
    for m in range(L // BLK):
        r = slice(m * BLK, (m + 1) * BLK)
        att = dot(cav[r, :], wov[...]) + dot(cbv[r, :], wbv[...])
        mid = xv[r, :].astype(f32) + (att + bo)
        mv_[r, :] = mid
        xhat, _ = standard(mid)
        nv[r, :] = (xhat * gain + shift).astype(bf16)
    mv.put(mv_, mid_ref)
    mv.put(nv, n_ref)
    for op in later:
        op.wait()
    for j in range(F // CHUNK):
        at = slice(j * CHUNK, (j + 1) * CHUNK)
        db = jnp.zeros((1, CHUNK), f32)
        for m in range(L // BLK):
            r = slice(m * BLK, (m + 1) * BLK)
            a, d = gelu_pair(dot(nv[r, :], wuv[:, at]) + bu[:, at])
            a = a.astype(bf16)
            gu = d * gav[r, at].astype(f32)
            db = db + jnp.sum(gu, axis=0, keepdims=True)
            gu = gu.astype(bf16)
            av[r, :] = a
            guv[r, :] = gu
            mo = dot(a, wdv[at, :])
            gn = dot(gu, wuv[:, at], 1, 1)
            if j == 0:
                mov[r, :] = mo
                gnv[r, :] = gn
            else:
                mov[r, :] += mo
                gnv[r, :] += gn
        dbu_ref[:, at] = db
        dwu = dot(nv[...], guv[...], 0, 0)
        dwd = dot(cv[...], av[...], 0, 0)
        keepv[:, at] = jnp.where(core == 0, dwu, dwd).astype(bf16)
        sendv[:, at] = jnp.where(core == 0, dwd, dwu).astype(bf16)
        mv.put(sendv.at[:, at], send_ref.at[:, at])
        mv.put(keepv.at[:, at], keep_ref.at[:, at])
        if j == F // CHUNK - 1:
            mv.put(gnv, gn_ref)
            mv.put(mov, mo_ref)
    mv.finish()


def own_call(x, ca, cb, w_out, parts, w_up, w_down, ga, c, b_out, gain, shift, b_up):
    L, D = x.shape
    HL = ca.shape[1]
    F = w_up.shape[1]
    return call(
        own_kernel,
        "mlp_own",
        [ANY] * 12 + [None] * 4,
        [
            (sds((L, D), f32), False),
            (sds((L, D), bf16), False),
            (sds((L, D), f32), False),
            (sds((L, D), f32), False),
            (sds((D, F), bf16), False),
            (sds((D, F), bf16), False),
            (sds((1, F), f32), True),
        ],
        [
            ((L, D), bf16),
            ((L, HL), bf16),
            ((L, HL), bf16),
            ((HL, D), bf16),
            ((HL, D), bf16),
            ((D, F), bf16),
            ((F, D), bf16),
            ((L, F), bf16),
            ((L, D), bf16),
            ((L, D), f32),
            ((L, D), bf16),
            ((L, D), f32),
            ((L, D), f32),
            ((L, CHUNK), bf16),
            ((L, CHUNK), bf16),
            ((D, F), bf16),
            ((D, F), bf16),
        ],
        16 + 2 * (F // CHUNK),
        2 * L * D * F * 5 + 4 * L * D * HL,
        36e6,
        x, ca, cb, w_out, *parts, w_up, w_down, ga, c, b_out, gain, shift, b_up,
    )


def other_kernel(
    n_ref, c_ref, a0_ref, d0_ref, d1_ref, d2_ref, d3_ref, gn_ref, mo_ref, mid_ref, wo_ref, ctx_ref,
    g_ref, bd_ref, inv_ref,
    out_ref, gm_ref, gc_ref, dd_ref, sums_ref, keep_ref, send_ref,
    nv, cv, wuv, wdv, bv, gnv, mov, midv, wov, ctxv, gna, moa, outv, gmv, gcv, sems,
):
    mv = Mover(sems)
    L, D = n_ref.shape
    F = wdv.shape[0]
    HL = ctx_ref.shape[1]
    halves = F // D
    gets = [mv.start(n_ref, nv)]
    parts = list(zip((d0_ref, d1_ref, d2_ref, d3_ref), quarters()))
    ru, rd = D // 4, F // 4
    for part, slot in parts:
        for h in range(halves):
            dst = wuv.at[pl.ds(pl.multiple_of(slot * ru, 16), ru), h * D : (h + 1) * D]
            gets.append(mv.start(part.at[h * ru : (h + 1) * ru], dst))
    n = a0_ref.shape[0]
    gets.append(mv.start(a0_ref.at[n - 16 : n], bv))
    downs = [mv.start(c_ref, cv)]
    for part, slot in parts:
        dst = wdv.at[pl.ds(pl.multiple_of(slot * rd, 16), rd)]
        downs.append(mv.start(part.at[halves * ru : halves * ru + rd], dst))
    _, core, _ = ids()
    later = [
        mv.start(src, dst)
        for src, dst in ((gn_ref, gnv), (mo_ref, mov), (mid_ref, midv), (wo_ref, wov), (ctx_ref, ctxv))
    ]
    gain, bd = row_of(g_ref), row_of(bd_ref)
    for op in gets:
        op.wait()
    b = bv[...].astype(f32)
    bu = [b[h : h + 1] + b[halves + h : halves + h + 1] + b[2 * halves + h : 2 * halves + h + 1] for h in range(halves)]
    bu = jnp.concatenate(bu, axis=1)
    for j in range(F // CHUNK):
        at = slice(j * CHUNK, (j + 1) * CHUNK)
        for m in range(L // BLK):
            r = slice(m * BLK, (m + 1) * BLK)
            a, d = gelu_pair(dot(nv[r, :], wuv[:, at]) + bu[:, at])
            if j == 0 and m == 0:
                for op in downs:
                    op.wait()
            gu = (d * dot(cv[r, :], wdv[at, :], 1, 1)).astype(bf16)
            mo = dot(a.astype(bf16), wdv[at, :])
            gn = dot(gu, wuv[:, at], 1, 1)
            if j == 0:
                moa[r, :] = mo
                gna[r, :] = gn
            else:
                moa[r, :] += mo
                gna[r, :] += gn
    for op in later:
        op.wait()
    heads = lax.broadcasted_iota(jnp.int32, (8, HL), 0)
    lane = lax.broadcasted_iota(jnp.int32, (8, HL), 1)
    pick = jnp.where(lane // HEAD_DIM == heads, 1.0, 0.0).astype(bf16)
    s0 = s1 = s2 = jnp.zeros((1, D), f32)
    for m in range(L // BLK):
        r = slice(m * BLK, (m + 1) * BLK)
        mid = midv[r, :]
        outv[r, :] = (mid + (mov[r, :] + moa[r, :]) + bd).astype(bf16)
        gn = gnv[r, :] + gna[r, :]
        xhat, rstd = standard(mid)
        gm = cv[r, :].astype(f32) + norm_back(xhat, rstd, gain, gn)
        s0 = s0 + jnp.sum(gn * xhat, axis=0, keepdims=True)
        s1 = s1 + jnp.sum(gn, axis=0, keepdims=True)
        s2 = s2 + jnp.sum(gm, axis=0, keepdims=True)
        gb = gm.astype(bf16)
        gmv[r, :] = gb
        inv = inv_ref[:, r]
        high = inv.astype(bf16)
        low = (inv - high.astype(f32)).astype(bf16)
        gc = (dot(gb, wov[...], 1, 1) * (dot(high, pick, 0, 0) + dot(low, pick, 0, 0))).astype(bf16)
        gcv[r, :] = gc
        prod = gc.astype(f32) * ctxv[r, :].astype(f32)
        high = prod.astype(bf16)
        low = (prod - high.astype(f32)).astype(bf16)
        dd_ref[:, r] = dot(pick, high, 1, 1) + dot(pick, low, 1, 1)
        if m == L // BLK // 2 - 1 or m == L // BLK - 1:
            half = slice((m + 1) * BLK - L // 2, (m + 1) * BLK)
            for src, dst in ((gcv, gc_ref), (gmv, gm_ref), (outv, out_ref)):
                mv.put(src.at[half, :], dst.at[half, :])
    sums_ref[...] = jnp.concatenate([s0, s1, s2, jnp.zeros((5, D), f32)], axis=0)
    dwo = dot(gmv[...], ctxv[...], 0, 0)
    left, right = dwo[:, : HL // 2], dwo[:, HL // 2 :]
    keep_ref[...] = jnp.where(core == 0, left, right).astype(bf16)
    send_ref[...] = jnp.where(core == 0, right, left).astype(bf16)
    mv.finish()


def other_call(n, c, one, twos, gn, mo, mid, w_out, ctx, gain, b_down, inv):
    L, D = n.shape
    HL = ctx.shape[1]
    F = twos[0].shape[0] * 2
    return call(
        other_kernel,
        "mlp_other",
        [ANY] * 12 + [None] * 3,
        [
            (sds((L, D), bf16), False),
            (sds((L, D), bf16), False),
            (sds((L, HL), bf16), False),
            (sds((8, L), f32), True),
            (sds((8, D), f32), True),
            (sds((D, HL // 2), bf16), True),
            (sds((D, HL // 2), bf16), True),
        ],
        [
            ((L, D), bf16),
            ((L, D), bf16),
            ((D, F), bf16),
            ((F, D), bf16),
            ((16, D), bf16),
            ((L, D), f32),
            ((L, D), f32),
            ((L, D), f32),
            ((HL, D), bf16),
            ((L, HL), bf16),
            ((L, D), f32),
            ((L, D), f32),
            ((L, D), bf16),
            ((L, D), bf16),
            ((L, HL), bf16),
        ],
        4 * (F // D) + 4 + 8 + 6,
        2 * L * D * F * 4 + 2 * L * D * HL,
        30e6,
        n, c, one, *twos, gn, mo, mid, w_out, ctx, gain, b_down, inv,
    )


def head_grads(pairs, offset, wins, blocks, dd_ref, qv, kv, vv, gv, pv, dqa, dpv, gp_of, done):
    width = len(pairs) * 128
    scale = HEAD_DIM**-0.5
    lane = lax.broadcasted_iota(jnp.int32, (1, 128), 1)
    seen = set()
    for j, (lo, hi, at) in enumerate(wins):
        here = slice(j * BLK, (j + 1) * BLK)
        n = (hi - lo) // BLK
        blocks[j].wait()
        gps = [gp_of(j, t) for t in range(n)]
        for o, p in enumerate(pairs):
            cs = slice((p - offset) * 128, (p - offset + 1) * 128)
            kb, vb = kv[here, cs], vv[here, cs]
            dk = dv = jnp.zeros((BLK, 128), f32)
            for t in range(n):
                i = slice(lo + t * BLK, lo + (t + 1) * BLK)
                b = slice(at + t * BLK, at + (t + 1) * BLK)
                q, g = qv[i, cs], gv[i, cs]
                dq = jnp.zeros((BLK, 128), f32)
                for h in range(2):
                    mine = (lane // HEAD_DIM) == h
                    only = lambda a: jnp.where(mine, a, jnp.zeros_like(a))
                    gh = only(g)
                    pb = pv[2 * (p - offset) + h, :, b]
                    dp = dot(vb, gh, 1, 1)
                    ds = pb.astype(f32) * (dp - dd_ref[2 * p + h : 2 * p + h + 1, i])
                    gps[t] = gps[t] - ds
                    sb = ds.astype(bf16)
                    dv = dv + dot(pb, gh)
                    dk = dk + dot(sb, only(q))
                    dq = dq + dot(sb, only(kb), 0, 0)
                if (p, i.start) in seen:
                    dqa[i, cs] += dq
                else:
                    seen.add((p, i.start))
                    dqa[i, cs] = dq
            os = slice(o * 128, (o + 1) * 128)
            dpv[here, width + o * 128 : width + (o + 1) * 128] = dk.astype(bf16)
            dpv[here, 2 * width + o * 128 : 2 * width + (o + 1) * 128] = dv.astype(bf16)
            dpv[here, os] = (dqa[here, cs] * scale).astype(bf16)
        done(j, gps)


def halves_out(acc, keep, gone):
    _, core, _ = ids()
    half = acc.shape[1] // 2
    left, right = acc[:, :half], acc[:, half:]
    keep[...] = jnp.where(core == 0, left, right).astype(bf16)
    gone[...] = jnp.where(core == 0, right, left).astype(bf16)


def back_a_kernel(
    q_ref, k_ref, v_ref, g_ref, p_ref, n_ref, dd_ref,
    dp_ref, gp_ref, keep_ref, send_ref,
    qv, kv, vv, gv, pv, nv, dqa, dpv, gpv, sems,
):
    mv = Mover(sems)
    L, HL = q_ref.shape
    wins, _ = back_windows(L)
    pairs = range(HL // 128 - 1)
    heads = 2 * len(pairs)
    part = slice(0, len(pairs) * 128)
    gets = [mv.start(v_ref.at[:, part], vv), mv.start(g_ref.at[:, part], gv)]
    blocks = []
    for j, (lo, hi, at) in enumerate(wins):
        w = slice(at, at + hi - lo)
        blocks.append(mv.start(p_ref.at[0:heads, :, w], pv.at[:, :, w]))
        if j == 0:
            gets += [mv.start(q_ref.at[:, part], qv), mv.start(k_ref.at[:, part], kv)]
    later = mv.start(n_ref, nv)
    for op in gets:
        op.wait()

    def done(j, gps):
        lo, hi, at = wins[j]
        for t, gp in enumerate(gps):
            gpv[:, at + t * BLK : at + (t + 1) * BLK] = gp
        mv.put(gpv.at[:, at : at + hi - lo], gp_ref.at[:, at : at + hi - lo])

    zero = jnp.zeros((BLK, BLK), f32)
    head_grads(pairs, 0, wins, blocks, dd_ref, qv, kv, vv, gv, pv, dqa, dpv, lambda j, t: zero, done)
    mv.put(dpv, dp_ref)
    later.wait()
    halves_out(dot(nv[...], dpv[...], 0, 0), keep_ref, send_ref)
    mv.finish()


def back_a_call(q, k, v, g, p, n, dd):
    L, HL = q.shape
    D = n.shape[1]
    heads = HL // HEAD_DIM - 2
    _, wide = back_windows(L)
    width = heads * HEAD_DIM
    part = (L, width)
    return call(
        back_a_kernel,
        "attend_back_a",
        [ANY] * 6 + [None],
        [
            (sds((L, 3 * width), bf16), False),
            (sds((BLK, wide), f32), False),
            (sds((D, 3 * width // 2), bf16), True),
            (sds((D, 3 * width // 2), bf16), True),
        ],
        [(part, bf16)] * 4
        + [((heads, BLK, wide), bf16), ((L, D), bf16), (part, f32), ((L, 3 * width), bf16), ((BLK, wide), f32)],
        8 + 2 * (L // BLK),
        BLK * wide * 128 * 2 * 4 * heads + 2 * L * D * 3 * width,
        18e6,
        q, k, v, g, p, n, dd,
    )


def back_b_kernel(
    q_ref, k_ref, v_ref, g_ref, p_ref, gp_ref, r_ref, dpa_ref, x_ref, w_ref, pq_ref, pk_ref, dd_ref, wpa_ref, wpb_ref,
    gn_ref, dp_ref, sums_ref,
    qv, kv, vv, gv, pv, gpv, rv, dpav, xv, wv, dqa, pqa, dpv, gnv, sems,
):
    mv = Mover(sems)
    L, HL = q_ref.shape
    D = x_ref.shape[1]
    wins, _ = back_windows(L)
    pair = HL // 128 - 1
    part = slice(pair * 128, HL)
    gets = [mv.start(v_ref.at[:, part], vv), mv.start(g_ref.at[:, part], gv)]
    blocks = []
    for j, (lo, hi, at) in enumerate(wins):
        w = slice(at, at + hi - lo)
        blocks.append(mv.start(p_ref.at[2 * pair : 2 * pair + 2, :, w], pv.at[:, :, w]))
        if j == 0:
            gets += [mv.start(q_ref.at[:, part], qv), mv.start(k_ref.at[:, part], kv), mv.start(gp_ref, gpv)]
    later = [mv.start(r_ref, rv), mv.start(dpa_ref, dpav), mv.start(w_ref, wv), mv.start(x_ref, xv)]
    rr = lax.broadcasted_iota(jnp.int32, (BLK, BLK), 0)
    cc = lax.broadcasted_iota(jnp.int32, (BLK, BLK), 1)
    later_of = jnp.where(rr > cc, 1.0, 0.0).astype(bf16)
    wp = pick_weights(wpa_ref[...], wpb_ref[...])
    scale = HEAD_DIM**-0.5
    sums = [jnp.zeros((1, D), f32)] * 2
    seen = set()
    for op in gets:
        op.wait()

    def done(j, gps):
        lo, hi, at = wins[j]
        here = slice(j * BLK, (j + 1) * BLK)
        if j == 0:
            for op in later:
                op.wait()
        kb = pk_ref[here, :]
        carry = jnp.zeros((BLK, 1), f32)
        dk0 = jnp.zeros((BLK, 128), f32)
        for t in reversed(range((hi - lo) // BLK)):
            i = slice(lo + t * BLK, lo + (t + 1) * BLK)
            b = slice(at + t * BLK, at + (t + 1) * BLK)
            gs = ((carry + dot(gps[t].astype(bf16), later_of)) * rv[:, b].astype(f32)).astype(bf16)
            carry = carry + jnp.sum(gps[t], axis=1, keepdims=True)
            dk0 = dk0 + dot(gs, pq_ref[i, :])
            dq = dot(gs, kb, 0, 0)
            if i.start in seen:
                pqa[i, :] += dq
            else:
                seen.add(i.start)
                pqa[i, :] = dq
        dpv[here, 384:512] = (pltpu.roll(dk0, HEAD_DIM, 1) + pqa[here, :] * scale).astype(bf16)
        gn = dot(dpv[here, 384:], wp, 1, 1)
        n = pair * 128
        for c in range(3):
            gn = gn + dot(dpav[here, c * n : (c + 1) * n], wv[c, :, 0:n], 1, 1)
            gn = gn + dot(dpv[here, c * 128 : (c + 1) * 128], wv[c, :, n:], 1, 1)
        gnv[here, :] = gn.astype(bf16)
        mv.put(gnv.at[here, :], gn_ref.at[here, :])
        mv.put(dpv.at[here, :], dp_ref.at[here, :])
        xhat, _ = standard(xv[here, :].astype(f32))
        sums[0] = sums[0] + jnp.sum(gn * xhat, axis=0, keepdims=True)
        sums[1] = sums[1] + jnp.sum(gn, axis=0, keepdims=True)

    gp_of = lambda j, t: gpv[:, wins[j][2] + t * BLK : wins[j][2] + (t + 1) * BLK]
    head_grads([pair], pair, wins, blocks, dd_ref, qv, kv, vv, gv, pv, dqa, dpv, gp_of, done)
    sums_ref[...] = jnp.concatenate(sums + [jnp.zeros((6, D), f32)], axis=0)
    mv.finish()


def back_b_call(q, k, v, g, p, gp, r, dpa, x, w3, pq, pk, dd, wpa, wpb):
    L, HL = q.shape
    D = x.shape[1]
    _, wide = back_windows(L)
    one = (L, 128)
    return call(
        back_b_kernel,
        "attend_back_b",
        [ANY] * 10 + [None] * 5,
        [(sds((L, D), bf16), False), (sds((L, 512), bf16), False), (sds((8, D), f32), True)],
        [(one, bf16)] * 4
        + [
            ((2, BLK, wide), bf16),
            ((BLK, wide), f32),
            ((BLK, wide), bf16),
            (dpa.shape, bf16),
            ((L, D), bf16),
            ((3, D, HL), bf16),
            (one, f32),
            (one, f32),
            ((L, 512), bf16),
            ((L, D), bf16),
        ],
        9 + 3 * (L // BLK),
        BLK * wide * 128 * 2 * 4 * 3 + 2 * L * D * (3 * HL + 128),
        20e6,
        q, k, v, g, p, gp, r, dpa, x, w3, pq, pk, dd, wpa, wpb,
    )


def dw_kernel(n_ref, dp_ref, keep_ref, send_ref, sems):
    halves_out(dot(n_ref[...], dp_ref[...], 0, 0), keep_ref, send_ref)


def dw_call(n, dp):
    L, D = n.shape
    N = dp.shape[1]
    half = sds((D, N // 2), bf16)
    return call(
        dw_kernel, "dw_last", [None] * 2, [(half, True), (half, True)], [], 1, 2 * L * D * N, 4e6, n, dp
    )


def last_kernel(x_ref, ga_ref, gb_ref, gm_ref, g_ref, o_ref):
    xhat, rstd = standard(x_ref[...].astype(f32))
    gn = ga_ref[...].astype(f32) + gb_ref[...].astype(f32)
    o_ref[...] = gm_ref[...].astype(f32) + norm_back(xhat, rstd, row_of(g_ref), gn)


def last_call(x, ga, gb, gm, gain):
    L, D = x.shape
    row = spec((L // 2, D), lambda i: (i, 0))
    return pl.pallas_call(
        last_kernel,
        grid=(2,),
        in_specs=[row] * 4 + [spec((D,))],
        out_specs=row,
        out_shape=sds((L, D), f32),
        compiler_params=params(),
        cost_estimate=cost(1e3, 1e3),
        name="norm_back",
    )(x, ga, gb, gm, gain)


def links(dp, tensor):
    def swap(bit):
        return [(p * tensor + t, (p ^ bit) * tensor + t) for p in range(dp) for t in range(tensor)]

    across = [(p * tensor + t, p * tensor + (1 - t)) for p in range(dp) for t in range(tensor)]
    head_zero = [(p * tensor, p * tensor + 1) for p in range(dp)]
    return swap, across, head_zero


def after(value, *others):
    return lax.optimization_barrier((value, *others))[0]


def after3(a, b, c, *others):
    return lax.optimization_barrier((a, b, c, *others))[:3]


def shards(
    dp,
    tensor,
    tokens,
    lengths,
    cotangent,
    norm_gain_one,
    norm_shift_one,
    w_qkv,
    w_out,
    b_out,
    norm_gain_two,
    norm_shift_two,
    w_up,
    b_up,
    w_down,
    b_down,
):
    _, L, D = tokens.shape
    HL = w_out.shape[0]
    F = w_up.shape[1]
    swap, across, head_zero = links(dp, tensor)
    t = lax.axis_index("tensor")
    d = lax.axis_index("dp")
    core = d % 2
    groups = dp // 2
    rows = D // groups
    send = lambda a, perm: lax.ppermute(a, AXES, perm)

    def sum_dp(v, bit, end):
        while bit < end:
            v = v + send(v, swap(bit))
            bit *= 2
        return v

    def fold(pieces, bit):
        totals = [(keep.astype(f32) + got.astype(f32)).astype(bf16) for keep, got in pieces]
        totals = [a.reshape(groups // (2 * bit), 2, rows, a.shape[-1]) for a in totals]
        mine = (d // (2 * bit)) % 2
        pick = lambda which: jnp.concatenate([lax.dynamic_index_in_dim(a, which, 1, False) for a in totals], axis=-1)
        return pick(mine), pick(1 - mine)

    def finish(keep, got):
        total = (keep.astype(f32) + got.astype(f32)).reshape(2, rows // 2, keep.shape[-1])
        mine = lax.dynamic_index_in_dim(total, core, 0, False)
        got = send(lax.dynamic_index_in_dim(total, 1 - core, 0, False), swap(1))
        return jnp.where(core == 0, mine, got), jnp.where(core == 0, got, mine)

    x = tokens.reshape(L, D)
    cot = cotangent.reshape(L, D)
    w3 = jnp.transpose(w_qkv, (1, 0, 2))

    wp_own = pick_call(w3)
    one, two = pack_call(w_down, w_up, w_out, after(b_up, wp_own))
    wp_got = send(wp_own, head_zero)
    q, k, v, n1 = start_call(after(x, one), w3, norm_gain_one, norm_shift_one)
    one_x, two_x = send(one, across), send(two, across)
    ctx, inv, pq, pk, prob, reach = attend_call(lengths, n1, wp_own, wp_got, q, k, v)
    ctx_b = send(ctx, across)
    one_y = send(after(one_x, ctx), swap(2))
    ga, cot_sum = cot_call(after(cot, ctx), w_down)
    two_y = send(after(two_x, ga, one_y), swap(2))
    one_x, one_y = lax.optimization_barrier((one_x, one_y, ga))[:2]
    ones = [one_x, one_y, send(one_x, swap(1)), send(one_y, swap(1))]
    mid, n2, gn2, mo, keep_a, gone_a, dbu = own_call(
        x, ctx, after(ctx_b, ga), w_out, ones, w_up, w_down, ga, cot, b_out, norm_gain_two, norm_shift_two, b_up
    )
    got_a = send(after(gone_a, two_y), swap(1))
    two_x, two_y = lax.optimization_barrier((two_x, two_y, mid))[:2]
    twos = [two_x, two_y, send(two_x, swap(1)), send(two_y, swap(1))]
    keep_a, gone_a = fold([(keep_a, got_a)], 1)
    got_a = send(gone_a, swap(2))
    out, gm, gc, dd, sums2, keep_o, gone_o = other_call(
        n2, after(cot, gone_a), one_x, twos, gn2, mo, mid, w_out, ctx, norm_gain_two, b_down, inv
    )
    got_o = send(gone_o, swap(1))
    dp_a, gp, keep_c, gone_c = back_a_call(q, k, v, gc, prob, n1, dd)
    got_c = send(gone_c, swap(1))
    keep_a, gone_a = fold([(keep_a, after(got_a, dp_a))], 2)
    got_a = send(gone_a, swap(4))
    gn1, dp_b, sums1 = back_b_call(
        q, k, v, gc, prob, after(gp, gone_a), reach, dp_a, x, w3, pq, pk, dd, wp_own, wp_got
    )
    gn1_got = send(gn1, across)
    keep_d, gone_d = dw_call(n1, dp_b)
    got_d = send(gone_d, swap(1))
    got_c = after(got_c, dp_b)
    keep_c, gone_c = fold([(keep_c, got_c), (keep_o, got_o), (keep_d, got_d)], 1)
    got_c = send(gone_c, swap(2))
    keep_c, gone_c = fold([(keep_c, got_c)], 2)
    got_c = send(gone_c, swap(4))

    small = jnp.concatenate(
        [sums1[:2].reshape(-1), sums2[:3].reshape(-1), cot_sum.reshape(-1), dbu.reshape(-1)]
    ).reshape(-1, 128)
    small = sum_dp(after(small, gone_c), 1, 4)
    keep_c, gone_c = fold([(keep_c, got_c)], 4)
    got_c = send(gone_c, swap(8))
    small = sum_dp(after(small, gn1_got, gone_c), 4, dp)
    late = small[: 2 * D // 128]
    late = (late + send(late, across)).reshape(2, D)
    early = small[2 * D // 128 :].reshape(-1)

    ends = []

    def rest(keep, got, bit):
        while 2 * bit < dp:
            keep, gone = fold([(keep, got)], bit)
            bit *= 2
            got = send(gone, swap(bit))
            ends.append(got)
        return finish(keep, got)

    keep_a, gone_a = fold([(keep_a, got_a)], 4)
    left_a, right_a = rest(keep_a, send(gone_a, swap(8)), 8)
    left_c, right_c = rest(keep_c, got_c, 8)
    up_share, down_share = left_a, right_a
    n = 3 * (HL - 128) // 2
    m = n + HL // 2
    out_share = jnp.concatenate([left_c[:, n:m], right_c[:, n:m]], axis=1)
    c = jnp.concatenate([left_c[:, :n], right_c[:, :n]], axis=1).reshape(-1, 3, HL - 128)
    e = jnp.concatenate([left_c[:, m:], right_c[:, m:]], axis=1)
    extra = e[:, 384:]
    extra = extra + send(extra, across)
    extra = jnp.where(t == 0, extra, jnp.zeros_like(extra))
    zeros = jnp.zeros((extra.shape[0], HL - HEAD_DIM), f32)
    extra = jnp.concatenate(
        [extra[:, :HEAD_DIM], zeros, extra[:, HEAD_DIM:], zeros, jnp.zeros((extra.shape[0], HL), f32)], axis=1
    )
    qkv_share = jnp.concatenate([c, e[:, :384].reshape(-1, 3, 128)], axis=2) + extra.reshape(-1, 3, HL)
    grad_tokens = last_call(x, gn1, gn1_got, gm, norm_gain_one)
    return (
        out.reshape(1, L, D),
        grad_tokens.reshape(1, L, D),
        late[0],
        late[1],
        qkv_share,
        out_share.T,
        early[2 * D : 3 * D],
        early[:D],
        early[D : 2 * D],
        up_share,
        early[4 * D :],
        down_share.T,
        early[3 * D : 4 * D],
    )


def solution(mesh):
    in_specs = (
        P("dp", None, None),
        P("dp", None),
        P("dp", None, None),
        P(),
        P(),
        P(None, None, "tensor"),
        P("tensor", None),
        P(),
        P(),
        P(),
        P(None, "tensor"),
        P("tensor"),
        P("tensor", None),
        P(),
    )
    out_specs = (
        P("dp", None, None),
        P("dp", None, None),
        P(),
        P(),
        P("dp", None, "tensor"),
        P("tensor", "dp"),
        P(),
        P(),
        P(),
        P("dp", "tensor"),
        P("tensor"),
        P("tensor", "dp"),
        P(),
    )
    body = functools.partial(shards, mesh.shape["dp"], mesh.shape["tensor"])
    return jax.shard_map(body, mesh=mesh, in_specs=in_specs, out_specs=out_specs, check_vma=False)
```

```python
import functools

import jax
import jax.numpy as jnp
from jax import lax
from jax.experimental import pallas as pl
from jax.experimental.pallas import tpu as pltpu
from jax.sharding import PartitionSpec as P

HEAD_DIM = 64
LONGEST = 512
BLK = 256
EPS = 1e-05
FAR = 1e30
AXES = ("dp", "tensor")
f32 = jnp.float32
bf16 = jnp.bfloat16


def dot(a, b, ca=1, cb=0, precision=None):
    return lax.dot_general(
        a, b, (((ca,), (cb,)), ((), ())), preferred_element_type=f32, precision=precision
    )


def spec(shape, index=None):
    if index is None:
        zeros = (0,) * len(shape)
        return pl.BlockSpec(shape, lambda *_: zeros)
    return pl.BlockSpec(shape, index)


def params(mib=60):
    return pltpu.CompilerParams(vmem_limit_bytes=60 * 1024 * 1024)


ANY = pl.BlockSpec(memory_space=pl.ANY)
SMEM = pl.BlockSpec(memory_space=pltpu.SMEM)


def sds(shape, dtype):
    return jax.ShapeDtypeStruct(shape, dtype)


def cost(flops, nbytes, trans=0):
    return pl.CostEstimate(flops=int(flops), bytes_accessed=int(nbytes), transcendentals=int(trans))


def starts_at(pos, lengths_ref, docs):
    start = jnp.zeros_like(pos)
    end = lengths_ref[0, 0]
    for d in range(1, docs):
        start = jnp.where(pos >= end, end, start)
        end = end + lengths_ref[0, d]
    return start


def standard(x):
    mean = jnp.mean(x, axis=-1, keepdims=True)
    c = x - mean
    var = jnp.mean(c * c, axis=-1, keepdims=True)
    rstd = lax.rsqrt(var + EPS)
    return c * rstd, rstd


def norm_back(xhat, rstd, gain, grad):
    gg = grad * gain
    m1 = jnp.mean(gg, axis=-1, keepdims=True)
    m2 = jnp.mean(gg * xhat, axis=-1, keepdims=True)
    return rstd * (gg - m1 - xhat * m2)


def ids():
    d = lax.axis_index("dp")
    return lax.axis_index("tensor"), lax.rem(d, 2), lax.rem(d // 2, 2)


def quarters():
    _, core, y = ids()
    return [2 * y + core, 2 * (1 - y) + core, 2 * y + 1 - core, 2 * (1 - y) + 1 - core]


def pick_weights(own, got):
    t, _, _ = ids()
    return jnp.where(t == 0, own.astype(f32), got.astype(f32)).astype(bf16)


def eighths():
    d = lax.axis_index("dp")
    core, y, z = lax.rem(d, 2), lax.rem(d // 2, 2), lax.rem(d // 4, 2)
    at = lambda z, y, c: 4 * z + 2 * y + c
    return [at(b, a, c) for c in (core, 1 - core) for b, a in ((z, y), (z, 1 - y), (1 - z, y), (1 - z, 1 - y))]


class Mover:
    def __init__(self, sems):
        self.sems, self.count, self.open = sems, 0, []

    def start(self, src, dst):
        op = pltpu.make_async_copy(src, dst, self.sems.at[self.count])
        self.count += 1
        op.start()
        return op

    def put(self, src, dst):
        self.open.append(self.start(src, dst))

    def finish(self):
        for op in self.open:
            op.wait()


def row_of(ref):
    return ref[...].reshape(1, -1)


LIGHT = ("mlp_own", "dw_last", "norm_qkv", "cot_down")


def call(kernel, name, ins, outs, scratch, sems, flops, nbytes, *args):
    full = lambda a: pl.BlockSpec(memory_space=pltpu.VMEM)
    return pl.pallas_call(
        kernel,
        in_specs=[full(a) if s is None else s for s, a in zip(ins, args, strict=True)],
        out_specs=[full(o) if inside else ANY for o, inside in outs],
        out_shape=[o for o, _ in outs],
        scratch_shapes=[pltpu.VMEM(s, t) for s, t in scratch] + [pltpu.SemaphoreType.DMA((sems,))],
        compiler_params=params(),
        cost_estimate=cost(1e3, 1e3) if name in LIGHT else cost(flops, nbytes),
        name=name,
    )(*args)


def pick_kernel(w_ref, wp_ref, qv, kv, sems):
    mv = Mover(sems)
    a = mv.start(w_ref.at[0, :, 0:128], qv)
    b = mv.start(w_ref.at[1, :, 0:128], kv)
    a.wait()
    b.wait()
    lane = lax.broadcasted_iota(jnp.int32, (1, 128), 1)
    k = pltpu.roll(kv[...].astype(f32), HEAD_DIM, 1)
    wp_ref[...] = jnp.where(lane < HEAD_DIM, qv[...].astype(f32), k).astype(bf16)


def pick_call(w3):
    D = w3.shape[1]
    return call(
        pick_kernel, "pick", [ANY], [(sds((D, 128), bf16), True)], [((D, 128), bf16)] * 2, 2, 1e3, 4e5, w3
    )[0]


def pack_kernel(wd_ref, wu_ref, wo_ref, bu_ref, one_ref, two_ref, onev, twov, sems):
    mv = Mover(sems)
    _, core, y = ids()
    s = 2 * y + core
    D = wo_ref.shape[1]
    s8 = eighths()[0]
    ro, ru, rd = wo_ref.shape[0] // 4, wu_ref.shape[0] // 8, wd_ref.shape[0] // 8
    halves = wu_ref.shape[1] // D
    from_row = lambda n: pl.ds(pl.multiple_of(s8 * n, 16), n)
    get_one = mv.start(wo_ref.at[pl.ds(pl.multiple_of(s * ro, 16), ro)], onev.at[0:ro])
    packs = []
    for h in range(halves):
        packs.append(mv.start(wu_ref.at[from_row(ru), h * D : (h + 1) * D], twov.at[h * ru : (h + 1) * ru]))
    packs.append(mv.start(wd_ref.at[from_row(rd)], twov.at[halves * ru : halves * ru + rd]))
    rest = row_of(bu_ref)
    pieces = []
    for _ in range(3):
        piece = rest.astype(bf16)
        rest = rest - piece.astype(f32)
        pieces.append(piece.astype(f32))
    flat = [p[:, h * D : (h + 1) * D] for p in pieces for h in range(halves)]
    onev[ro : ro + 16, :] = jnp.concatenate(flat + [jnp.zeros((16 - len(flat), D), f32)], axis=0).astype(bf16)
    get_one.wait()
    mv.put(onev, one_ref)
    for op in packs:
        op.wait()
    mv.put(twov, two_ref)
    mv.finish()


def pack_call(w_down, w_up, w_out, b_up):
    F, D = w_down.shape
    one = w_out.shape[0] // 4 + 16
    two = (w_up.shape[0] * (F // D) + F) // 8
    return call(
        pack_kernel,
        "pack",
        [ANY] * 3 + [None],
        [(sds((one, D), bf16), False), (sds((two, D), bf16), False)],
        [((one, D), bf16), ((two, D), bf16)],
        8,
        1e3,
        3e6,
        w_down, w_up, w_out, b_up,
    )


def start_kernel(x_ref, w_ref, g_ref, b_ref, q_ref, k_ref, v_ref, n_ref, xv, wv, nv, qv, kv, vv, sems):
    mv = Mover(sems)
    L, D = x_ref.shape
    half = L // 2
    gets = [mv.start(x_ref.at[0:half], xv.at[0:half]), mv.start(w_ref, wv), mv.start(x_ref.at[half:L], xv.at[half:L])]
    gain, shift = row_of(g_ref), row_of(b_ref)
    gets[0].wait()
    for m in range(L // BLK):
        r = slice(m * BLK, (m + 1) * BLK)
        if m * BLK == half:
            gets[2].wait()
        xhat, _ = standard(xv[r, :].astype(f32))
        n = (xhat * gain + shift).astype(bf16)
        nv[r, :] = n
        if m == 0:
            gets[1].wait()
        qv[r, :] = (dot(n, wv[0]).astype(bf16).astype(f32) * HEAD_DIM**-0.5).astype(bf16)
        kv[r, :] = dot(n, wv[1]).astype(bf16)
        vv[r, :] = dot(n, wv[2]).astype(bf16)
        if (m + 1) * BLK % half == 0:
            done = slice((m + 1) * BLK - half, (m + 1) * BLK)
            for src, dst in ((nv, n_ref), (qv, q_ref), (kv, k_ref), (vv, v_ref)):
                mv.put(src.at[done, :], dst.at[done, :])
    mv.finish()


def start_call(x, w3, gain, shift):
    L, D = x.shape
    HL = w3.shape[2]
    half = (L, HL)
    return call(
        start_kernel,
        "norm_qkv",
        [ANY] * 2 + [None] * 2,
        [(sds(half, bf16), False)] * 3 + [(sds((L, D), bf16), False)],
        [((L, D), bf16), ((3, D, HL), bf16), ((L, D), bf16)] + [(half, bf16)] * 3,
        11,
        2 * L * D * 3 * HL,
        9e6,
        x, w3, gain, shift,
    )


def cot_kernel(c_ref, wd_ref, ga_ref, cs_ref, cv, wdv, gav, sems):
    mv = Mover(sems)
    L, D = c_ref.shape
    gets = [mv.start(c_ref, cv), mv.start(wd_ref, wdv)]
    for op in gets:
        op.wait()
    cs = jnp.zeros((1, D), f32)
    for m in range(L // BLK):
        r = slice(m * BLK, (m + 1) * BLK)
        c = cv[r, :]
        cs = cs + jnp.sum(c.astype(f32), axis=0, keepdims=True)
        gav[r, :] = dot(c, wdv[...], 1, 1).astype(bf16)
        mv.put(gav.at[r, :], ga_ref.at[r, :])
    cs_ref[...] = cs
    mv.finish()


def cot_call(c, w_down):
    L, D = c.shape
    F = w_down.shape[0]
    return call(
        cot_kernel,
        "cot_down",
        [ANY] * 2,
        [(sds((L, F), bf16), False), (sds((1, D), f32), True)],
        [((L, D), bf16), ((F, D), bf16), ((L, F), bf16)],
        2 + L // BLK,
        2 * L * D * F,
        7e6,
        c, w_down,
    )


def windows(L):
    reach = LONGEST // BLK
    return [range(max(0, i - reach), i + 1) for i in range(L // BLK)]


def back_windows(L):
    reach = LONGEST // BLK
    found, at = [], 0
    for j in range(L // BLK):
        lo, hi = j * BLK, min(L, (j + reach + 1) * BLK)
        found.append((lo, hi, at))
        at += hi - lo
    return found, at


def attend_kernel(
    docs, strength, len_ref, n_ref, wpa_ref, wpb_ref, q_ref, k_ref, v_ref,
    ctx_ref, inv_ref, pq_ref, pk_ref, p_ref, r_ref,
    nv, qv, kv, vv, vt, cv, pv, rv, bias_ref, sems,
):
    mv = Mover(sems)
    get_n = mv.start(n_ref, nv)
    get_v = mv.start(v_ref, vv)
    get_q = mv.start(q_ref, qv)
    get_k = mv.start(k_ref, kv)
    L, HL = q_ref.shape
    wins, _ = back_windows(L)
    lane = lax.broadcasted_iota(jnp.int32, (1, 128), 1)
    left = lane < HEAD_DIM
    w = pick_weights(wpa_ref[...], wpb_ref[...])
    get_n.wait()
    both = dot(nv[...], w)
    pq_ref[...] = jnp.where(left, both.astype(bf16).astype(f32) * HEAD_DIM**-0.5, 0.0).astype(bf16)
    pk_ref[...] = jnp.where(left, pltpu.roll(both, HEAD_DIM, 1), 0.0).astype(bf16)
    get_v.wait()
    for m in range(L // BLK):
        vt[:, m * BLK : (m + 1) * BLK] = vv[m * BLK : (m + 1) * BLK, :].T
    rows = lax.broadcasted_iota(jnp.int32, (BLK, BLK), 0)
    cols = lax.broadcasted_iota(jnp.int32, (BLK, BLK), 1)
    above = jnp.where(rows < cols, 1.0, 0.0).astype(bf16)
    carry = [jnp.zeros((BLK, 1), f32)] * (L // BLK)
    get_q.wait()
    get_k.wait()
    for i, blocks in enumerate(windows(L)):
        mine = slice(i * BLK, (i + 1) * BLK)
        ipos = i * BLK + lax.broadcasted_iota(jnp.int32, (1, BLK), 1)
        istart = starts_at(ipos, len_ref, docs)
        places = {}
        for j in blocks:
            here = slice(j * BLK, (j + 1) * BLK)
            at = wins[j][2] + (i - j) * BLK
            places[j] = slice(at, at + BLK)
            s = dot(pk_ref[here, :], pq_ref[mine, :], 1, 1)
            jpos = j * BLK + lax.broadcasted_iota(jnp.int32, (BLK, 1), 0)
            inside = jpos >= istart
            fresh = jpos != starts_at(jpos, len_ref, docs)
            if j == i:
                allowed = inside & (jpos <= ipos)
                selectable = inside & (jpos < ipos) & fresh
            else:
                allowed, selectable = inside, inside & fresh
            r = jnp.where(selectable, jnp.maximum(s, 0.0), 0.0)
            rv[:, places[j]] = (r * (2.0 * strength)).astype(bf16)
            c = r * r
            pen = strength * (carry[j] + dot(c.astype(bf16), above))
            bias_ref[j - blocks[0]] = jnp.where(allowed, pen, FAR)
            if i + 1 < L // BLK and j in windows(L)[i + 1]:
                carry[j] = carry[j] + jnp.sum(c, axis=1, keepdims=True)
        invs, outs = [], []
        for h in range(HL // HEAD_DIM):
            cs = slice(h // 2 * 128, (h // 2 + 1) * 128)
            q = jnp.where((lane // HEAD_DIM) == h % 2, qv[mine, cs], jnp.zeros((BLK, 128), bf16))
            ss = [dot(kv[j * BLK : (j + 1) * BLK, cs], q, 1, 1) - bias_ref[j - blocks[0]] for j in blocks]
            top = functools.reduce(jnp.maximum, [jnp.max(s, axis=0, keepdims=True) for s in ss])
            total = jnp.zeros((1, BLK), f32)
            out = jnp.zeros((HEAD_DIM, BLK), f32)
            for j, s in zip(blocks, ss, strict=True):
                e = jnp.exp(s - top)
                total = total + jnp.sum(e, axis=0, keepdims=True)
                e = e.astype(bf16)
                pv[h, :, places[j]] = e
                out = out + dot(vt[h * HEAD_DIM : (h + 1) * HEAD_DIM, j * BLK : (j + 1) * BLK], e)
            inv = 1.0 / total
            invs.append(inv)
            outs.append(out * inv)
        inv_ref[:, mine] = jnp.concatenate(invs + [jnp.zeros((8 - len(invs), BLK), f32)], axis=0)
        for p in range(HL // 128):
            pair = jnp.concatenate(outs[2 * p : 2 * p + 2], axis=0)
            cv[mine, p * 128 : (p + 1) * 128] = pair.T.astype(bf16)
        mv.put(cv.at[mine, :], ctx_ref.at[mine, :])
        for j in blocks:
            mv.put(pv.at[:, :, places[j]], p_ref.at[:, :, places[j]])
    mv.put(rv, r_ref)
    mv.finish()


def attend_call(lengths, n, wpa, wpb, q, k, v):
    L, HL = q.shape
    D = n.shape[1]
    heads = HL // HEAD_DIM
    _, wide = back_windows(L)
    half = (L, HL)
    return call(
        functools.partial(attend_kernel, lengths.shape[1], 2.0 / L),
        "attend",
        [SMEM, ANY, None, None, ANY, ANY, ANY],
        [
            (sds(half, bf16), False),
            (sds((8, L), f32), True),
            (sds((L, 128), bf16), True),
            (sds((L, 128), bf16), True),
            (sds((heads, BLK, wide), bf16), False),
            (sds((BLK, wide), bf16), False),
        ],
        [((L, D), bf16)]
        + [(half, bf16)] * 3
        + [
            ((HL, L), bf16),
            (half, bf16),
            ((heads, BLK, wide), bf16),
            ((BLK, wide), bf16),
            ((LONGEST // BLK + 1, BLK, BLK), f32),
        ],
        5 + L // BLK + wide // BLK,
        1e12,
        14e6,
        lengths, n, wpa, wpb, q, k, v,
    )


C0 = 0.7978845608028654
C1 = 0.044715
CHUNK = 512


def gelu_pair(u):
    u2 = u * u
    t = jnp.tanh(u * (C0 + (C0 * C1) * u2))
    h = 0.5 + 0.5 * t
    a = u * h
    d = h + a * (1.0 - h) * (2.0 * C0 + (6.0 * C0 * C1) * u2)
    return a, d


def own_kernel(
    x_ref, ca_ref, cb_ref, wo_ref, p0_ref, p1_ref, p2_ref, p3_ref, wu_ref, wd_ref, ga_ref, c_ref,
    bo_ref, g_ref, b_ref, bu_ref,
    mid_ref, n_ref, gn_ref, mo_ref, keep_ref, send_ref, dbu_ref,
    xv, cav, cbv, wov, wbv, wuv, wdv, gav, cv, mv_, nv, gnv, mov, av, guv, keepv, sendv, sems,
):
    mv = Mover(sems)
    L, D = x_ref.shape
    F = wu_ref.shape[1]
    HL = ca_ref.shape[1]
    _, core, _ = ids()
    gets = [mv.start(ca_ref, cav), mv.start(wo_ref, wov), mv.start(cb_ref, cbv), mv.start(x_ref, xv)]
    ro, at = HL // 4, 0
    for part, slot in zip((p0_ref, p1_ref, p2_ref, p3_ref), quarters()):
        gets.append(mv.start(part.at[at : at + ro], wbv.at[pl.ds(pl.multiple_of(slot * ro, 16), ro)]))
    later = [mv.start(wu_ref, wuv), mv.start(ga_ref, gav), mv.start(wd_ref, wdv), mv.start(c_ref, cv)]
    bo, gain, shift, bu = row_of(bo_ref), row_of(g_ref), row_of(b_ref), row_of(bu_ref)
    for op in gets:
        op.wait()
    for m in range(L // BLK):
        r = slice(m * BLK, (m + 1) * BLK)
        att = dot(cav[r, :], wov[...]) + dot(cbv[r, :], wbv[...])
        mid = xv[r, :].astype(f32) + (att + bo)
        mv_[r, :] = mid
        xhat, _ = standard(mid)
        nv[r, :] = (xhat * gain + shift).astype(bf16)
    mv.put(mv_, mid_ref)
    mv.put(nv, n_ref)
    for op in later:
        op.wait()
    for j in range(F // CHUNK):
        at = slice(j * CHUNK, (j + 1) * CHUNK)
        db = jnp.zeros((1, CHUNK), f32)
        for m in range(L // BLK):
            r = slice(m * BLK, (m + 1) * BLK)
            a, d = gelu_pair(dot(nv[r, :], wuv[:, at]) + bu[:, at])
            a = a.astype(bf16)
            gu = d * gav[r, at].astype(f32)
            db = db + jnp.sum(gu, axis=0, keepdims=True)
            gu = gu.astype(bf16)
            av[r, :] = a
            guv[r, :] = gu
            mo = dot(a, wdv[at, :])
            gn = dot(gu, wuv[:, at], 1, 1)
            if j == 0:
                mov[r, :] = mo
                gnv[r, :] = gn
            else:
                mov[r, :] += mo
                gnv[r, :] += gn
        dbu_ref[:, at] = db
        dwu = dot(nv[...], guv[...], 0, 0)
        dwd = dot(cv[...], av[...], 0, 0)
        keepv[:, at] = jnp.where(core == 0, dwu, dwd).astype(bf16)
        sendv[:, at] = jnp.where(core == 0, dwd, dwu).astype(bf16)
        mv.put(sendv.at[:, at], send_ref.at[:, at])
        mv.put(keepv.at[:, at], keep_ref.at[:, at])
        if j == F // CHUNK - 1:
            mv.put(gnv, gn_ref)
            mv.put(mov, mo_ref)
    mv.finish()


def own_call(x, ca, cb, w_out, parts, w_up, w_down, ga, c, b_out, gain, shift, b_up):
    L, D = x.shape
    HL = ca.shape[1]
    F = w_up.shape[1]
    return call(
        own_kernel,
        "mlp_own",
        [ANY] * 12 + [None] * 4,
        [
            (sds((L, D), f32), False),
            (sds((L, D), bf16), False),
            (sds((L, D), f32), False),
            (sds((L, D), f32), False),
            (sds((D, F), bf16), False),
            (sds((D, F), bf16), False),
            (sds((1, F), f32), True),
        ],
        [
            ((L, D), bf16),
            ((L, HL), bf16),
            ((L, HL), bf16),
            ((HL, D), bf16),
            ((HL, D), bf16),
            ((D, F), bf16),
            ((F, D), bf16),
            ((L, F), bf16),
            ((L, D), bf16),
            ((L, D), f32),
            ((L, D), bf16),
            ((L, D), f32),
            ((L, D), f32),
            ((L, CHUNK), bf16),
            ((L, CHUNK), bf16),
            ((D, F), bf16),
            ((D, F), bf16),
        ],
        16 + 2 * (F // CHUNK),
        2 * L * D * F * 5 + 4 * L * D * HL,
        36e6,
        x, ca, cb, w_out, *parts, w_up, w_down, ga, c, b_out, gain, shift, b_up,
    )


def other_kernel(
    n_ref, c_ref, a0_ref, d0_ref, d1_ref, d2_ref, d3_ref, d4_ref, d5_ref, d6_ref, d7_ref, gn_ref, mo_ref, mid_ref, wo_ref, ctx_ref,
    g_ref, bd_ref, inv_ref,
    out_ref, gm_ref, gc_ref, dd_ref, sums_ref, keep_ref, send_ref,
    nv, cv, wuv, wdv, bv, gnv, mov, midv, wov, ctxv, gna, moa, outv, gmv, gcv, sems,
):
    mv = Mover(sems)
    L, D = n_ref.shape
    F = wdv.shape[0]
    HL = ctx_ref.shape[1]
    halves = F // D
    gets = [mv.start(n_ref, nv)]
    parts = list(zip((d0_ref, d1_ref, d2_ref, d3_ref, d4_ref, d5_ref, d6_ref, d7_ref), eighths()))
    ru, rd = D // 8, F // 8
    for part, slot in parts:
        for h in range(halves):
            dst = wuv.at[pl.ds(pl.multiple_of(slot * ru, 16), ru), h * D : (h + 1) * D]
            gets.append(mv.start(part.at[h * ru : (h + 1) * ru], dst))
    n = a0_ref.shape[0]
    gets.append(mv.start(a0_ref.at[n - 16 : n], bv))
    downs = [mv.start(c_ref, cv)]
    for part, slot in parts:
        dst = wdv.at[pl.ds(pl.multiple_of(slot * rd, 16), rd)]
        downs.append(mv.start(part.at[halves * ru : halves * ru + rd], dst))
    _, core, _ = ids()
    later = [
        mv.start(src, dst)
        for src, dst in ((gn_ref, gnv), (mo_ref, mov), (mid_ref, midv), (wo_ref, wov), (ctx_ref, ctxv))
    ]
    gain, bd = row_of(g_ref), row_of(bd_ref)
    for op in gets:
        op.wait()
    b = bv[...].astype(f32)
    bu = [b[h : h + 1] + b[halves + h : halves + h + 1] + b[2 * halves + h : 2 * halves + h + 1] for h in range(halves)]
    bu = jnp.concatenate(bu, axis=1)
    for j in range(F // CHUNK):
        at = slice(j * CHUNK, (j + 1) * CHUNK)
        for m in range(L // BLK):
            r = slice(m * BLK, (m + 1) * BLK)
            a, d = gelu_pair(dot(nv[r, :], wuv[:, at]) + bu[:, at])
            if j == 0 and m == 0:
                for op in downs:
                    op.wait()
            gu = (d * dot(cv[r, :], wdv[at, :], 1, 1)).astype(bf16)
            mo = dot(a.astype(bf16), wdv[at, :])
            gn = dot(gu, wuv[:, at], 1, 1)
            if j == 0:
                moa[r, :] = mo
                gna[r, :] = gn
            else:
                moa[r, :] += mo
                gna[r, :] += gn
    for op in later:
        op.wait()
    heads = lax.broadcasted_iota(jnp.int32, (8, HL), 0)
    lane = lax.broadcasted_iota(jnp.int32, (8, HL), 1)
    pick = jnp.where(lane // HEAD_DIM == heads, 1.0, 0.0).astype(bf16)
    s0 = s1 = s2 = jnp.zeros((1, D), f32)
    for m in range(L // BLK):
        r = slice(m * BLK, (m + 1) * BLK)
        mid = midv[r, :]
        outv[r, :] = (mid + (mov[r, :] + moa[r, :]) + bd).astype(bf16)
        gn = gnv[r, :] + gna[r, :]
        xhat, rstd = standard(mid)
        gm = cv[r, :].astype(f32) + norm_back(xhat, rstd, gain, gn)
        s0 = s0 + jnp.sum(gn * xhat, axis=0, keepdims=True)
        s1 = s1 + jnp.sum(gn, axis=0, keepdims=True)
        s2 = s2 + jnp.sum(gm, axis=0, keepdims=True)
        gb = gm.astype(bf16)
        gmv[r, :] = gb
        inv = inv_ref[:, r]
        high = inv.astype(bf16)
        low = (inv - high.astype(f32)).astype(bf16)
        gc = (dot(gb, wov[...], 1, 1) * (dot(high, pick, 0, 0) + dot(low, pick, 0, 0))).astype(bf16)
        gcv[r, :] = gc
        prod = gc.astype(f32) * ctxv[r, :].astype(f32)
        high = prod.astype(bf16)
        low = (prod - high.astype(f32)).astype(bf16)
        dd_ref[:, r] = dot(pick, high, 1, 1) + dot(pick, low, 1, 1)
        if m == L // BLK // 2 - 1 or m == L // BLK - 1:
            half = slice((m + 1) * BLK - L // 2, (m + 1) * BLK)
            for src, dst in ((gcv, gc_ref), (gmv, gm_ref), (outv, out_ref)):
                mv.put(src.at[half, :], dst.at[half, :])
    sums_ref[...] = jnp.concatenate([s0, s1, s2, jnp.zeros((5, D), f32)], axis=0)
    dwo = dot(gmv[...], ctxv[...], 0, 0)
    left, right = dwo[:, : HL // 2], dwo[:, HL // 2 :]
    keep_ref[...] = jnp.where(core == 0, left, right).astype(bf16)
    send_ref[...] = jnp.where(core == 0, right, left).astype(bf16)
    mv.finish()


def other_call(n, c, one, twos, gn, mo, mid, w_out, ctx, gain, b_down, inv):
    L, D = n.shape
    HL = ctx.shape[1]
    F = twos[0].shape[0] * 4
    return call(
        other_kernel,
        "mlp_other",
        [ANY] * 16 + [None] * 3,
        [
            (sds((L, D), bf16), False),
            (sds((L, D), bf16), False),
            (sds((L, HL), bf16), False),
            (sds((8, L), f32), True),
            (sds((8, D), f32), True),
            (sds((D, HL // 2), bf16), True),
            (sds((D, HL // 2), bf16), True),
        ],
        [
            ((L, D), bf16),
            ((L, D), bf16),
            ((D, F), bf16),
            ((F, D), bf16),
            ((16, D), bf16),
            ((L, D), f32),
            ((L, D), f32),
            ((L, D), f32),
            ((HL, D), bf16),
            ((L, HL), bf16),
            ((L, D), f32),
            ((L, D), f32),
            ((L, D), bf16),
            ((L, D), bf16),
            ((L, HL), bf16),
        ],
        8 * (F // D + 1) + 3 + 5 + 6,
        2 * L * D * F * 4 + 2 * L * D * HL,
        30e6,
        n, c, one, *twos, gn, mo, mid, w_out, ctx, gain, b_down, inv,
    )


def head_grads(pairs, offset, wins, blocks, dd_ref, qv, kv, vv, gv, pv, dqa, dpv, gp_of, done):
    width = len(pairs) * 128
    scale = HEAD_DIM**-0.5
    lane = lax.broadcasted_iota(jnp.int32, (1, 128), 1)
    seen = set()
    for j, (lo, hi, at) in enumerate(wins):
        here = slice(j * BLK, (j + 1) * BLK)
        n = (hi - lo) // BLK
        blocks[j].wait()
        gps = [gp_of(j, t) for t in range(n)]
        for o, p in enumerate(pairs):
            cs = slice((p - offset) * 128, (p - offset + 1) * 128)
            kb, vb = kv[here, cs], vv[here, cs]
            dk = dv = jnp.zeros((BLK, 128), f32)
            for t in range(n):
                i = slice(lo + t * BLK, lo + (t + 1) * BLK)
                b = slice(at + t * BLK, at + (t + 1) * BLK)
                q, g = qv[i, cs], gv[i, cs]
                dq = jnp.zeros((BLK, 128), f32)
                for h in range(2):
                    mine = (lane // HEAD_DIM) == h
                    only = lambda a: jnp.where(mine, a, jnp.zeros_like(a))
                    gh = only(g)
                    pb = pv[2 * (p - offset) + h, :, b]
                    dp = dot(vb, gh, 1, 1)
                    ds = pb.astype(f32) * (dp - dd_ref[2 * p + h : 2 * p + h + 1, i])
                    gps[t] = gps[t] - ds
                    sb = ds.astype(bf16)
                    dv = dv + dot(pb, gh)
                    dk = dk + dot(sb, only(q))
                    dq = dq + dot(sb, only(kb), 0, 0)
                if (p, i.start) in seen:
                    dqa[i, cs] += dq
                else:
                    seen.add((p, i.start))
                    dqa[i, cs] = dq
            os = slice(o * 128, (o + 1) * 128)
            dpv[here, width + o * 128 : width + (o + 1) * 128] = dk.astype(bf16)
            dpv[here, 2 * width + o * 128 : 2 * width + (o + 1) * 128] = dv.astype(bf16)
            dpv[here, os] = (dqa[here, cs] * scale).astype(bf16)
        done(j, gps)


def halves_out(acc, keep, gone):
    _, core, _ = ids()
    half = acc.shape[1] // 2
    left, right = acc[:, :half], acc[:, half:]
    keep[...] = jnp.where(core == 0, left, right).astype(bf16)
    gone[...] = jnp.where(core == 0, right, left).astype(bf16)


def back_a_kernel(
    q_ref, k_ref, v_ref, g_ref, p_ref, n_ref, dd_ref,
    dp_ref, gp_ref, keep_ref, send_ref,
    qv, kv, vv, gv, pv, nv, dqa, dpv, gpv, sems,
):
    mv = Mover(sems)
    L, HL = q_ref.shape
    wins, _ = back_windows(L)
    pairs = range(HL // 128 - 1)
    heads = 2 * len(pairs)
    part = slice(0, len(pairs) * 128)
    gets = [mv.start(v_ref.at[:, part], vv), mv.start(g_ref.at[:, part], gv)]
    blocks = []
    for j, (lo, hi, at) in enumerate(wins):
        w = slice(at, at + hi - lo)
        blocks.append(mv.start(p_ref.at[0:heads, :, w], pv.at[:, :, w]))
        if j == 0:
            gets += [mv.start(q_ref.at[:, part], qv), mv.start(k_ref.at[:, part], kv)]
    later = mv.start(n_ref, nv)
    for op in gets:
        op.wait()

    def done(j, gps):
        lo, hi, at = wins[j]
        for t, gp in enumerate(gps):
            gpv[:, at + t * BLK : at + (t + 1) * BLK] = gp
        mv.put(gpv.at[:, at : at + hi - lo], gp_ref.at[:, at : at + hi - lo])

    zero = jnp.zeros((BLK, BLK), f32)
    head_grads(pairs, 0, wins, blocks, dd_ref, qv, kv, vv, gv, pv, dqa, dpv, lambda j, t: zero, done)
    mv.put(dpv, dp_ref)
    later.wait()
    halves_out(dot(nv[...], dpv[...], 0, 0), keep_ref, send_ref)
    mv.finish()


def back_a_call(q, k, v, g, p, n, dd):
    L, HL = q.shape
    D = n.shape[1]
    heads = HL // HEAD_DIM - 2
    _, wide = back_windows(L)
    width = heads * HEAD_DIM
    part = (L, width)
    return call(
        back_a_kernel,
        "attend_back_a",
        [ANY] * 6 + [None],
        [
            (sds((L, 3 * width), bf16), False),
            (sds((BLK, wide), f32), False),
            (sds((D, 3 * width // 2), bf16), True),
            (sds((D, 3 * width // 2), bf16), True),
        ],
        [(part, bf16)] * 4
        + [((heads, BLK, wide), bf16), ((L, D), bf16), (part, f32), ((L, 3 * width), bf16), ((BLK, wide), f32)],
        8 + 2 * (L // BLK),
        BLK * wide * 128 * 2 * 4 * heads + 2 * L * D * 3 * width,
        18e6,
        q, k, v, g, p, n, dd,
    )


def back_b_kernel(
    q_ref, k_ref, v_ref, g_ref, p_ref, gp_ref, r_ref, dpa_ref, x_ref, w_ref, pq_ref, pk_ref, dd_ref, wpa_ref, wpb_ref,
    gn_ref, dp_ref, sums_ref,
    qv, kv, vv, gv, pv, gpv, rv, dpav, xv, wv, dqa, pqa, dpv, gnv, sems,
):
    mv = Mover(sems)
    L, HL = q_ref.shape
    D = x_ref.shape[1]
    wins, _ = back_windows(L)
    pair = HL // 128 - 1
    part = slice(pair * 128, HL)
    gets = [mv.start(v_ref.at[:, part], vv), mv.start(g_ref.at[:, part], gv)]
    blocks = []
    for j, (lo, hi, at) in enumerate(wins):
        w = slice(at, at + hi - lo)
        blocks.append(mv.start(p_ref.at[2 * pair : 2 * pair + 2, :, w], pv.at[:, :, w]))
        if j == 0:
            gets += [mv.start(q_ref.at[:, part], qv), mv.start(k_ref.at[:, part], kv), mv.start(gp_ref, gpv)]
    later = [mv.start(r_ref, rv), mv.start(dpa_ref, dpav), mv.start(w_ref, wv), mv.start(x_ref, xv)]
    rr = lax.broadcasted_iota(jnp.int32, (BLK, BLK), 0)
    cc = lax.broadcasted_iota(jnp.int32, (BLK, BLK), 1)
    later_of = jnp.where(rr > cc, 1.0, 0.0).astype(bf16)
    wp = pick_weights(wpa_ref[...], wpb_ref[...])
    scale = HEAD_DIM**-0.5
    sums = [jnp.zeros((1, D), f32)] * 2
    seen = set()
    for op in gets:
        op.wait()

    def done(j, gps):
        lo, hi, at = wins[j]
        here = slice(j * BLK, (j + 1) * BLK)
        if j == 0:
            for op in later:
                op.wait()
        kb = pk_ref[here, :]
        carry = jnp.zeros((BLK, 1), f32)
        dk0 = jnp.zeros((BLK, 128), f32)
        for t in reversed(range((hi - lo) // BLK)):
            i = slice(lo + t * BLK, lo + (t + 1) * BLK)
            b = slice(at + t * BLK, at + (t + 1) * BLK)
            gs = ((carry + dot(gps[t].astype(bf16), later_of)) * rv[:, b].astype(f32)).astype(bf16)
            carry = carry + jnp.sum(gps[t], axis=1, keepdims=True)
            dk0 = dk0 + dot(gs, pq_ref[i, :])
            dq = dot(gs, kb, 0, 0)
            if i.start in seen:
                pqa[i, :] += dq
            else:
                seen.add(i.start)
                pqa[i, :] = dq
        dpv[here, 384:512] = (pltpu.roll(dk0, HEAD_DIM, 1) + pqa[here, :] * scale).astype(bf16)
        gn = dot(dpv[here, 384:], wp, 1, 1)
        n = pair * 128
        for c in range(3):
            gn = gn + dot(dpav[here, c * n : (c + 1) * n], wv[c, :, 0:n], 1, 1)
            gn = gn + dot(dpv[here, c * 128 : (c + 1) * 128], wv[c, :, n:], 1, 1)
        gnv[here, :] = gn.astype(bf16)
        mv.put(gnv.at[here, :], gn_ref.at[here, :])
        mv.put(dpv.at[here, :], dp_ref.at[here, :])
        xhat, _ = standard(xv[here, :].astype(f32))
        sums[0] = sums[0] + jnp.sum(gn * xhat, axis=0, keepdims=True)
        sums[1] = sums[1] + jnp.sum(gn, axis=0, keepdims=True)

    gp_of = lambda j, t: gpv[:, wins[j][2] + t * BLK : wins[j][2] + (t + 1) * BLK]
    head_grads([pair], pair, wins, blocks, dd_ref, qv, kv, vv, gv, pv, dqa, dpv, gp_of, done)
    sums_ref[...] = jnp.concatenate(sums + [jnp.zeros((6, D), f32)], axis=0)
    mv.finish()


def back_b_call(q, k, v, g, p, gp, r, dpa, x, w3, pq, pk, dd, wpa, wpb):
    L, HL = q.shape
    D = x.shape[1]
    _, wide = back_windows(L)
    one = (L, 128)
    return call(
        back_b_kernel,
        "attend_back_b",
        [ANY] * 10 + [None] * 5,
        [(sds((L, D), bf16), False), (sds((L, 512), bf16), False), (sds((8, D), f32), True)],
        [(one, bf16)] * 4
        + [
            ((2, BLK, wide), bf16),
            ((BLK, wide), f32),
            ((BLK, wide), bf16),
            (dpa.shape, bf16),
            ((L, D), bf16),
            ((3, D, HL), bf16),
            (one, f32),
            (one, f32),
            ((L, 512), bf16),
            ((L, D), bf16),
        ],
        9 + 3 * (L // BLK),
        BLK * wide * 128 * 2 * 4 * 3 + 2 * L * D * (3 * HL + 128),
        20e6,
        q, k, v, g, p, gp, r, dpa, x, w3, pq, pk, dd, wpa, wpb,
    )


def dw_kernel(n_ref, dp_ref, keep_ref, send_ref, sems):
    halves_out(dot(n_ref[...], dp_ref[...], 0, 0), keep_ref, send_ref)


def dw_call(n, dp):
    L, D = n.shape
    N = dp.shape[1]
    half = sds((D, N // 2), bf16)
    return call(
        dw_kernel, "dw_last", [None] * 2, [(half, True), (half, True)], [], 1, 2 * L * D * N, 4e6, n, dp
    )


def last_kernel(x_ref, ga_ref, gb_ref, gm_ref, g_ref, o_ref):
    xhat, rstd = standard(x_ref[...].astype(f32))
    gn = ga_ref[...].astype(f32) + gb_ref[...].astype(f32)
    o_ref[...] = gm_ref[...].astype(f32) + norm_back(xhat, rstd, row_of(g_ref), gn)


def last_call(x, ga, gb, gm, gain):
    L, D = x.shape
    row = spec((L // 2, D), lambda i: (i, 0))
    return pl.pallas_call(
        last_kernel,
        grid=(2,),
        in_specs=[row] * 4 + [spec((D,))],
        out_specs=row,
        out_shape=sds((L, D), f32),
        compiler_params=params(),
        cost_estimate=cost(1e3, 1e3),
        name="norm_back",
    )(x, ga, gb, gm, gain)


def links(dp, tensor):
    def swap(bit):
        return [(p * tensor + t, (p ^ bit) * tensor + t) for p in range(dp) for t in range(tensor)]

    across = [(p * tensor + t, p * tensor + (1 - t)) for p in range(dp) for t in range(tensor)]
    head_zero = [(p * tensor, p * tensor + 1) for p in range(dp)]
    return swap, across, head_zero


def after(value, *others):
    return lax.optimization_barrier((value, *others))[0]


def after3(a, b, c, *others):
    return lax.optimization_barrier((a, b, c, *others))[:3]


def shards(
    dp,
    tensor,
    tokens,
    lengths,
    cotangent,
    norm_gain_one,
    norm_shift_one,
    w_qkv,
    w_out,
    b_out,
    norm_gain_two,
    norm_shift_two,
    w_up,
    b_up,
    w_down,
    b_down,
):
    _, L, D = tokens.shape
    HL = w_out.shape[0]
    F = w_up.shape[1]
    swap, across, head_zero = links(dp, tensor)
    t = lax.axis_index("tensor")
    d = lax.axis_index("dp")
    core = d % 2
    groups = dp // 2
    rows = D // groups
    send = lambda a, perm: lax.ppermute(a, AXES, perm)

    def sum_dp(v, bit, end):
        while bit < end:
            v = v + send(v, swap(bit))
            bit *= 2
        return v

    def fold(pieces, bit):
        totals = [(keep.astype(f32) + got.astype(f32)).astype(bf16) for keep, got in pieces]
        totals = [a.reshape(groups // (2 * bit), 2, rows, a.shape[-1]) for a in totals]
        mine = (d // (2 * bit)) % 2
        pick = lambda which: jnp.concatenate([lax.dynamic_index_in_dim(a, which, 1, False) for a in totals], axis=-1)
        return pick(mine), pick(1 - mine)

    def finish(keep, got):
        total = (keep.astype(f32) + got.astype(f32)).reshape(2, rows // 2, keep.shape[-1])
        mine = lax.dynamic_index_in_dim(total, core, 0, False)
        got = send(lax.dynamic_index_in_dim(total, 1 - core, 0, False), swap(1))
        return jnp.where(core == 0, mine, got), jnp.where(core == 0, got, mine)

    x = tokens.reshape(L, D)
    cot = cotangent.reshape(L, D)
    w3 = jnp.transpose(w_qkv, (1, 0, 2))

    wp_own = pick_call(w3)
    one, two = pack_call(w_down, w_up, w_out, after(b_up, wp_own))
    wp_got = send(wp_own, head_zero)
    q, k, v, n1 = start_call(after(x, one), w3, norm_gain_one, norm_shift_one)
    one_x, two_x = send(one, across), send(two, across)
    ctx, inv, pq, pk, prob, reach = attend_call(lengths, n1, wp_own, wp_got, q, k, v)
    ctx_b = send(ctx, across)
    one_y = send(after(one_x, ctx), swap(2))
    ga, cot_sum = cot_call(after(cot, ctx), w_down)
    two_y = send(after(two_x, ctx, one_x), swap(2))
    two_z = send(after(two_x, ctx), swap(4))
    two_zy = send(after(two_y, ga, one_y), swap(4))
    one_x, one_y = lax.optimization_barrier((one_x, one_y, ga))[:2]
    ones = [one_x, one_y, send(one_x, swap(1)), send(one_y, swap(1))]
    mid, n2, gn2, mo, keep_a, gone_a, dbu = own_call(
        x, ctx, after(ctx_b, ga), w_out, ones, w_up, w_down, ga, cot, b_out, norm_gain_two, norm_shift_two, b_up
    )
    got_a = send(after(gone_a, two_zy, two_z), swap(1))
    twos = list(lax.optimization_barrier((two_x, two_y, two_z, two_zy, mid))[:4])
    twos = twos + [send(a, swap(1)) for a in twos]
    keep_a, gone_a = fold([(keep_a, got_a)], 1)
    got_a = send(gone_a, swap(2))
    out, gm, gc, dd, sums2, keep_o, gone_o = other_call(
        n2, after(cot, gone_a), one_x, twos, gn2, mo, mid, w_out, ctx, norm_gain_two, b_down, inv
    )
    got_o = send(gone_o, swap(1))
    dp_a, gp, keep_c, gone_c = back_a_call(q, k, v, gc, prob, n1, dd)
    got_c = send(gone_c, swap(1))
    keep_a, gone_a = fold([(keep_a, after(got_a, dp_a))], 2)
    got_a = send(gone_a, swap(4))
    gn1, dp_b, sums1 = back_b_call(
        q, k, v, gc, prob, after(gp, gone_a), reach, dp_a, x, w3, pq, pk, dd, wp_own, wp_got
    )
    gn1_got = send(gn1, across)
    keep_d, gone_d = dw_call(n1, dp_b)
    got_d = send(gone_d, swap(1))
    got_c = after(got_c, dp_b)
    keep_c, gone_c = fold([(keep_c, got_c), (keep_o, got_o), (keep_d, got_d)], 1)
    got_c = send(gone_c, swap(2))
    keep_c, gone_c = fold([(keep_c, got_c)], 2)
    got_c = send(gone_c, swap(4))

    small = jnp.concatenate(
        [sums1[:2].reshape(-1), sums2[:3].reshape(-1), cot_sum.reshape(-1), dbu.reshape(-1)]
    ).reshape(-1, 128)
    small = sum_dp(after(small, gone_c), 1, 4)
    keep_c, gone_c = fold([(keep_c, got_c)], 4)
    got_c = send(gone_c, swap(8))
    small = sum_dp(after(small, gn1_got, gone_c), 4, dp)
    late = small[: 2 * D // 128]
    late = (late + send(late, across)).reshape(2, D)
    early = small[2 * D // 128 :].reshape(-1)

    ends = []

    def rest(keep, got, bit):
        while 2 * bit < dp:
            keep, gone = fold([(keep, got)], bit)
            bit *= 2
            got = send(gone, swap(bit))
            ends.append(got)
        return finish(keep, got)

    keep_a, gone_a = fold([(keep_a, got_a)], 4)
    left_a, right_a = rest(keep_a, send(gone_a, swap(8)), 8)
    left_c, right_c = rest(keep_c, got_c, 8)
    up_share, down_share = left_a, right_a
    n = 3 * (HL - 128) // 2
    m = n + HL // 2
    out_share = jnp.concatenate([left_c[:, n:m], right_c[:, n:m]], axis=1)
    c = jnp.concatenate([left_c[:, :n], right_c[:, :n]], axis=1).reshape(-1, 3, HL - 128)
    e = jnp.concatenate([left_c[:, m:], right_c[:, m:]], axis=1)
    extra = e[:, 384:]
    extra = extra + send(extra, across)
    extra = jnp.where(t == 0, extra, jnp.zeros_like(extra))
    zeros = jnp.zeros((extra.shape[0], HL - HEAD_DIM), f32)
    extra = jnp.concatenate(
        [extra[:, :HEAD_DIM], zeros, extra[:, HEAD_DIM:], zeros, jnp.zeros((extra.shape[0], HL), f32)], axis=1
    )
    qkv_share = jnp.concatenate([c, e[:, :384].reshape(-1, 3, 128)], axis=2) + extra.reshape(-1, 3, HL)
    grad_tokens = last_call(x, gn1, gn1_got, gm, norm_gain_one)
    return (
        out.reshape(1, L, D),
        grad_tokens.reshape(1, L, D),
        late[0],
        late[1],
        qkv_share,
        out_share.T,
        early[2 * D : 3 * D],
        early[:D],
        early[D : 2 * D],
        up_share,
        early[4 * D :],
        down_share.T,
        early[3 * D : 4 * D],
    )


def solution(mesh):
    in_specs = (
        P("dp", None, None),
        P("dp", None),
        P("dp", None, None),
        P(),
        P(),
        P(None, None, "tensor"),
        P("tensor", None),
        P(),
        P(),
        P(),
        P(None, "tensor"),
        P("tensor"),
        P("tensor", None),
        P(),
    )
    out_specs = (
        P("dp", None, None),
        P("dp", None, None),
        P(),
        P(),
        P("dp", None, "tensor"),
        P("tensor", "dp"),
        P(),
        P(),
        P(),
        P("dp", "tensor"),
        P("tensor"),
        P("tensor", "dp"),
        P(),
    )
    body = functools.partial(shards, mesh.shape["dp"], mesh.shape["tensor"])
    return jax.shard_map(body, mesh=mesh, in_specs=in_specs, out_specs=out_specs, check_vma=False)
```

```python
import functools

import jax
import jax.numpy as jnp
from jax import lax
from jax.experimental import pallas as pl
from jax.experimental.pallas import tpu as pltpu
from jax.sharding import PartitionSpec as P

HEAD_DIM = 64
LONGEST = 512
BLK = 256
EPS = 1e-05
FAR = 1e30
AXES = ("dp", "tensor")
f32 = jnp.float32
bf16 = jnp.bfloat16


def dot(a, b, ca=1, cb=0, precision=None):
    return lax.dot_general(
        a, b, (((ca,), (cb,)), ((), ())), preferred_element_type=f32, precision=precision
    )


def spec(shape, index=None):
    if index is None:
        zeros = (0,) * len(shape)
        return pl.BlockSpec(shape, lambda *_: zeros)
    return pl.BlockSpec(shape, index)


def params(mib=60):
    return pltpu.CompilerParams(vmem_limit_bytes=60 * 1024 * 1024)


ANY = pl.BlockSpec(memory_space=pl.ANY)
SMEM = pl.BlockSpec(memory_space=pltpu.SMEM)


def sds(shape, dtype):
    return jax.ShapeDtypeStruct(shape, dtype)


def cost(flops, nbytes, trans=0):
    return pl.CostEstimate(flops=int(flops), bytes_accessed=int(nbytes), transcendentals=int(trans))


def starts_at(pos, lengths_ref, docs):
    start = jnp.zeros_like(pos)
    end = lengths_ref[0, 0]
    for d in range(1, docs):
        start = jnp.where(pos >= end, end, start)
        end = end + lengths_ref[0, d]
    return start


def standard(x):
    mean = jnp.mean(x, axis=-1, keepdims=True)
    c = x - mean
    var = jnp.mean(c * c, axis=-1, keepdims=True)
    rstd = lax.rsqrt(var + EPS)
    return c * rstd, rstd


def norm_back(xhat, rstd, gain, grad):
    gg = grad * gain
    m1 = jnp.mean(gg, axis=-1, keepdims=True)
    m2 = jnp.mean(gg * xhat, axis=-1, keepdims=True)
    return rstd * (gg - m1 - xhat * m2)


def ids():
    d = lax.axis_index("dp")
    return lax.axis_index("tensor"), lax.rem(d, 2), lax.rem(d // 2, 2)


def quarters():
    _, core, y = ids()
    return [2 * y + core, 2 * (1 - y) + core, 2 * y + 1 - core, 2 * (1 - y) + 1 - core]


def pick_weights(own, got):
    t, _, _ = ids()
    return jnp.where(t == 0, own.astype(f32), got.astype(f32)).astype(bf16)


def eighths():
    d = lax.axis_index("dp")
    core, y, z = lax.rem(d, 2), lax.rem(d // 2, 2), lax.rem(d // 4, 2)
    at = lambda z, y, c: 4 * z + 2 * y + c
    return [at(b, a, c) for c in (core, 1 - core) for b, a in ((z, y), (z, 1 - y), (1 - z, y), (1 - z, 1 - y))]


class Mover:
    def __init__(self, sems):
        self.sems, self.count, self.open = sems, 0, []

    def start(self, src, dst):
        op = pltpu.make_async_copy(src, dst, self.sems.at[self.count])
        self.count += 1
        op.start()
        return op

    def put(self, src, dst):
        self.open.append(self.start(src, dst))

    def finish(self):
        for op in self.open:
            op.wait()


def row_of(ref):
    return ref[...].reshape(1, -1)


LIGHT = ("mlp_own", "norm_qkv", "cot_down")


def call(kernel, name, ins, outs, scratch, sems, flops, nbytes, *args):
    full = lambda a: pl.BlockSpec(memory_space=pltpu.VMEM)
    return pl.pallas_call(
        kernel,
        in_specs=[full(a) if s is None else s for s, a in zip(ins, args, strict=True)],
        out_specs=[full(o) if inside else ANY for o, inside in outs],
        out_shape=[o for o, _ in outs],
        scratch_shapes=[pltpu.VMEM(s, t) for s, t in scratch] + [pltpu.SemaphoreType.DMA((sems,))],
        compiler_params=params(),
        cost_estimate=cost(1e3, 1e3) if name in LIGHT else cost(flops, nbytes),
        name=name,
    )(*args)


def pick_kernel(w_ref, wp_ref, qv, kv, sems):
    mv = Mover(sems)
    a = mv.start(w_ref.at[0, :, 0:128], qv)
    b = mv.start(w_ref.at[1, :, 0:128], kv)
    a.wait()
    b.wait()
    lane = lax.broadcasted_iota(jnp.int32, (1, 128), 1)
    k = pltpu.roll(kv[...].astype(f32), HEAD_DIM, 1)
    wp_ref[...] = jnp.where(lane < HEAD_DIM, qv[...].astype(f32), k).astype(bf16)


def pick_call(w3):
    D = w3.shape[1]
    return call(
        pick_kernel, "pick", [ANY], [(sds((D, 128), bf16), True)], [((D, 128), bf16)] * 2, 2, 1e3, 4e5, w3
    )[0]


def pack_kernel(wd_ref, wu_ref, wo_ref, bu_ref, one_ref, two_ref, onev, twov, sems):
    mv = Mover(sems)
    _, core, y = ids()
    s = 2 * y + core
    D = wo_ref.shape[1]
    s8 = eighths()[0]
    ro, ru, rd = wo_ref.shape[0] // 4, wu_ref.shape[0] // 8, wd_ref.shape[0] // 8
    halves = wu_ref.shape[1] // D
    from_row = lambda n: pl.ds(pl.multiple_of(s8 * n, 16), n)
    get_one = mv.start(wo_ref.at[pl.ds(pl.multiple_of(s * ro, 16), ro)], onev.at[0:ro])
    packs = []
    for h in range(halves):
        packs.append(mv.start(wu_ref.at[from_row(ru), h * D : (h + 1) * D], twov.at[h * ru : (h + 1) * ru]))
    packs.append(mv.start(wd_ref.at[from_row(rd)], twov.at[halves * ru : halves * ru + rd]))
    rest = row_of(bu_ref)
    pieces = []
    for _ in range(3):
        piece = rest.astype(bf16)
        rest = rest - piece.astype(f32)
        pieces.append(piece.astype(f32))
    flat = [p[:, h * D : (h + 1) * D] for p in pieces for h in range(halves)]
    onev[ro : ro + 16, :] = jnp.concatenate(flat + [jnp.zeros((16 - len(flat), D), f32)], axis=0).astype(bf16)
    get_one.wait()
    mv.put(onev, one_ref)
    for op in packs:
        op.wait()
    mv.put(twov, two_ref)
    mv.finish()


def pack_call(w_down, w_up, w_out, b_up):
    F, D = w_down.shape
    one = w_out.shape[0] // 4 + 16
    two = (w_up.shape[0] * (F // D) + F) // 8
    return call(
        pack_kernel,
        "pack",
        [ANY] * 3 + [None],
        [(sds((one, D), bf16), False), (sds((two, D), bf16), False)],
        [((one, D), bf16), ((two, D), bf16)],
        8,
        1e3,
        3e6,
        w_down, w_up, w_out, b_up,
    )


def start_kernel(x_ref, w_ref, g_ref, b_ref, q_ref, k_ref, v_ref, n_ref, xv, wv, nv, qv, kv, vv, sems):
    mv = Mover(sems)
    L, D = x_ref.shape
    half = L // 2
    gets = [mv.start(x_ref.at[0:half], xv.at[0:half]), mv.start(w_ref, wv), mv.start(x_ref.at[half:L], xv.at[half:L])]
    gain, shift = row_of(g_ref), row_of(b_ref)
    gets[0].wait()
    for m in range(L // BLK):
        r = slice(m * BLK, (m + 1) * BLK)
        if m * BLK == half:
            gets[2].wait()
        xhat, _ = standard(xv[r, :].astype(f32))
        n = (xhat * gain + shift).astype(bf16)
        nv[r, :] = n
        if m == 0:
            gets[1].wait()
        qv[r, :] = (dot(n, wv[0]).astype(bf16).astype(f32) * HEAD_DIM**-0.5).astype(bf16)
        kv[r, :] = dot(n, wv[1]).astype(bf16)
        vv[r, :] = dot(n, wv[2]).astype(bf16)
        if (m + 1) * BLK % half == 0:
            done = slice((m + 1) * BLK - half, (m + 1) * BLK)
            for src, dst in ((nv, n_ref), (qv, q_ref), (kv, k_ref), (vv, v_ref)):
                mv.put(src.at[done, :], dst.at[done, :])
    mv.finish()


def start_call(x, w3, gain, shift):
    L, D = x.shape
    HL = w3.shape[2]
    half = (L, HL)
    return call(
        start_kernel,
        "norm_qkv",
        [ANY] * 2 + [None] * 2,
        [(sds(half, bf16), False)] * 3 + [(sds((L, D), bf16), False)],
        [((L, D), bf16), ((3, D, HL), bf16), ((L, D), bf16)] + [(half, bf16)] * 3,
        11,
        2 * L * D * 3 * HL,
        9e6,
        x, w3, gain, shift,
    )


def cot_kernel(c_ref, wd_ref, ga_ref, cs_ref, cv, wdv, gav, sems):
    mv = Mover(sems)
    L, D = c_ref.shape
    gets = [mv.start(c_ref, cv), mv.start(wd_ref, wdv)]
    for op in gets:
        op.wait()
    cs = jnp.zeros((1, D), f32)
    for m in range(L // BLK):
        r = slice(m * BLK, (m + 1) * BLK)
        c = cv[r, :]
        cs = cs + jnp.sum(c.astype(f32), axis=0, keepdims=True)
        gav[r, :] = dot(c, wdv[...], 1, 1).astype(bf16)
        mv.put(gav.at[r, :], ga_ref.at[r, :])
    cs_ref[...] = cs
    mv.finish()


def cot_call(c, w_down):
    L, D = c.shape
    F = w_down.shape[0]
    return call(
        cot_kernel,
        "cot_down",
        [ANY] * 2,
        [(sds((L, F), bf16), False), (sds((1, D), f32), True)],
        [((L, D), bf16), ((F, D), bf16), ((L, F), bf16)],
        2 + L // BLK,
        2 * L * D * F,
        7e6,
        c, w_down,
    )


def windows(L):
    reach = LONGEST // BLK
    return [range(max(0, i - reach), i + 1) for i in range(L // BLK)]


def back_windows(L):
    reach = LONGEST // BLK
    found, at = [], 0
    for j in range(L // BLK):
        lo, hi = j * BLK, min(L, (j + reach + 1) * BLK)
        found.append((lo, hi, at))
        at += hi - lo
    return found, at


def attend_kernel(
    docs, strength, len_ref, n_ref, wpa_ref, wpb_ref, q_ref, k_ref, v_ref,
    ctx_ref, inv_ref, pq_ref, pk_ref, p_ref, r_ref,
    nv, qv, kv, vv, vt, cv, pv, rv, bias_ref, sems,
):
    mv = Mover(sems)
    get_n = mv.start(n_ref, nv)
    get_v = mv.start(v_ref, vv)
    get_q = mv.start(q_ref, qv)
    get_k = mv.start(k_ref, kv)
    L, HL = q_ref.shape
    wins, _ = back_windows(L)
    lane = lax.broadcasted_iota(jnp.int32, (1, 128), 1)
    left = lane < HEAD_DIM
    w = pick_weights(wpa_ref[...], wpb_ref[...])
    get_n.wait()
    both = dot(nv[...], w)
    pq_ref[...] = jnp.where(left, both.astype(bf16).astype(f32) * HEAD_DIM**-0.5, 0.0).astype(bf16)
    pk_ref[...] = jnp.where(left, pltpu.roll(both, HEAD_DIM, 1), 0.0).astype(bf16)
    get_v.wait()
    for m in range(L // BLK):
        vt[:, m * BLK : (m + 1) * BLK] = vv[m * BLK : (m + 1) * BLK, :].T
    rows = lax.broadcasted_iota(jnp.int32, (BLK, BLK), 0)
    cols = lax.broadcasted_iota(jnp.int32, (BLK, BLK), 1)
    above = jnp.where(rows < cols, 1.0, 0.0).astype(bf16)
    carry = [jnp.zeros((BLK, 1), f32)] * (L // BLK)
    get_q.wait()
    get_k.wait()
    for i, blocks in enumerate(windows(L)):
        mine = slice(i * BLK, (i + 1) * BLK)
        ipos = i * BLK + lax.broadcasted_iota(jnp.int32, (1, BLK), 1)
        istart = starts_at(ipos, len_ref, docs)
        places = {}
        for j in blocks:
            here = slice(j * BLK, (j + 1) * BLK)
            at = wins[j][2] + (i - j) * BLK
            places[j] = slice(at, at + BLK)
            s = dot(pk_ref[here, :], pq_ref[mine, :], 1, 1)
            jpos = j * BLK + lax.broadcasted_iota(jnp.int32, (BLK, 1), 0)
            inside = jpos >= istart
            fresh = jpos != starts_at(jpos, len_ref, docs)
            if j == i:
                allowed = inside & (jpos <= ipos)
                selectable = inside & (jpos < ipos) & fresh
            else:
                allowed, selectable = inside, inside & fresh
            r = jnp.where(selectable, jnp.maximum(s, 0.0), 0.0)
            rv[:, places[j]] = (r * (2.0 * strength)).astype(bf16)
            c = r * r
            pen = strength * (carry[j] + dot(c.astype(bf16), above))
            bias_ref[j - blocks[0]] = jnp.where(allowed, pen, FAR)
            if i + 1 < L // BLK and j in windows(L)[i + 1]:
                carry[j] = carry[j] + jnp.sum(c, axis=1, keepdims=True)
        invs, outs = [], []
        for h in range(HL // HEAD_DIM):
            cs = slice(h // 2 * 128, (h // 2 + 1) * 128)
            q = jnp.where((lane // HEAD_DIM) == h % 2, qv[mine, cs], jnp.zeros((BLK, 128), bf16))
            ss = [dot(kv[j * BLK : (j + 1) * BLK, cs], q, 1, 1) - bias_ref[j - blocks[0]] for j in blocks]
            top = functools.reduce(jnp.maximum, [jnp.max(s, axis=0, keepdims=True) for s in ss])
            total = jnp.zeros((1, BLK), f32)
            out = jnp.zeros((HEAD_DIM, BLK), f32)
            for j, s in zip(blocks, ss, strict=True):
                e = jnp.exp(s - top)
                total = total + jnp.sum(e, axis=0, keepdims=True)
                e = e.astype(bf16)
                pv[h, :, places[j]] = e
                out = out + dot(vt[h * HEAD_DIM : (h + 1) * HEAD_DIM, j * BLK : (j + 1) * BLK], e)
            inv = 1.0 / total
            invs.append(inv)
            outs.append(out * inv)
        inv_ref[:, mine] = jnp.concatenate(invs + [jnp.zeros((8 - len(invs), BLK), f32)], axis=0)
        for p in range(HL // 128):
            pair = jnp.concatenate(outs[2 * p : 2 * p + 2], axis=0)
            cv[mine, p * 128 : (p + 1) * 128] = pair.T.astype(bf16)
        mv.put(cv.at[mine, :], ctx_ref.at[mine, :])
        for j in blocks:
            mv.put(pv.at[:, :, places[j]], p_ref.at[:, :, places[j]])
    mv.put(rv, r_ref)
    mv.finish()


def attend_call(lengths, n, wpa, wpb, q, k, v):
    L, HL = q.shape
    D = n.shape[1]
    heads = HL // HEAD_DIM
    _, wide = back_windows(L)
    half = (L, HL)
    return call(
        functools.partial(attend_kernel, lengths.shape[1], 2.0 / L),
        "attend",
        [SMEM, ANY, None, None, ANY, ANY, ANY],
        [
            (sds(half, bf16), False),
            (sds((8, L), f32), True),
            (sds((L, 128), bf16), True),
            (sds((L, 128), bf16), True),
            (sds((heads, BLK, wide), bf16), False),
            (sds((BLK, wide), bf16), False),
        ],
        [((L, D), bf16)]
        + [(half, bf16)] * 3
        + [
            ((HL, L), bf16),
            (half, bf16),
            ((heads, BLK, wide), bf16),
            ((BLK, wide), bf16),
            ((LONGEST // BLK + 1, BLK, BLK), f32),
        ],
        5 + L // BLK + wide // BLK,
        1e12,
        14e6,
        lengths, n, wpa, wpb, q, k, v,
    )


C0 = 0.7978845608028654
C1 = 0.044715
CHUNK = 512


def gelu_pair(u):
    u2 = u * u
    t = jnp.tanh(u * (C0 + (C0 * C1) * u2))
    h = 0.5 + 0.5 * t
    a = u * h
    d = h + a * (1.0 - h) * (2.0 * C0 + (6.0 * C0 * C1) * u2)
    return a, d


def own_kernel(
    x_ref, ca_ref, cb_ref, wo_ref, p0_ref, p1_ref, p2_ref, p3_ref, wu_ref, wd_ref, ga_ref, c_ref,
    bo_ref, g_ref, b_ref, bu_ref,
    mid_ref, n_ref, gn_ref, mo_ref, keep_ref, send_ref, dbu_ref,
    xv, cav, cbv, wov, wbv, wuv, wdv, gav, cv, mv_, nv, gnv, mov, av, guv, keepv, sendv, sems,
):
    mv = Mover(sems)
    L, D = x_ref.shape
    F = wu_ref.shape[1]
    HL = ca_ref.shape[1]
    _, core, _ = ids()
    gets = [mv.start(ca_ref, cav), mv.start(wo_ref, wov), mv.start(cb_ref, cbv), mv.start(x_ref, xv)]
    ro, at = HL // 4, 0
    for part, slot in zip((p0_ref, p1_ref, p2_ref, p3_ref), quarters()):
        gets.append(mv.start(part.at[at : at + ro], wbv.at[pl.ds(pl.multiple_of(slot * ro, 16), ro)]))
    later = [mv.start(wu_ref, wuv), mv.start(ga_ref, gav), mv.start(wd_ref, wdv), mv.start(c_ref, cv)]
    bo, gain, shift, bu = row_of(bo_ref), row_of(g_ref), row_of(b_ref), row_of(bu_ref)
    for op in gets:
        op.wait()
    for m in range(L // BLK):
        r = slice(m * BLK, (m + 1) * BLK)
        att = dot(cav[r, :], wov[...]) + dot(cbv[r, :], wbv[...])
        mid = xv[r, :].astype(f32) + (att + bo)
        mv_[r, :] = mid
        xhat, _ = standard(mid)
        nv[r, :] = (xhat * gain + shift).astype(bf16)
    mv.put(mv_, mid_ref)
    mv.put(nv, n_ref)
    for op in later:
        op.wait()
    for j in range(F // CHUNK):
        at = slice(j * CHUNK, (j + 1) * CHUNK)
        db = jnp.zeros((1, CHUNK), f32)
        for m in range(L // BLK):
            r = slice(m * BLK, (m + 1) * BLK)
            a, d = gelu_pair(dot(nv[r, :], wuv[:, at]) + bu[:, at])
            a = a.astype(bf16)
            gu = d * gav[r, at].astype(f32)
            db = db + jnp.sum(gu, axis=0, keepdims=True)
            gu = gu.astype(bf16)
            av[r, :] = a
            guv[r, :] = gu
            mo = dot(a, wdv[at, :])
            gn = dot(gu, wuv[:, at], 1, 1)
            if j == 0:
                mov[r, :] = mo
                gnv[r, :] = gn
            else:
                mov[r, :] += mo
                gnv[r, :] += gn
        dbu_ref[:, at] = db
        dwu = dot(nv[...], guv[...], 0, 0)
        dwd = dot(cv[...], av[...], 0, 0)
        keepv[:, at] = jnp.where(core == 0, dwu, dwd).astype(bf16)
        sendv[:, at] = jnp.where(core == 0, dwd, dwu).astype(bf16)
        mv.put(sendv.at[:, at], send_ref.at[:, at])
        mv.put(keepv.at[:, at], keep_ref.at[:, at])
        if j == F // CHUNK - 1:
            mv.put(gnv, gn_ref)
            mv.put(mov, mo_ref)
    mv.finish()


def own_call(x, ca, cb, w_out, parts, w_up, w_down, ga, c, b_out, gain, shift, b_up):
    L, D = x.shape
    HL = ca.shape[1]
    F = w_up.shape[1]
    return call(
        own_kernel,
        "mlp_own",
        [ANY] * 12 + [None] * 4,
        [
            (sds((L, D), f32), False),
            (sds((L, D), bf16), False),
            (sds((L, D), f32), False),
            (sds((L, D), f32), False),
            (sds((D, F), bf16), False),
            (sds((D, F), bf16), False),
            (sds((1, F), f32), True),
        ],
        [
            ((L, D), bf16),
            ((L, HL), bf16),
            ((L, HL), bf16),
            ((HL, D), bf16),
            ((HL, D), bf16),
            ((D, F), bf16),
            ((F, D), bf16),
            ((L, F), bf16),
            ((L, D), bf16),
            ((L, D), f32),
            ((L, D), bf16),
            ((L, D), f32),
            ((L, D), f32),
            ((L, CHUNK), bf16),
            ((L, CHUNK), bf16),
            ((D, F), bf16),
            ((D, F), bf16),
        ],
        16 + 2 * (F // CHUNK),
        2 * L * D * F * 5 + 4 * L * D * HL,
        36e6,
        x, ca, cb, w_out, *parts, w_up, w_down, ga, c, b_out, gain, shift, b_up,
    )


def other_kernel(
    n_ref, c_ref, a0_ref, d0_ref, d1_ref, d2_ref, d3_ref, d4_ref, d5_ref, d6_ref, d7_ref, gn_ref, mo_ref, mid_ref, wo_ref, ctx_ref,
    g_ref, bd_ref, inv_ref,
    out_ref, gm_ref, gc_ref, dd_ref, sums_ref, keep_ref, send_ref,
    nv, cv, wuv, wdv, bv, gnv, mov, midv, wov, ctxv, gna, moa, outv, gmv, gcv, sems,
):
    mv = Mover(sems)
    L, D = n_ref.shape
    F = wdv.shape[0]
    HL = ctx_ref.shape[1]
    halves = F // D
    gets = [mv.start(n_ref, nv)]
    parts = list(zip((d0_ref, d1_ref, d2_ref, d3_ref, d4_ref, d5_ref, d6_ref, d7_ref), eighths()))
    ru, rd = D // 8, F // 8
    for part, slot in parts:
        for h in range(halves):
            dst = wuv.at[pl.ds(pl.multiple_of(slot * ru, 16), ru), h * D : (h + 1) * D]
            gets.append(mv.start(part.at[h * ru : (h + 1) * ru], dst))
    n = a0_ref.shape[0]
    gets.append(mv.start(a0_ref.at[n - 16 : n], bv))
    downs = [mv.start(c_ref, cv)]
    for part, slot in parts:
        dst = wdv.at[pl.ds(pl.multiple_of(slot * rd, 16), rd)]
        downs.append(mv.start(part.at[halves * ru : halves * ru + rd], dst))
    _, core, _ = ids()
    later = [
        mv.start(src, dst)
        for src, dst in ((gn_ref, gnv), (mo_ref, mov), (mid_ref, midv), (wo_ref, wov), (ctx_ref, ctxv))
    ]
    gain, bd = row_of(g_ref), row_of(bd_ref)
    for op in gets:
        op.wait()
    b = bv[...].astype(f32)
    bu = [b[h : h + 1] + b[halves + h : halves + h + 1] + b[2 * halves + h : 2 * halves + h + 1] for h in range(halves)]
    bu = jnp.concatenate(bu, axis=1)
    for j in range(F // CHUNK):
        at = slice(j * CHUNK, (j + 1) * CHUNK)
        for m in range(L // BLK):
            r = slice(m * BLK, (m + 1) * BLK)
            a, d = gelu_pair(dot(nv[r, :], wuv[:, at]) + bu[:, at])
            if j == 0 and m == 0:
                for op in downs:
                    op.wait()
            gu = (d * dot(cv[r, :], wdv[at, :], 1, 1)).astype(bf16)
            mo = dot(a.astype(bf16), wdv[at, :])
            gn = dot(gu, wuv[:, at], 1, 1)
            if j == 0:
                moa[r, :] = mo
                gna[r, :] = gn
            else:
                moa[r, :] += mo
                gna[r, :] += gn
    for op in later:
        op.wait()
    heads = lax.broadcasted_iota(jnp.int32, (8, HL), 0)
    lane = lax.broadcasted_iota(jnp.int32, (8, HL), 1)
    pick = jnp.where(lane // HEAD_DIM == heads, 1.0, 0.0).astype(bf16)
    s0 = s1 = s2 = jnp.zeros((1, D), f32)
    for m in range(L // BLK):
        r = slice(m * BLK, (m + 1) * BLK)
        mid = midv[r, :]
        outv[r, :] = (mid + (mov[r, :] + moa[r, :]) + bd).astype(bf16)
        gn = gnv[r, :] + gna[r, :]
        xhat, rstd = standard(mid)
        gm = cv[r, :].astype(f32) + norm_back(xhat, rstd, gain, gn)
        s0 = s0 + jnp.sum(gn * xhat, axis=0, keepdims=True)
        s1 = s1 + jnp.sum(gn, axis=0, keepdims=True)
        s2 = s2 + jnp.sum(gm, axis=0, keepdims=True)
        gb = gm.astype(bf16)
        gmv[r, :] = gb
        inv = inv_ref[:, r]
        high = inv.astype(bf16)
        low = (inv - high.astype(f32)).astype(bf16)
        gc = (dot(gb, wov[...], 1, 1) * (dot(high, pick, 0, 0) + dot(low, pick, 0, 0))).astype(bf16)
        gcv[r, :] = gc
        prod = gc.astype(f32) * ctxv[r, :].astype(f32)
        high = prod.astype(bf16)
        low = (prod - high.astype(f32)).astype(bf16)
        dd_ref[:, r] = dot(pick, high, 1, 1) + dot(pick, low, 1, 1)
        if m == L // BLK // 2 - 1 or m == L // BLK - 1:
            half = slice((m + 1) * BLK - L // 2, (m + 1) * BLK)
            for src, dst in ((gcv, gc_ref), (gmv, gm_ref), (outv, out_ref)):
                mv.put(src.at[half, :], dst.at[half, :])
    sums_ref[...] = jnp.concatenate([s0, s1, s2, jnp.zeros((5, D), f32)], axis=0)
    dwo = dot(gmv[...], ctxv[...], 0, 0)
    left, right = dwo[:, : HL // 2], dwo[:, HL // 2 :]
    keep_ref[...] = jnp.where(core == 0, left, right).astype(bf16)
    send_ref[...] = jnp.where(core == 0, right, left).astype(bf16)
    mv.finish()


def other_call(n, c, one, twos, gn, mo, mid, w_out, ctx, gain, b_down, inv):
    L, D = n.shape
    HL = ctx.shape[1]
    F = twos[0].shape[0] * 4
    return call(
        other_kernel,
        "mlp_other",
        [ANY] * 16 + [None] * 3,
        [
            (sds((L, D), bf16), False),
            (sds((L, D), bf16), False),
            (sds((L, HL), bf16), False),
            (sds((8, L), f32), True),
            (sds((8, D), f32), True),
            (sds((D, HL // 2), bf16), True),
            (sds((D, HL // 2), bf16), True),
        ],
        [
            ((L, D), bf16),
            ((L, D), bf16),
            ((D, F), bf16),
            ((F, D), bf16),
            ((16, D), bf16),
            ((L, D), f32),
            ((L, D), f32),
            ((L, D), f32),
            ((HL, D), bf16),
            ((L, HL), bf16),
            ((L, D), f32),
            ((L, D), f32),
            ((L, D), bf16),
            ((L, D), bf16),
            ((L, HL), bf16),
        ],
        8 * (F // D + 1) + 3 + 5 + 6,
        2 * L * D * F * 4 + 2 * L * D * HL,
        30e6,
        n, c, one, *twos, gn, mo, mid, w_out, ctx, gain, b_down, inv,
    )


def head_grads(pairs, offset, wins, blocks, dd_ref, qv, kv, vv, gv, pv, dqa, dpv, gp_of, done):
    width = len(pairs) * 128
    scale = HEAD_DIM**-0.5
    lane = lax.broadcasted_iota(jnp.int32, (1, 128), 1)
    seen = set()
    for j, (lo, hi, at) in enumerate(wins):
        here = slice(j * BLK, (j + 1) * BLK)
        n = (hi - lo) // BLK
        blocks[j].wait()
        gps = [gp_of(j, t) for t in range(n)]
        for o, p in enumerate(pairs):
            cs = slice((p - offset) * 128, (p - offset + 1) * 128)
            kb, vb = kv[here, cs], vv[here, cs]
            dk = dv = jnp.zeros((BLK, 128), f32)
            for t in range(n):
                i = slice(lo + t * BLK, lo + (t + 1) * BLK)
                b = slice(at + t * BLK, at + (t + 1) * BLK)
                q, g = qv[i, cs], gv[i, cs]
                dq = jnp.zeros((BLK, 128), f32)
                for h in range(2):
                    mine = (lane // HEAD_DIM) == h
                    only = lambda a: jnp.where(mine, a, jnp.zeros_like(a))
                    gh = only(g)
                    pb = pv[2 * (p - offset) + h, :, b]
                    dp = dot(vb, gh, 1, 1)
                    ds = pb.astype(f32) * (dp - dd_ref[2 * p + h : 2 * p + h + 1, i])
                    gps[t] = gps[t] - ds
                    sb = ds.astype(bf16)
                    dv = dv + dot(pb, gh)
                    dk = dk + dot(sb, only(q))
                    dq = dq + dot(sb, only(kb), 0, 0)
                if (p, i.start) in seen:
                    dqa[i, cs] += dq
                else:
                    seen.add((p, i.start))
                    dqa[i, cs] = dq
            os = slice(o * 128, (o + 1) * 128)
            dpv[here, width + o * 128 : width + (o + 1) * 128] = dk.astype(bf16)
            dpv[here, 2 * width + o * 128 : 2 * width + (o + 1) * 128] = dv.astype(bf16)
            dpv[here, os] = (dqa[here, cs] * scale).astype(bf16)
        done(j, gps)


def halves_out(acc, keep, gone):
    _, core, _ = ids()
    half = acc.shape[1] // 2
    left, right = acc[:, :half], acc[:, half:]
    keep[...] = jnp.where(core == 0, left, right).astype(bf16)
    gone[...] = jnp.where(core == 0, right, left).astype(bf16)


def back_a_kernel(
    q_ref, k_ref, v_ref, g_ref, p_ref, n_ref, dd_ref,
    dp_ref, gp_ref, keep_ref, send_ref,
    qv, kv, vv, gv, pv, nv, dqa, dpv, gpv, sems,
):
    mv = Mover(sems)
    L, HL = q_ref.shape
    wins, _ = back_windows(L)
    pairs = range(HL // 128 - 1)
    heads = 2 * len(pairs)
    part = slice(0, len(pairs) * 128)
    gets = [mv.start(v_ref.at[:, part], vv), mv.start(g_ref.at[:, part], gv)]
    blocks = []
    for j, (lo, hi, at) in enumerate(wins):
        w = slice(at, at + hi - lo)
        blocks.append(mv.start(p_ref.at[0:heads, :, w], pv.at[:, :, w]))
        if j == 0:
            gets += [mv.start(q_ref.at[:, part], qv), mv.start(k_ref.at[:, part], kv)]
    later = mv.start(n_ref, nv)
    for op in gets:
        op.wait()

    def done(j, gps):
        lo, hi, at = wins[j]
        for t, gp in enumerate(gps):
            gpv[:, at + t * BLK : at + (t + 1) * BLK] = gp
        mv.put(gpv.at[:, at : at + hi - lo], gp_ref.at[:, at : at + hi - lo])

    zero = jnp.zeros((BLK, BLK), f32)
    head_grads(pairs, 0, wins, blocks, dd_ref, qv, kv, vv, gv, pv, dqa, dpv, lambda j, t: zero, done)
    mv.put(dpv, dp_ref)
    later.wait()
    halves_out(dot(nv[...], dpv[...], 0, 0), keep_ref, send_ref)
    mv.finish()


def back_a_call(q, k, v, g, p, n, dd):
    L, HL = q.shape
    D = n.shape[1]
    heads = HL // HEAD_DIM - 2
    _, wide = back_windows(L)
    width = heads * HEAD_DIM
    part = (L, width)
    return call(
        back_a_kernel,
        "attend_back_a",
        [ANY] * 6 + [None],
        [
            (sds((L, 3 * width), bf16), False),
            (sds((BLK, wide), f32), False),
            (sds((D, 3 * width // 2), bf16), True),
            (sds((D, 3 * width // 2), bf16), True),
        ],
        [(part, bf16)] * 4
        + [((heads, BLK, wide), bf16), ((L, D), bf16), (part, f32), ((L, 3 * width), bf16), ((BLK, wide), f32)],
        8 + 2 * (L // BLK),
        BLK * wide * 128 * 2 * 4 * heads + 2 * L * D * 3 * width,
        18e6,
        q, k, v, g, p, n, dd,
    )


def back_b_kernel(
    q_ref, k_ref, v_ref, g_ref, p_ref, gp_ref, r_ref, dpa_ref, x_ref, w_ref, pq_ref, pk_ref, dd_ref, wpa_ref, wpb_ref,
    gn_ref, dp_ref, sums_ref,
    qv, kv, vv, gv, pv, gpv, rv, dpav, xv, wv, dqa, pqa, dpv, gnv, sems,
):
    mv = Mover(sems)
    L, HL = q_ref.shape
    D = x_ref.shape[1]
    wins, _ = back_windows(L)
    pair = HL // 128 - 1
    part = slice(pair * 128, HL)
    gets = [mv.start(v_ref.at[:, part], vv), mv.start(g_ref.at[:, part], gv)]
    blocks = []
    for j, (lo, hi, at) in enumerate(wins):
        w = slice(at, at + hi - lo)
        blocks.append(mv.start(p_ref.at[2 * pair : 2 * pair + 2, :, w], pv.at[:, :, w]))
        if j == 0:
            gets += [mv.start(q_ref.at[:, part], qv), mv.start(k_ref.at[:, part], kv), mv.start(gp_ref, gpv)]
    later = [mv.start(r_ref, rv), mv.start(dpa_ref, dpav), mv.start(w_ref, wv), mv.start(x_ref, xv)]
    rr = lax.broadcasted_iota(jnp.int32, (BLK, BLK), 0)
    cc = lax.broadcasted_iota(jnp.int32, (BLK, BLK), 1)
    later_of = jnp.where(rr > cc, 1.0, 0.0).astype(bf16)
    wp = pick_weights(wpa_ref[...], wpb_ref[...])
    scale = HEAD_DIM**-0.5
    sums = [jnp.zeros((1, D), f32)] * 2
    seen = set()
    for op in gets:
        op.wait()

    def done(j, gps):
        lo, hi, at = wins[j]
        here = slice(j * BLK, (j + 1) * BLK)
        if j == 0:
            for op in later:
                op.wait()
        kb = pk_ref[here, :]
        carry = jnp.zeros((BLK, 1), f32)
        dk0 = jnp.zeros((BLK, 128), f32)
        for t in reversed(range((hi - lo) // BLK)):
            i = slice(lo + t * BLK, lo + (t + 1) * BLK)
            b = slice(at + t * BLK, at + (t + 1) * BLK)
            gs = ((carry + dot(gps[t].astype(bf16), later_of)) * rv[:, b].astype(f32)).astype(bf16)
            carry = carry + jnp.sum(gps[t], axis=1, keepdims=True)
            dk0 = dk0 + dot(gs, pq_ref[i, :])
            dq = dot(gs, kb, 0, 0)
            if i.start in seen:
                pqa[i, :] += dq
            else:
                seen.add(i.start)
                pqa[i, :] = dq
        dpv[here, 384:512] = (pltpu.roll(dk0, HEAD_DIM, 1) + pqa[here, :] * scale).astype(bf16)
        gn = dot(dpv[here, 384:], wp, 1, 1)
        n = pair * 128
        for c in range(3):
            gn = gn + dot(dpav[here, c * n : (c + 1) * n], wv[c, :, 0:n], 1, 1)
            gn = gn + dot(dpv[here, c * 128 : (c + 1) * 128], wv[c, :, n:], 1, 1)
        gnv[here, :] = gn.astype(bf16)
        mv.put(gnv.at[here, :], gn_ref.at[here, :])
        mv.put(dpv.at[here, :], dp_ref.at[here, :])
        xhat, _ = standard(xv[here, :].astype(f32))
        sums[0] = sums[0] + jnp.sum(gn * xhat, axis=0, keepdims=True)
        sums[1] = sums[1] + jnp.sum(gn, axis=0, keepdims=True)

    gp_of = lambda j, t: gpv[:, wins[j][2] + t * BLK : wins[j][2] + (t + 1) * BLK]
    head_grads([pair], pair, wins, blocks, dd_ref, qv, kv, vv, gv, pv, dqa, dpv, gp_of, done)
    sums_ref[...] = jnp.concatenate(sums + [jnp.zeros((6, D), f32)], axis=0)
    mv.finish()


def back_b_call(q, k, v, g, p, gp, r, dpa, x, w3, pq, pk, dd, wpa, wpb):
    L, HL = q.shape
    D = x.shape[1]
    _, wide = back_windows(L)
    one = (L, 128)
    return call(
        back_b_kernel,
        "attend_back_b",
        [ANY] * 10 + [None] * 5,
        [(sds((L, D), bf16), False), (sds((L, 512), bf16), False), (sds((8, D), f32), True)],
        [(one, bf16)] * 4
        + [
            ((2, BLK, wide), bf16),
            ((BLK, wide), f32),
            ((BLK, wide), bf16),
            (dpa.shape, bf16),
            ((L, D), bf16),
            ((3, D, HL), bf16),
            (one, f32),
            (one, f32),
            ((L, 512), bf16),
            ((L, D), bf16),
        ],
        9 + 3 * (L // BLK),
        BLK * wide * 128 * 2 * 4 * 3 + 2 * L * D * (3 * HL + 128),
        20e6,
        q, k, v, g, p, gp, r, dpa, x, w3, pq, pk, dd, wpa, wpb,
    )


def dw_kernel(n_ref, dp_ref, keep_ref, send_ref, sems):
    halves_out(dot(n_ref[...], dp_ref[...], 0, 0), keep_ref, send_ref)


def dw_call(n, dp):
    L, D = n.shape
    N = dp.shape[1]
    half = sds((D, N // 2), bf16)
    return call(
        dw_kernel, "dw_last", [None] * 2, [(half, True), (half, True)], [], 1, 1e12, 4e6, n, dp
    )


def last_kernel(x_ref, ga_ref, gb_ref, gm_ref, g_ref, o_ref):
    xhat, rstd = standard(x_ref[...].astype(f32))
    gn = ga_ref[...].astype(f32) + gb_ref[...].astype(f32)
    o_ref[...] = gm_ref[...].astype(f32) + norm_back(xhat, rstd, row_of(g_ref), gn)


def last_call(x, ga, gb, gm, gain):
    L, D = x.shape
    row = spec((L // 2, D), lambda i: (i, 0))
    return pl.pallas_call(
        last_kernel,
        grid=(2,),
        in_specs=[row] * 4 + [spec((D,))],
        out_specs=row,
        out_shape=sds((L, D), f32),
        compiler_params=params(),
        cost_estimate=cost(1e3, 1e3),
        name="norm_back",
    )(x, ga, gb, gm, gain)


def links(dp, tensor):
    def swap(bit):
        return [(p * tensor + t, (p ^ bit) * tensor + t) for p in range(dp) for t in range(tensor)]

    across = [(p * tensor + t, p * tensor + (1 - t)) for p in range(dp) for t in range(tensor)]
    head_zero = [(p * tensor, p * tensor + 1) for p in range(dp)]
    return swap, across, head_zero


def after(value, *others):
    return lax.optimization_barrier((value, *others))[0]


def after3(a, b, c, *others):
    return lax.optimization_barrier((a, b, c, *others))[:3]


def shards(
    dp,
    tensor,
    tokens,
    lengths,
    cotangent,
    norm_gain_one,
    norm_shift_one,
    w_qkv,
    w_out,
    b_out,
    norm_gain_two,
    norm_shift_two,
    w_up,
    b_up,
    w_down,
    b_down,
):
    _, L, D = tokens.shape
    HL = w_out.shape[0]
    F = w_up.shape[1]
    swap, across, head_zero = links(dp, tensor)
    t = lax.axis_index("tensor")
    d = lax.axis_index("dp")
    core = d % 2
    groups = dp // 2
    rows = D // groups
    send = lambda a, perm: lax.ppermute(a, AXES, perm)

    def sum_dp(v, bit, end):
        while bit < end:
            v = v + send(v, swap(bit))
            bit *= 2
        return v

    def fold(pieces, bit):
        totals = [(keep.astype(f32) + got.astype(f32)).astype(bf16) for keep, got in pieces]
        totals = [a.reshape(groups // (2 * bit), 2, rows, a.shape[-1]) for a in totals]
        mine = (d // (2 * bit)) % 2
        pick = lambda which: jnp.concatenate([lax.dynamic_index_in_dim(a, which, 1, False) for a in totals], axis=-1)
        return pick(mine), pick(1 - mine)

    def finish(keep, got):
        total = (keep.astype(f32) + got.astype(f32)).reshape(2, rows // 2, keep.shape[-1])
        mine = lax.dynamic_index_in_dim(total, core, 0, False)
        got = send(lax.dynamic_index_in_dim(total, 1 - core, 0, False), swap(1))
        return jnp.where(core == 0, mine, got), jnp.where(core == 0, got, mine)

    x = tokens.reshape(L, D)
    cot = cotangent.reshape(L, D)
    w3 = jnp.transpose(w_qkv, (1, 0, 2))

    wp_own = pick_call(w3)
    one, two = pack_call(w_down, w_up, w_out, after(b_up, wp_own))
    wp_got = send(wp_own, head_zero)
    q, k, v, n1 = start_call(after(x, one), w3, norm_gain_one, norm_shift_one)
    one_x, two_x = send(one, across), send(two, across)
    ctx, inv, pq, pk, prob, reach = attend_call(lengths, n1, wp_own, wp_got, q, k, v)
    ctx_b = send(ctx, across)
    one_y = send(after(one_x, ctx), swap(2))
    ga, cot_sum = cot_call(after(cot, ctx), w_down)
    two_y = send(after(two_x, ctx, one_x), swap(2))
    two_z = send(after(two_x, ctx), swap(4))
    two_zy = send(after(two_y, ga, one_y), swap(4))
    one_x, one_y = lax.optimization_barrier((one_x, one_y, ga))[:2]
    ones = [one_x, one_y, send(one_x, swap(1)), send(one_y, swap(1))]
    mid, n2, gn2, mo, keep_a, gone_a, dbu = own_call(
        x, ctx, after(ctx_b, ga), w_out, ones, w_up, w_down, ga, cot, b_out, norm_gain_two, norm_shift_two, b_up
    )
    got_a = send(after(gone_a, two_zy, two_z), swap(1))
    twos = list(lax.optimization_barrier((two_x, two_y, two_z, two_zy, mid))[:4])
    twos = twos + [send(a, swap(1)) for a in twos]
    keep_a, gone_a = fold([(keep_a, got_a)], 1)
    got_a = send(gone_a, swap(2))
    out, gm, gc, dd, sums2, keep_o, gone_o = other_call(
        n2, after(cot, gone_a), one_x, twos, gn2, mo, mid, w_out, ctx, norm_gain_two, b_down, inv
    )
    got_o = send(gone_o, swap(1))
    dp_a, gp, keep_c, gone_c = back_a_call(q, k, v, gc, prob, n1, dd)
    got_c = send(gone_c, swap(1))
    keep_a, gone_a = fold([(keep_a, after(got_a, dp_a))], 2)
    got_a = send(gone_a, swap(4))
    gn1, dp_b, sums1 = back_b_call(
        q, k, v, gc, prob, after(gp, gone_a), reach, dp_a, x, w3, pq, pk, dd, wp_own, wp_got
    )
    gn1_got = send(gn1, across)
    keep_d, gone_d = dw_call(n1, dp_b)
    got_d = send(gone_d, swap(1))
    got_c = after(got_c, dp_b)
    keep_c, gone_c = fold([(keep_c, got_c), (keep_o, got_o), (keep_d, got_d)], 1)
    got_c = send(gone_c, swap(2))
    keep_c, gone_c = fold([(keep_c, got_c)], 2)
    got_c = send(gone_c, swap(4))

    small = jnp.concatenate(
        [sums1[:2].reshape(-1), sums2[:3].reshape(-1), cot_sum.reshape(-1), dbu.reshape(-1)]
    ).reshape(-1, 128)
    small = sum_dp(after(small, gone_c), 1, 4)
    keep_c, gone_c = fold([(keep_c, got_c)], 4)
    got_c = send(gone_c, swap(8))
    small = sum_dp(after(small, gn1_got, gone_c), 4, dp)
    late = small[: 2 * D // 128]
    early = small[2 * D // 128 :].reshape(-1)

    ends = []

    def rest(keep, got, bit):
        while 2 * bit < dp:
            keep, gone = fold([(keep, got)], bit)
            bit *= 2
            got = send(gone, swap(bit))
            ends.append(got)
        return finish(keep, got)

    keep_a, gone_a = fold([(keep_a, got_a)], 4)
    left_a, right_a = rest(keep_a, send(gone_a, swap(8)), 8)
    left_c, right_c = rest(keep_c, got_c, 8)
    up_share, down_share = left_a, right_a
    n = 3 * (HL - 128) // 2
    m = n + HL // 2
    out_share = jnp.concatenate([left_c[:, n:m], right_c[:, n:m]], axis=1)
    c = jnp.concatenate([left_c[:, :n], right_c[:, :n]], axis=1).reshape(-1, 3, HL - 128)
    e = jnp.concatenate([left_c[:, m:], right_c[:, m:]], axis=1)
    extra = e[:, 384:]
    late = (late + send(after(late, extra), across)).reshape(2, D)
    extra = extra + send(extra, across)
    extra = jnp.where(t == 0, extra, jnp.zeros_like(extra))
    zeros = jnp.zeros((extra.shape[0], HL - HEAD_DIM), f32)
    extra = jnp.concatenate(
        [extra[:, :HEAD_DIM], zeros, extra[:, HEAD_DIM:], zeros, jnp.zeros((extra.shape[0], HL), f32)], axis=1
    )
    qkv_share = jnp.concatenate([c, e[:, :384].reshape(-1, 3, 128)], axis=2) + extra.reshape(-1, 3, HL)
    grad_tokens = last_call(x, gn1, gn1_got, gm, norm_gain_one)
    return (
        out.reshape(1, L, D),
        grad_tokens.reshape(1, L, D),
        late[0],
        late[1],
        qkv_share,
        out_share.T,
        early[2 * D : 3 * D],
        early[:D],
        early[D : 2 * D],
        up_share,
        early[4 * D :],
        down_share.T,
        early[3 * D : 4 * D],
    )


def solution(mesh):
    in_specs = (
        P("dp", None, None),
        P("dp", None),
        P("dp", None, None),
        P(),
        P(),
        P(None, None, "tensor"),
        P("tensor", None),
        P(),
        P(),
        P(),
        P(None, "tensor"),
        P("tensor"),
        P("tensor", None),
        P(),
    )
    out_specs = (
        P("dp", None, None),
        P("dp", None, None),
        P(),
        P(),
        P("dp", None, "tensor"),
        P("tensor", "dp"),
        P(),
        P(),
        P(),
        P("dp", "tensor"),
        P("tensor"),
        P("tensor", "dp"),
        P(),
    )
    body = functools.partial(shards, mesh.shape["dp"], mesh.shape["tensor"])
    return jax.shard_map(body, mesh=mesh, in_specs=in_specs, out_specs=out_specs, check_vma=False)
```
